32 devices in a mesh: gx: 8 (over z, x), gy: 4 (over y, core).
Axes of the slice: x: 2, y: 2, z: 4, core: 2. Of those that a mesh axis runs over, the one named last changes fastest.
Arguments:
- tokens: bfloat16 [256, 128, 768], P(('gx', 'gy')), may hold values from -6 to 6
- land_mask: int32 [256, 128], P(('gx', 'gy')), may hold values from 0 to 1, as said below
- counts: int32 [256], replicated, may hold values from 1 to 128, as said below
- ln1_gain: bfloat16 [768], P(('gx', 'gy')), may hold values from 0.099609375 to 1.8984375
- ln1_shift: bfloat16 [768], P(('gx', 'gy')), may hold values from -3 to 3
- qkv_weight: bfloat16 [768, 2304], P(('gx', 'gy')), may hold values from -0.21875 to 0.21875
- qv_bias: bfloat16 [2, 768], P(None, ('gx', 'gy')), may hold values from -3 to 3
- out_weight: bfloat16 [768, 768], P(('gx', 'gy')), may hold values from -0.875 to 0.875
- out_bias: bfloat16 [768], P(('gx', 'gy')), may hold values from -3 to 3
- ln2_gain: bfloat16 [768], P(('gx', 'gy')), may hold values from 0.099609375 to 1.8984375
- ln2_shift: bfloat16 [768], P(('gx', 'gy')), may hold values from -3 to 3
- up_weight: bfloat16 [768, 3072], P(('gx', 'gy')), may hold values from -0.21875 to 0.21875
- up_bias: bfloat16 [3072], P(('gx', 'gy')), may hold values from -3 to 3
- down_weight: bfloat16 [3072, 768], P(('gx', 'gy')), may hold values from -0.109375 to 0.109375
- down_bias: bfloat16 [768], P(('gx', 'gy')), may hold values from -3 to 3
- cotangent: bfloat16 [256, 128, 768], P(('gx', 'gy')), may hold values from -6 to 6
Outputs:
- out_tokens: bfloat16 [256, 128, 768], P(('gx', 'gy'))
- grad_tokens: bfloat16 [256, 128, 768], P(('gx', 'gy'))
- grad_ln1_gain: float32 [768], P(('gx', 'gy'))
- grad_ln1_shift: float32 [768], P(('gx', 'gy'))
- grad_qkv_weight: float32 [768, 2304], P(('gx', 'gy'))
- grad_qv_bias: float32 [2, 768], P(None, ('gx', 'gy'))
- grad_out_weight: float32 [768, 768], P(('gx', 'gy'))
- grad_out_bias: float32 [768], P(('gx', 'gy'))
- grad_ln2_gain: float32 [768], P(('gx', 'gy'))
- grad_ln2_shift: float32 [768], P(('gx', 'gy'))
- grad_up_weight: float32 [768, 3072], P(('gx', 'gy'))
- grad_up_bias: float32 [3072], P(('gx', 'gy'))
- grad_down_weight: float32 [3072, 768], P(('gx', 'gy'))
- grad_down_bias: float32 [768], P(('gx', 'gy'))
The draws below stay inside these ranges and needn't reach their ends.
Inputs may be any that keep to these rules, and one draw needn't show every extreme that they name: `land_mask`: each sample has at least as many land patches as its count. Sample i of a device (in the device's own order) is processed by the device with gy index i mod 4 and the same gx index. On every device, the counts of the samples that go to one gy index add up to at most 3 * 128 * 2 / 4 (192 here); exactly that for some pair of devices in every draw.
All inputs are finite; a program needn't handle non-finite values.
Results may differ from the reference program's by a relative error of at most 0.012.
Values may be sent and summed in bfloat16 or wider, within the bound.
A program may use at most 192 MiB of HBM per device.

```python
import math
import jax
import jax.numpy as jnp
from jax import lax

D = 768
HEADS = 12
HD = 64
FF = 3072
SAMPLE_PATCHES = 128
SAMPLES_PER_PEER = 2
DEVICE_SAMPLES = 8
SAMPLES = 256


def routing_draw(key):
    n_dev = SAMPLES // DEVICE_SAMPLES
    column_groups = DEVICE_SAMPLES // SAMPLES_PER_PEER
    slot_capacity = 3 * SAMPLE_PATCHES * SAMPLES_PER_PEER // 4
    shape_dev = (n_dev, DEVICE_SAMPLES)
    choose = jax.random.randint(jax.random.fold_in(key, 11), shape_dev, 0, 10)
    small_count = jax.random.randint(jax.random.fold_in(key, 12), shape_dev, 1, SAMPLE_PATCHES // 4 + 1)
    middle_count = jax.random.randint(jax.random.fold_in(key, 13), shape_dev, SAMPLE_PATCHES // 4, 3 * SAMPLE_PATCHES // 4 + 1)
    large_count = jax.random.randint(jax.random.fold_in(key, 14), shape_dev, 3 * SAMPLE_PATCHES // 4, SAMPLE_PATCHES + 1)
    unscaled_count = jnp.where(choose < 3, small_count, jnp.where(choose < 6, middle_count, large_count))
    target_gy = jnp.broadcast_to((jnp.arange(DEVICE_SAMPLES) % column_groups)[None, :], shape_dev).astype(jnp.int32)
    same_dest = target_gy[:, :, None] == target_gy[:, None, :]
    group_total = jnp.sum(jnp.where(same_dest, unscaled_count[:, None, :], 0), axis=2)
    scaled_count = jnp.where(group_total > slot_capacity, unscaled_count * (slot_capacity - SAMPLES_PER_PEER) // jnp.maximum(group_total, 1) + 1, unscaled_count)
    forced_dev = jax.random.randint(jax.random.fold_in(key, 16), (), 0, n_dev)
    forced_gy = jax.random.randint(jax.random.fold_in(key, 17), (), 0, column_groups)
    earlier = jnp.arange(DEVICE_SAMPLES)[None, :] < jnp.arange(DEVICE_SAMPLES)[:, None]
    before_same = same_dest & earlier[None]
    placement_index = jnp.sum(before_same.astype(jnp.int32), axis=2)
    forced_count = jnp.where(placement_index < SAMPLES_PER_PEER // 2, SAMPLE_PATCHES, SAMPLE_PATCHES // 2)
    in_forced = (jnp.arange(n_dev)[:, None] == forced_dev) & (target_gy == forced_gy)
    final_count = jnp.where(in_forced, forced_count, scaled_count).astype(jnp.int32).reshape(-1)
    extra = jax.random.randint(jax.random.fold_in(key, 19), (SAMPLES,), 0, SAMPLE_PATCHES // 4 + 1)
    land_total = jnp.minimum(final_count + extra, SAMPLE_PATCHES)
    perms = jax.vmap(lambda sub_key: jax.random.permutation(sub_key, SAMPLE_PATCHES))(jax.random.split(jax.random.fold_in(key, 18), SAMPLES))
    land = (perms < land_total[:, None]).astype(jnp.int32)
    return (land, final_count)


def draw_land_mask(key, part):
    return routing_draw(key)[0]


def draw_counts(key, part):
    return routing_draw(key)[1]


def level_of(own_key, shape, cuts, least, high):
    factor_of, own = 1.0, jax.random.fold_in(own_key, 6)
    for axis_at, shards_of in cuts:
        steps = jnp.exp(jax.random.uniform(jax.random.fold_in(own, axis_at), (shards_of,), jnp.float32, least / len(cuts), high / len(cuts)))
        factor_of = factor_of * jnp.repeat(steps, shape[axis_at] // shards_of).reshape([-1 if axis == axis_at else 1 for axis in range(len(shape))])
    return factor_of


def scatter_about(own_key, extent, width, most, pieces=(), dtype=jnp.bfloat16):
    values = width * jax.random.normal(own_key, extent, jnp.float32)
    if pieces:
        values = values * level_of(own_key, extent, pieces, -0.22, 0.18)
    return jnp.clip(values, -most, most).astype(dtype)


def setup_inputs(seed: int = 0) -> dict:
    key_list = jax.random.split(jax.random.key(seed), 17)
    tokens = scatter_about(key_list[0], (SAMPLES, SAMPLE_PATCHES, D), 1.0, 6.0, ((0, 32),))
    land_mask = draw_land_mask(jax.random.fold_in(key_list[16], 71), 0)
    counts = draw_counts(jax.random.fold_in(key_list[16], 71), 0)
    ln1_gain = jnp.clip(1.0 + 0.18 * jax.random.normal(key_list[3], (D,), jnp.float32), 0.099609375, 1.8984375).astype(jnp.bfloat16)
    ln1_shift = scatter_about(key_list[4], (D,), 0.3, 3.0, ((0, 32),))
    qkv_weight = scatter_about(key_list[5], (D, 3 * D), D ** -0.5, 0.21875, ((0, 32),))
    qv_bias = scatter_about(key_list[6], (2, D), 0.5, 3.0, ((1, 32),))
    out_weight = scatter_about(key_list[7], (D, D), (D // 16) ** -0.5, 0.875, ((0, 32),))
    out_bias = scatter_about(key_list[8], (D,), 0.3, 3.0, ((0, 32),))
    ln2_gain = jnp.clip(1.0 + 0.18 * jax.random.normal(key_list[9], (D,), jnp.float32), 0.099609375, 1.8984375).astype(jnp.bfloat16)
    ln2_shift = scatter_about(key_list[10], (D,), 0.3, 3.0, ((0, 32),))
    up_weight = scatter_about(key_list[11], (D, FF), D ** -0.5, 0.21875, ((0, 32),))
    up_bias = scatter_about(key_list[12], (FF,), 0.5, 3.0, ((0, 32),))
    down_weight = scatter_about(key_list[13], (FF, D), FF ** -0.5, 0.109375, ((0, 32),))
    down_bias = scatter_about(key_list[14], (D,), 0.3, 3.0, ((0, 32),))
    cotangent = scatter_about(key_list[15], (SAMPLES, SAMPLE_PATCHES, D), 1.0, 6.0, ((0, 32),))
    return dict(tokens=tokens, land_mask=land_mask, counts=counts, ln1_gain=ln1_gain, ln1_shift=ln1_shift, qkv_weight=qkv_weight, qv_bias=qv_bias, out_weight=out_weight, out_bias=out_bias, ln2_gain=ln2_gain, ln2_shift=ln2_shift, up_weight=up_weight, up_bias=up_bias, down_weight=down_weight, down_bias=down_bias, cotangent=cotangent)


@jax.custom_vjp
def low(v):
    return lax.optimization_barrier(v.astype(jnp.bfloat16)).astype(jnp.float32)

@jax.custom_vjp
def low_back(v):
    return v

def low_keep(v):
    return (low(v), None)

def low_pass(kept, grad):
    return (grad,)

def back_keep(v):
    return (v, None)

def back_low(kept, grad):
    return (low(grad),)
low.defvjp(low_keep, low_pass)
low_back.defvjp(back_keep, back_low)

def layer_norm(values, gain, shift):
    center = values - lax.optimization_barrier(jnp.mean(values, axis=-1, keepdims=True))
    spread = lax.optimization_barrier(jnp.mean(center * center, axis=-1, keepdims=True))
    return center * lax.rsqrt(spread + 1e-05) * gain + shift

def layer_block(inputs, visible, gain_one, shift_one, qkv_full, bias_qv, out_full, bias_out, gain_two, shift_two, up_full, bias_up, down_full, bias_down):
    highest = lax.Precision.HIGHEST
    normed = low(layer_norm(inputs, gain_one, shift_one))
    joined_qkv = jnp.einsum('gpd,de->gpe', normed, qkv_full, precision=highest)
    queries = low_back(low(joined_qkv[..., :D] + bias_qv[0]))
    key_rows = low_back(low(joined_qkv[..., D:2 * D]))
    value_rows = low_back(low(joined_qkv[..., 2 * D:] + bias_qv[1]))
    head_shape = inputs.shape[:2] + (HEADS, HD)
    scores = jnp.einsum('gqhe,gkhe->ghqk', queries.reshape(head_shape), key_rows.reshape(head_shape), precision=highest) * HD ** (-0.5)
    scores = low_back(scores)
    allowed = (visible == 1)[:, None, None, :]
    scores = jnp.where(allowed, scores, -1000000000.0)
    attn_probs = low(jax.nn.softmax(scores, axis=-1))
    context = jnp.einsum('ghqk,gkhe->gqhe', attn_probs, value_rows.reshape(head_shape), precision=highest).reshape(inputs.shape)
    context = low_back(low(context))
    branch = low_back(jnp.einsum('gpd,de->gpe', context, out_full, precision=highest) + bias_out)
    middle = inputs + branch
    normed_two = low(layer_norm(middle, gain_two, shift_two))
    hidden = low_back(jnp.einsum('gpd,df->gpf', normed_two, up_full, precision=highest) + bias_up)
    active = low(jax.nn.gelu(hidden, approximate=False))
    result = middle + jnp.einsum('gpf,fd->gpd', active, down_full, precision=highest) + bias_down
    return result * (visible == 1)[..., None].astype(jnp.float32)

def reference(tokens, land_mask, counts, ln1_gain, ln1_shift, qkv_weight, qv_bias, out_weight, out_bias, ln2_gain, ln2_shift, up_weight, up_bias, down_weight, down_bias, cotangent):
    params = tuple((item.astype(jnp.float32) for item in (ln1_gain, ln1_shift, qkv_weight, qv_bias, out_weight, out_bias, ln2_gain, ln2_shift, up_weight, up_bias, down_weight, down_bias)))
    land_rank = jnp.cumsum(land_mask, axis=1) - 1
    kept = ((land_mask == 1) & (land_rank < counts[:, None])).astype(jnp.int32)
    group_size = math.gcd(SAMPLES, max(1, 4096 // SAMPLE_PATCHES))
    turns = SAMPLES // group_size
    inputs_all = tokens.astype(jnp.float32).reshape(turns, group_size, SAMPLE_PATCHES, D)
    masks_all = kept.reshape(turns, group_size, SAMPLE_PATCHES)
    grads_all = cotangent.astype(jnp.float32).reshape(turns, group_size, SAMPLE_PATCHES, D)

    def one_group(carry, item):
        inputs, visible, upstream = item

        def forward(input_rows, *weights):
            return layer_block(input_rows, visible, *weights)
        result, pull = jax.vjp(forward, inputs, *params)
        grads = pull(upstream)
        summed = tuple((acc + grad for acc, grad in zip(carry, grads[1:])))
        return (summed, (result, grads[0]))
    start_sums = tuple((jnp.zeros(item.shape, jnp.float32) for item in params))
    totals, (results, input_grads) = lax.scan(one_group, start_sums, (inputs_all, masks_all, grads_all))
    out_tokens = results.reshape(SAMPLES, SAMPLE_PATCHES, D).astype(jnp.bfloat16)
    grad_tokens = input_grads.reshape(SAMPLES, SAMPLE_PATCHES, D).astype(jnp.bfloat16)
    return (out_tokens, grad_tokens, totals[0], totals[1], totals[2], totals[3], totals[4], totals[5], totals[6], totals[7], totals[8], totals[9], totals[10], totals[11])
```

```python
import functools
import math

import jax
import jax.numpy as jnp
from jax import lax
from jax.experimental import pallas as pl
from jax.experimental.pallas import tpu as pltpu
from jax.sharding import PartitionSpec as P

HEADS = 12
HD = 64
MESH = pl.DeviceIdType.MESH


class Place:
    def __init__(self, chain):
        gx = lax.axis_index("gx")
        gy = lax.axis_index("gy")
        self.chain = chain
        self.a = gx // 2
        self.b = gx % 2
        self.c = gy // 2
        self.d = gy % 2

    def shard(self, a=None, b=None, c=None, d=None):
        a = self.a if a is None else a
        b = self.b if b is None else b
        c = self.c if c is None else c
        d = self.d if d is None else d
        return ((a * 2 + b) * 2 + c) * 2 + d

    def device(self, a=None, b=None, c=None, d=None):
        a = self.a if a is None else a
        b = self.b if b is None else b
        c = self.c if c is None else c
        d = self.d if d is None else d
        return (a * 2 + b, c * 2 + d)

    def greet(self):
        barrier = pltpu.get_barrier_semaphore()
        has_below = self.a > 0
        has_above = self.a < self.chain - 1
        for to in (
            self.device(d=1 - self.d),
            self.device(c=1 - self.c),
            self.device(b=1 - self.b),
        ):
            pl.semaphore_signal(barrier, inc=1, device_id=to, device_id_type=MESH)

        @pl.when(has_below)
        def _():
            pl.semaphore_signal(
                barrier, inc=1, device_id=self.device(a=self.a - 1), device_id_type=MESH
            )

        @pl.when(has_above)
        def _():
            pl.semaphore_signal(
                barrier, inc=1, device_id=self.device(a=self.a + 1), device_id_type=MESH
            )

        pl.semaphore_wait(
            barrier, 3 + has_below.astype(jnp.int32) + has_above.astype(jnp.int32)
        )


def halves(widths):
    parts = []
    for at, width in enumerate(widths):
        if width % 256:
            parts.append((at, 0, width, "b"))
        else:
            parts.append((at, 0, width // 2, "b"))
            parts.append((at, width // 2, width // 2, "c"))
    return parts


class Gather:
    def __init__(self, place, parts, own, full, sems):
        self.place, self.parts, self.own, self.full = place, parts, own, full
        self.chain_sem, self.send_sem, self.recv_sem = sems

    def view(self, part, index):
        at, first, width, _ = self.parts[part]
        return self.full[at].at[index, :, pl.ds(first, width)]

    def copy(self, part, index, to, send, own=False):
        at, first, width, _ = self.parts[part]
        src = self.own[at].at[:, pl.ds(first, width)] if own else self.view(part, index)
        return pltpu.make_async_remote_copy(
            src_ref=src,
            dst_ref=self.view(part, index),
            send_sem=send,
            recv_sem=self.recv_sem.at[part, index],
            device_id=to,
            device_id_type=MESH,
        )

    def flip(self, axis):
        place = self.place
        return {axis: 1 - {"b": place.b, "c": place.c, "d": place.d}[axis]}

    def links(self, part):
        first = self.parts[part][3]
        return first, ("c" if first == "b" else "b")

    def send_pair(self, part, index, axis, own=False):
        self.copy(part, index, self.place.device(**self.flip(axis)), self.send_sem.at[part], own).start()

    def arrived(self, part, index):
        self.copy(part, index, self.place.device(d=1 - self.place.d), self.send_sem.at[part]).wait_recv()

    def begin(self, part):
        place = self.place
        mine = place.shard()
        first, second = self.links(part)

        @pl.when(place.a < place.chain - 1)
        def _():
            self.copy(part, mine, place.device(a=place.a + 1), self.chain_sem.at[part, 0, 0], True).start()

        @pl.when(place.a > 0)
        def _():
            self.copy(part, mine, place.device(a=place.a - 1), self.chain_sem.at[part, 1, 0], True).start()

        for axis in (first, second, "d"):
            self.send_pair(part, mine, axis, True)

    def chain_step(self, part, step):
        place = self.place
        first, second = self.links(part)

        @pl.when(place.a - 1 - step >= 0)
        def _():
            index = place.shard(a=place.a - 1 - step)
            self.arrived(part, index)

            @pl.when(place.a < place.chain - 1)
            def _():
                self.copy(
                    part, index, place.device(a=place.a + 1), self.chain_sem.at[part, 0, step + 1]
                ).start()

            for axis in (first, second, "d"):
                self.send_pair(part, index, axis)

        @pl.when(place.a + 1 + step < place.chain)
        def _():
            index = place.shard(a=place.a + 1 + step)
            self.arrived(part, index)

            @pl.when(place.a > 0)
            def _():
                self.copy(
                    part, index, place.device(a=place.a - 1), self.chain_sem.at[part, 1, step + 1]
                ).start()

            for axis in (first, second, "d"):
                self.send_pair(part, index, axis)

    def cross_one(self, part, row):
        place = self.place
        first, second = self.links(part)
        index = place.shard(a=row, **self.flip(first))
        self.arrived(part, index)
        for axis in (second, "d"):
            self.send_pair(part, index, axis)

    def cross_step(self, part, step):
        place = self.place
        if isinstance(step, int) and step == 0:
            self.cross_one(part, place.a)
            return

        @pl.when(place.a - step >= 0)
        def _():
            self.cross_one(part, place.a - step)

        @pl.when(place.a + step < place.chain)
        def _():
            self.cross_one(part, place.a + step)

    def last_one(self, part, row, other):
        place = self.place
        first, second = self.links(part)
        where = self.flip(second)
        if other:
            where.update(self.flip(first))
        index = place.shard(a=row, **where)
        self.arrived(part, index)
        self.send_pair(part, index, "d")

    def last_step(self, part, step):
        place = self.place
        if isinstance(step, int) and step == 0:
            for other in (False, True):
                self.last_one(part, place.a, other)
            return

        @pl.when(place.a - step >= 0)
        def _():
            for other in (False, True):
                self.last_one(part, place.a - step, other)

        @pl.when(place.a + step < place.chain)
        def _():
            for other in (False, True):
                self.last_one(part, place.a + step, other)

    def finish(self, part):
        place = self.place

        def one(at, carry):
            self.arrived(part, at * 2 + 1 - place.d)
            return carry

        lax.fori_loop(0, 4 * place.chain, one, 0)
        at, first, width, _ = self.parts[part]
        block = self.full[at].at[pl.ds(0, 7 * place.chain), :, pl.ds(first, width)]
        pltpu.make_async_copy(block, block, self.send_sem.at[part]).wait()

        def sent(step, carry):
            @pl.when((place.a < place.chain - 1) & (place.a - step >= 0))
            def _():
                self.copy(
                    part, place.shard(a=place.a - step), place.device(a=place.a + 1), self.chain_sem.at[part, 0, step]
                ).wait_send()

            @pl.when((place.a > 0) & (place.a + step < place.chain))
            def _():
                self.copy(
                    part, place.shard(a=place.a + step), place.device(a=place.a - 1), self.chain_sem.at[part, 1, step]
                ).wait_send()

            return carry

        lax.fori_loop(0, place.chain - 1, sent, 0)


def gather_kernel(chain, parts, count, *refs):
    own, full = refs[:count], refs[count : 2 * count]
    chain_sem, send_sem, recv_sem, keep_sem = refs[2 * count :]
    place = Place(chain)
    mine = place.shard()
    place.greet()
    engine = Gather(place, parts, own, full, (chain_sem, send_sem, recv_sem))
    keeps = [
        pltpu.make_async_copy(own[at], full[at].at[mine], keep_sem.at[at]) for at in range(count)
    ]
    numbers = range(len(parts))
    for part in numbers:
        engine.begin(part)
    for keep in keeps:
        keep.start()

    def step(at, carry):
        for part in numbers:
            engine.chain_step(part, at)

        @pl.when(at == 0)
        def _():
            for part in numbers:
                engine.cross_step(part, 0)

        @pl.when(at > 0)
        def _():
            for part in numbers:
                engine.cross_step(part, at)

        return carry

    lax.fori_loop(0, chain - 1, step, 0)
    for part in numbers:
        engine.cross_step(part, chain - 1)
    for part in numbers:
        engine.last_step(part, 0)

    def last(at, carry):
        for part in numbers:
            engine.last_step(part, at)
        return carry

    lax.fori_loop(1, chain, last, 0)
    for part in numbers:
        engine.finish(part)
    for keep in keeps:
        keep.wait()


def gather_all(chain, shards):
    count = len(shards)
    devices = 8 * chain
    parts = halves([item.shape[1] for item in shards])
    return pl.pallas_call(
        functools.partial(gather_kernel, chain, parts, count),
        out_shape=[jax.ShapeDtypeStruct((devices,) + item.shape, item.dtype) for item in shards],
        in_specs=[pl.BlockSpec(memory_space=pl.ANY)] * count,
        out_specs=[pl.BlockSpec(memory_space=pl.ANY)] * count,
        scratch_shapes=[
            pltpu.SemaphoreType.DMA((len(parts), 2, chain)),
            pltpu.SemaphoreType.DMA((len(parts),)),
            pltpu.SemaphoreType.DMA((len(parts), devices)),
            pltpu.SemaphoreType.DMA((count,)),
        ],
        compiler_params=pltpu.CompilerParams(collective_id=0, has_side_effects=True),
        name="gather_all",
    )(*shards)


class Scatter:
    def __init__(self, place, parts, terms, got, sems):
        self.place, self.parts, self.terms = place, parts, terms
        self.got = got
        self.send_sem, self.recv_sem, self.chain_send, self.chain_recv = sems

    def pick(self, ref, lead, part):
        _, first, width, _ = self.parts[part]
        return ref.at[lead + (slice(None), pl.ds(first, width))]

    def exchange(self, part, level, src, dst, to):
        return pltpu.make_async_remote_copy(
            src_ref=src,
            dst_ref=dst,
            send_sem=self.send_sem.at[part, level],
            recv_sem=self.recv_sem.at[part, level],
            device_id=to,
            device_id_type=MESH,
        )

    def core(self, part):
        place = self.place
        at = self.parts[part][0]
        every = slice(None)
        return self.exchange(
            part,
            0,
            self.pick(self.terms[at], (every, every, every, 1 - place.d), part),
            self.pick(self.got[at][0], (every, every, every), part),
            place.device(d=1 - place.d),
        )

    def lead(self, part, level, mine):
        place = self.place
        every = slice(None)
        first = self.parts[part][3]
        b = place.b if mine else 1 - place.b
        c = place.c if mine else 1 - place.c
        if level == 1:
            return (every, b, every) if first == "b" else (every, every, c)
        return (every, c) if first == "b" else (every, b)

    def pair(self, part, level):
        place = self.place
        at, _, _, first = self.parts[part]
        axis = first if level == 1 else ("c" if first == "b" else "b")
        to = place.device(b=1 - place.b) if axis == "b" else place.device(c=1 - place.c)
        every = slice(None)
        dst = (every, every) if level == 1 else (every,)
        return self.exchange(
            part,
            level,
            self.pick(self.got[at][level - 1], self.lead(part, level, False), part),
            self.pick(self.got[at][level], dst, part),
            to,
        )

    def add_core(self, part):
        place = self.place
        at, first, width, _ = self.parts[part]
        self.core(part).wait_recv()
        terms, got = self.terms[at], self.got[at][0]
        columns = pl.ds(first, width)

        def one(i, carry):
            x = i // 4
            y = i // 2 % 2
            z = i % 2
            got[x, y, z, :, columns] = got[x, y, z, :, columns] + terms[x, y, z, place.d, :, columns]
            return carry

        lax.fori_loop(0, 4 * place.chain, one, 0)

    def add_pair(self, part, level):
        place = self.place
        at, first, width, axis = self.parts[part]
        self.pair(part, level).wait_recv()
        before, got = self.got[at][level - 1], self.got[at][level]
        columns = pl.ds(first, width)

        def one(i, carry):
            if level == 1:
                x, y = i // 2, i % 2
                if axis == "b":
                    kept = before[x, place.b, y, :, columns]
                else:
                    kept = before[x, y, place.c, :, columns]
                got[x, y, :, columns] = got[x, y, :, columns] + kept
            else:
                kept = before[i, place.c if axis == "b" else place.b, :, columns]
                got[i, :, columns] = got[i, :, columns] + kept
            return carry

        lax.fori_loop(0, (2 if level == 1 else 1) * place.chain, one, 0)

    def hop(self, part, way, row):
        place = self.place
        at = self.parts[part][0]
        to = place.device(a=place.a + 1) if way == 0 else place.device(a=place.a - 1)
        return pltpu.make_async_remote_copy(
            src_ref=self.pick(self.got[at][2], (row,), part),
            dst_ref=self.pick(self.got[at][3 + way], (row,), part),
            send_sem=self.chain_send.at[part, row],
            recv_sem=self.chain_recv.at[part, way, row],
            device_id=to,
            device_id_type=MESH,
        )

    def take(self, part, way, row):
        place = self.place
        at, first, width, _ = self.parts[part]
        columns = pl.ds(first, width)
        self.hop(part, way, row).wait_recv()
        got = self.got[at][2]
        got[row, :, columns] = got[row, :, columns] + self.got[at][3 + way][row, :, columns]

    def chain_step(self, part, step):
        place = self.place
        top = place.chain - 1 - step

        @pl.when(place.a < top)
        def _():
            @pl.when(place.a > 0)
            def _():
                self.take(part, 0, top)

            self.hop(part, 0, top).start()

        @pl.when(place.a > step)
        def _():
            @pl.when(place.a < place.chain - 1)
            def _():
                self.take(part, 1, step)

            self.hop(part, 1, step).start()

    def result(self, part, out):
        place = self.place
        at, first, width, _ = self.parts[part]
        columns = pl.ds(first, width)
        a = place.a
        got = self.got[at]

        def add(way):
            self.hop(part, way, a).wait_recv()
            out[at][:, columns] = out[at][:, columns] + got[3 + way][a, :, columns].astype(jnp.float32)

        out[at][:, columns] = got[2][a, :, columns].astype(jnp.float32)
        pl.when(a > 0)(lambda: add(0))
        pl.when(a < place.chain - 1)(lambda: add(1))

    def finish(self, part):
        place = self.place
        self.core(part).wait_send()
        for level in (1, 2):
            self.pair(part, level).wait_send()

        def one(row, carry):
            @pl.when(row > place.a)
            def _():
                self.hop(part, 0, row).wait_send()

            @pl.when(row < place.a)
            def _():
                self.hop(part, 1, row).wait_send()

            return carry

        lax.fori_loop(0, place.chain, one, 0)


def scatter_buffers(chain, shapes):
    out = []
    for rows, width, dtype in shapes:
        for lead in ((chain, 2, 2), (chain, 2), (chain,), (chain,), (chain,)):
            out.append(pltpu.VMEM(lead + (rows, width), dtype))
    return out


def scatter_kernel(chain, parts, count, *refs):
    terms, out = refs[:count], refs[count : 2 * count]
    buffers = refs[2 * count : 7 * count]
    sems = refs[7 * count :]
    got = [buffers[5 * at : 5 * at + 5] for at in range(count)]
    place = Place(chain)
    place.greet()
    engine = Scatter(place, parts, terms, got, sems)
    numbers = range(len(parts))
    for part in numbers:
        engine.core(part).start()
    for part in numbers:
        engine.add_core(part)
        engine.pair(part, 1).start()
    for part in numbers:
        engine.add_pair(part, 1)
        engine.pair(part, 2).start()
    for part in numbers:
        engine.add_pair(part, 2)

        def step(at, carry, part=part):
            engine.chain_step(part, at)
            return carry

        lax.fori_loop(0, chain - 1, step, 0)
    for part in numbers:
        engine.result(part, out)
    for part in numbers:
        engine.finish(part)


def scatter_all(chain, terms):
    count = len(terms)
    parts = halves([item.shape[-1] for item in terms])
    return pl.pallas_call(
        functools.partial(scatter_kernel, chain, parts, count),
        out_shape=[jax.ShapeDtypeStruct(item.shape[-2:], jnp.float32) for item in terms],
        in_specs=[pl.BlockSpec(memory_space=pltpu.VMEM)] * count,
        out_specs=[pl.BlockSpec(memory_space=pltpu.VMEM)] * count,
        scratch_shapes=scatter_buffers(chain, [item.shape[-2:] + (item.dtype,) for item in terms])
        + [
            pltpu.SemaphoreType.DMA((len(parts), 3)),
            pltpu.SemaphoreType.DMA((len(parts), 3)),
            pltpu.SemaphoreType.DMA((len(parts), chain)),
            pltpu.SemaphoreType.DMA((len(parts), 2, chain)),
        ],
        compiler_params=pltpu.CompilerParams(
            collective_id=1, has_side_effects=True, vmem_limit_bytes=60 * 2**20
        ),
        name="scatter_all",
    )(*terms)


def layer_norm(values, gain, shift):
    center = values - jnp.mean(values, axis=-1, keepdims=True)
    spread = jnp.mean(center * center, axis=-1, keepdims=True)
    return center * lax.rsqrt(spread + 1e-05) * gain + shift


def gelu_exact(values):
    return jax.nn.gelu(values, approximate=False)


def trans_dot(left, right):
    return lax.dot_general(
        left, right, (((0,), (0,)), ((), ())), preferred_element_type=jnp.float32
    )


def back_dot(left, right):
    return lax.dot_general(
        left, right, (((1,), (1,)), ((), ())), preferred_element_type=jnp.float32
    )


def start_rows(sample_counts, gy_count):
    grouped = sample_counts.reshape(sample_counts.shape[:-1] + (-1, gy_count))
    return (jnp.cumsum(grouped, axis=-2) - grouped).reshape(sample_counts.shape)


def attend_forward(pieces):
    query_rows, key_rows, value_rows, labels = pieces
    score_scale = query_rows.shape[-1] ** (-0.5)
    allowed = labels[:, :, None] == labels[:, None, :]
    scores = (
        jnp.einsum("gqhe,gkhe->ghqk", query_rows, key_rows, preferred_element_type=jnp.float32)
        * score_scale
    )
    scores = jnp.where(allowed[:, None], scores, -1000000000.0)
    row_peak = jnp.max(scores, axis=-1, keepdims=True)
    expo = jnp.exp(scores - row_peak)
    row_total = jnp.sum(expo, axis=-1, keepdims=True)
    attn_probs = (expo / row_total).astype(jnp.bfloat16)
    context = jnp.einsum(
        "ghqk,gkhe->gqhe", attn_probs, value_rows, preferred_element_type=jnp.float32
    )
    return (context.astype(jnp.bfloat16), row_peak[..., 0] + jnp.log(row_total[..., 0]))


def attend_backward(pieces):
    query_rows, key_rows, value_rows, labels, log_total, grad_context = pieces
    score_scale = query_rows.shape[-1] ** (-0.5)
    allowed = labels[:, :, None] == labels[:, None, :]
    scores = (
        jnp.einsum("gqhe,gkhe->ghqk", query_rows, key_rows, preferred_element_type=jnp.float32)
        * score_scale
    )
    scores = jnp.where(allowed[:, None], scores, -1000000000.0)
    probs_full = jnp.exp(scores - log_total[..., None])
    probs_low = probs_full.astype(jnp.bfloat16)
    grad_probs = jnp.einsum(
        "gqhe,gkhe->ghqk", grad_context, value_rows, preferred_element_type=jnp.float32
    )
    row_delta = jnp.sum(probs_full * grad_probs, axis=-1, keepdims=True)
    grad_scores = (probs_full * (grad_probs - row_delta)).astype(jnp.bfloat16)
    grad_query = (
        jnp.einsum("ghqk,gkhe->gqhe", grad_scores, key_rows, preferred_element_type=jnp.float32)
        * score_scale
    )
    grad_key = (
        jnp.einsum("ghqk,gqhe->gkhe", grad_scores, query_rows, preferred_element_type=jnp.float32)
        * score_scale
    )
    grad_value = jnp.einsum(
        "ghqk,gqhe->gkhe", probs_low, grad_context, preferred_element_type=jnp.float32
    )
    return (
        grad_query.astype(jnp.bfloat16),
        grad_key.astype(jnp.bfloat16),
        grad_value.astype(jnp.bfloat16),
    )


def per_device(
    tokens,
    land_mask,
    counts,
    ln1_gain,
    ln1_shift,
    qkv_weight,
    qv_bias,
    out_weight,
    out_bias,
    ln2_gain,
    ln2_shift,
    up_weight,
    up_bias,
    down_weight,
    down_bias,
    cotangent,
):
    chain = lax.axis_size("gx") // 2
    devices = 8 * chain
    samples, patches, model_width = tokens.shape
    small = [ln1_gain, ln1_shift, qv_bias[0], qv_bias[1], out_bias, ln2_gain, ln2_shift, down_bias, up_bias]
    vector_rows = jnp.stack([jnp.pad(item, (0, 128 - item.shape[0])) for item in small])
    vector_rows = jnp.pad(vector_rows, ((0, 16 - len(small)), (0, 0)))
    qkv_all, out_all, up_all, down_all, vectors = gather_all(
        chain, [qkv_weight, out_weight, up_weight, down_weight, vector_rows]
    )
    qkv_full = qkv_all.reshape(-1, qkv_weight.shape[1])
    out_full = out_all.reshape(-1, out_weight.shape[1])
    up_full = up_all.reshape(-1, up_weight.shape[1])
    down_full = down_all.reshape(-1, down_weight.shape[1])
    (gain_one, shift_one, bias_q, bias_v, bias_out, gain_two, shift_two, bias_down, bias_up) = [
        vectors[:, at, : item.shape[0]].reshape(-1) for at, item in enumerate(small)
    ]
    bias_qv = jnp.stack([bias_q, bias_v])
    gy_count = lax.axis_size("gy")
    row_index = lax.axis_index("gy")
    column_index = lax.axis_index("gx")
    device = column_index * gy_count + row_index
    own_count = lax.dynamic_slice_in_dim(counts, device * samples, samples)
    land_rank = jnp.cumsum(land_mask, axis=1) - 1
    kept = (land_mask == 1) & (land_rank < own_count[:, None])
    visible = kept.reshape(-1)
    per_peer = samples // gy_count
    slot_capacity = 3 * patches * per_peer // 4
    own_dest = jnp.arange(samples, dtype=jnp.int32) % gy_count
    own_offset = start_rows(own_count, gy_count)
    target = own_dest[:, None] * slot_capacity + own_offset[:, None] + land_rank
    target = jnp.where(kept, target, gy_count * slot_capacity).reshape(-1)
    send_rows = (
        jnp.zeros((gy_count * slot_capacity, model_width), jnp.bfloat16)
        .at[target]
        .set(tokens.reshape(-1, model_width), mode="drop")
    )
    send_grads = (
        jnp.zeros((gy_count * slot_capacity, model_width), jnp.bfloat16)
        .at[target]
        .set(cotangent.reshape(-1, model_width), mode="drop")
    )
    slot_rows = jnp.arange(slot_capacity, dtype=jnp.int32)
    first_count = own_count[:gy_count, None]
    both_count = first_count + own_count[gy_count:, None]
    labels = jnp.where(slot_rows < first_count, 0, jnp.where(slot_rows < both_count, 1, 2))
    rows_in = send_rows
    rows_grad = send_grads
    per_step = math.gcd(gy_count, max(1, -(-512 // slot_capacity)))
    total_rows = rows_in.shape[0]
    inputs = rows_in.astype(jnp.float32)
    normed_f, norm_one_pull = jax.vjp(
        layer_norm, inputs, gain_one.astype(jnp.float32), shift_one.astype(jnp.float32)
    )
    normed = normed_f.astype(jnp.bfloat16)
    joined_qkv = jnp.dot(normed, qkv_full, preferred_element_type=jnp.float32)
    bias_pair = bias_qv.astype(jnp.float32)
    queries = (joined_qkv[:, :model_width] + bias_pair[0]).astype(jnp.bfloat16)
    key_rows = joined_qkv[:, model_width : 2 * model_width].astype(jnp.bfloat16)
    value_rows = (joined_qkv[:, 2 * model_width :] + bias_pair[1]).astype(jnp.bfloat16)
    step_count = gy_count // per_step
    head_shape = (step_count, per_step, slot_capacity, HEADS, HD)
    query_blocks = queries.reshape(head_shape)
    key_blocks = key_rows.reshape(head_shape)
    value_blocks = value_rows.reshape(head_shape)
    label_blocks = labels.reshape(step_count, per_step, slot_capacity)
    context_blocks, log_totals = lax.map(
        attend_forward, (query_blocks, key_blocks, value_blocks, label_blocks)
    )
    context = context_blocks.reshape(total_rows, model_width)
    middle = (
        inputs
        + jnp.dot(context, out_full, preferred_element_type=jnp.float32)
        + bias_out.astype(jnp.float32)
    )
    normed_two_f, norm_two_pull = jax.vjp(
        layer_norm, middle, gain_two.astype(jnp.float32), shift_two.astype(jnp.float32)
    )
    normed_two = normed_two_f.astype(jnp.bfloat16)
    hidden = jnp.dot(normed_two, up_full, preferred_element_type=jnp.float32) + bias_up.astype(
        jnp.float32
    )
    active_f, gelu_pull = jax.vjp(gelu_exact, hidden)
    active = active_f.astype(jnp.bfloat16)
    result = (
        middle
        + jnp.dot(active, down_full, preferred_element_type=jnp.float32)
        + bias_down.astype(jnp.float32)
    )
    output_rows = result.astype(jnp.bfloat16)
    upstream = rows_grad.astype(jnp.float32)
    grad_down_weight = trans_dot(active, rows_grad)
    grad_down_bias = jnp.sum(upstream, axis=0)
    grad_active = back_dot(rows_grad, down_full)
    grad_hidden = gelu_pull(grad_active)[0].astype(jnp.bfloat16)
    grad_up_weight = trans_dot(normed_two, grad_hidden)
    grad_up_bias = jnp.sum(grad_hidden.astype(jnp.float32), axis=0)
    grad_normed_two = back_dot(grad_hidden, up_full)
    grad_mid_norm, grad_gain_two, grad_shift_two = norm_two_pull(grad_normed_two)
    grad_middle = upstream + grad_mid_norm
    grad_branch = grad_middle.astype(jnp.bfloat16)
    grad_out_weight = trans_dot(context, grad_branch)
    grad_out_bias = jnp.sum(grad_branch.astype(jnp.float32), axis=0)
    grad_context = back_dot(grad_branch, out_full).astype(jnp.bfloat16)
    grad_query_b, grad_key_b, grad_value_b = lax.map(
        attend_backward,
        (
            query_blocks,
            key_blocks,
            value_blocks,
            label_blocks,
            log_totals,
            grad_context.reshape(head_shape),
        ),
    )
    grad_query = grad_query_b.reshape(total_rows, model_width)
    grad_value = grad_value_b.reshape(total_rows, model_width)
    grad_joined = jnp.concatenate(
        [grad_query, grad_key_b.reshape(total_rows, model_width), grad_value], axis=1
    )
    grad_qkv_weight = trans_dot(normed, grad_joined)
    grad_qv_bias = jnp.stack(
        [
            jnp.sum(grad_query.astype(jnp.float32), axis=0),
            jnp.sum(grad_value.astype(jnp.float32), axis=0),
        ]
    )
    grad_normed = back_dot(grad_joined, qkv_full)
    grad_in_norm, grad_gain_one, grad_shift_one = norm_one_pull(grad_normed)
    input_grads = (grad_middle + grad_in_norm).astype(jnp.bfloat16)

    def terms(value):
        return value.astype(jnp.bfloat16).reshape(chain, 2, 2, 2, -1, value.shape[-1])

    vector_grads = [
        grad_gain_one,
        grad_shift_one,
        grad_qv_bias[0],
        grad_qv_bias[1],
        grad_out_bias,
        grad_gain_two,
        grad_shift_two,
        grad_down_bias,
        grad_up_bias,
    ]
    vector_terms = jnp.stack(
        [
            jnp.pad(item.reshape(devices, -1), ((0, 0), (0, 128 - item.shape[0] // devices)))
            for item in vector_grads
        ],
        axis=1,
    )
    vector_terms = jnp.pad(vector_terms, ((0, 0), (0, 16 - len(small)), (0, 0)))
    sum_qkv, sum_out, sum_up, sum_down, sum_vectors = scatter_all(
        chain,
        [
            terms(grad_qkv_weight),
            terms(grad_out_weight),
            terms(grad_up_weight),
            terms(grad_down_weight),
            vector_terms.reshape(chain, 2, 2, 2, 16, 128),
        ],
    )
    sums = [sum_vectors[at, : item.shape[0]] for at, item in enumerate(small)]
    pick_rows = jnp.where(target < gy_count * slot_capacity, target, 0)
    out_flat = output_rows[pick_rows]
    grad_flat = input_grads[pick_rows]
    zero_value = jnp.zeros((), jnp.bfloat16)
    out_tokens = jnp.where(visible[:, None], out_flat, zero_value).reshape(
        samples, patches, model_width
    )
    grad_tokens = jnp.where(visible[:, None], grad_flat, zero_value).reshape(
        samples, patches, model_width
    )
    return (
        out_tokens,
        grad_tokens,
        sums[0],
        sums[1],
        sum_qkv,
        jnp.stack([sums[2], sums[3]]),
        sum_out,
        sums[4],
        sums[5],
        sums[6],
        sum_up,
        sums[8],
        sum_down,
        sums[7],
    )


def solution(mesh):
    placed = (
        P(("gx", "gy"), None, None),
        P(("gx", "gy"), None),
        P(),
        P(("gx", "gy")),
        P(("gx", "gy")),
        P(("gx", "gy"), None),
        P(None, ("gx", "gy")),
        P(("gx", "gy"), None),
        P(("gx", "gy")),
        P(("gx", "gy")),
        P(("gx", "gy")),
        P(("gx", "gy"), None),
        P(("gx", "gy")),
        P(("gx", "gy"), None),
        P(("gx", "gy")),
        P(("gx", "gy"), None, None),
    )
    return jax.shard_map(
        per_device,
        mesh=mesh,
        in_specs=placed,
        out_specs=(
            P(("gx", "gy"), None, None),
            P(("gx", "gy"), None, None),
            P(("gx", "gy")),
            P(("gx", "gy")),
            P(("gx", "gy"), None),
            P(None, ("gx", "gy")),
            P(("gx", "gy"), None),
            P(("gx", "gy")),
            P(("gx", "gy")),
            P(("gx", "gy")),
            P(("gx", "gy"), None),
            P(("gx", "gy")),
            P(("gx", "gy"), None),
            P(("gx", "gy")),
        ),
        check_vma=False,
    )
```

```python
import functools
import types

import jax
import jax.numpy as jnp
from jax import lax
from jax.experimental import pallas as pl
from jax.experimental.pallas import tpu as pltpu
from jax.sharding import PartitionSpec as P

HEADS = 12
HD = 64
MESH = pl.DeviceIdType.MESH


class Place:
    def __init__(self, chain):
        gx = lax.axis_index("gx")
        gy = lax.axis_index("gy")
        self.chain = chain
        self.a = gx // 2
        self.b = gx % 2
        self.c = gy // 2
        self.d = gy % 2

    def shard(self, a=None, b=None, c=None, d=None):
        a = self.a if a is None else a
        b = self.b if b is None else b
        c = self.c if c is None else c
        d = self.d if d is None else d
        return ((a * 2 + b) * 2 + c) * 2 + d

    def device(self, a=None, b=None, c=None, d=None):
        a = self.a if a is None else a
        b = self.b if b is None else b
        c = self.c if c is None else c
        d = self.d if d is None else d
        return (a * 2 + b, c * 2 + d)

    def greet(self):
        barrier = pltpu.get_barrier_semaphore()
        has_below = self.a > 0
        has_above = self.a < self.chain - 1
        for to in (
            self.device(d=1 - self.d),
            self.device(c=1 - self.c),
            self.device(b=1 - self.b),
        ):
            pl.semaphore_signal(barrier, inc=1, device_id=to, device_id_type=MESH)

        @pl.when(has_below)
        def _():
            pl.semaphore_signal(
                barrier, inc=1, device_id=self.device(a=self.a - 1), device_id_type=MESH
            )

        @pl.when(has_above)
        def _():
            pl.semaphore_signal(
                barrier, inc=1, device_id=self.device(a=self.a + 1), device_id_type=MESH
            )

        pl.semaphore_wait(
            barrier, 3 + has_below.astype(jnp.int32) + has_above.astype(jnp.int32)
        )


def halves(widths):
    parts = []
    for at, width in enumerate(widths):
        if width % 256:
            parts.append((at, 0, width, "b"))
        else:
            parts.append((at, 0, width // 2, "b"))
            parts.append((at, width // 2, width // 2, "c"))
    return parts


class Gather:
    def __init__(self, place, parts, own, full, sems):
        self.place, self.parts, self.own, self.full = place, parts, own, full
        self.chain_sem, self.send_sem, self.recv_sem = sems

    def view(self, part, index):
        at, first, width, _ = self.parts[part]
        return self.full[at].at[index, :, pl.ds(first, width)]

    def copy(self, part, index, to, send, own=False):
        at, first, width, _ = self.parts[part]
        src = self.own[at].at[:, pl.ds(first, width)] if own else self.view(part, index)
        return pltpu.make_async_remote_copy(
            src_ref=src,
            dst_ref=self.view(part, index),
            send_sem=send,
            recv_sem=self.recv_sem.at[part, index],
            device_id=to,
            device_id_type=MESH,
        )

    def flip(self, axis):
        place = self.place
        return {axis: 1 - {"b": place.b, "c": place.c, "d": place.d}[axis]}

    def links(self, part):
        first = self.parts[part][3]
        return first, ("c" if first == "b" else "b")

    def send_pair(self, part, index, axis, own=False):
        self.copy(part, index, self.place.device(**self.flip(axis)), self.send_sem.at[part], own).start()

    def arrived(self, part, index):
        self.copy(part, index, self.place.device(d=1 - self.place.d), self.send_sem.at[part]).wait_recv()

    def begin(self, part):
        place = self.place
        mine = place.shard()
        first, second = self.links(part)

        @pl.when(place.a < place.chain - 1)
        def _():
            self.copy(part, mine, place.device(a=place.a + 1), self.chain_sem.at[part, 0, 0], True).start()

        @pl.when(place.a > 0)
        def _():
            self.copy(part, mine, place.device(a=place.a - 1), self.chain_sem.at[part, 1, 0], True).start()

        for axis in (first, second, "d"):
            self.send_pair(part, mine, axis, True)

    def chain_step(self, part, step):
        place = self.place
        first, second = self.links(part)

        @pl.when((place.a - 1 - step >= 0) & (step < place.chain - 1))
        def _():
            index = place.shard(a=place.a - 1 - step)
            self.arrived(part, index)

            @pl.when(place.a < place.chain - 1)
            def _():
                self.copy(
                    part, index, place.device(a=place.a + 1), self.chain_sem.at[part, 0, step + 1]
                ).start()

            for axis in (first, second, "d"):
                self.send_pair(part, index, axis)

        @pl.when((place.a + 1 + step < place.chain) & (step < place.chain - 1))
        def _():
            index = place.shard(a=place.a + 1 + step)
            self.arrived(part, index)

            @pl.when(place.a > 0)
            def _():
                self.copy(
                    part, index, place.device(a=place.a - 1), self.chain_sem.at[part, 1, step + 1]
                ).start()

            for axis in (first, second, "d"):
                self.send_pair(part, index, axis)

    def cross_one(self, part, row):
        place = self.place
        first, second = self.links(part)
        index = place.shard(a=row, **self.flip(first))
        self.arrived(part, index)
        for axis in (second, "d"):
            self.send_pair(part, index, axis)

    def cross_step(self, part, step):
        place = self.place

        @pl.when(place.a - step >= 0)
        def _():
            self.cross_one(part, place.a - step)

        @pl.when((place.a + step < place.chain) & (step > 0))
        def _():
            self.cross_one(part, place.a + step)

    def last_one(self, part, row, other):
        place = self.place
        first, second = self.links(part)
        where = self.flip(second)
        if other:
            where.update(self.flip(first))
        index = place.shard(a=row, **where)
        self.arrived(part, index)
        self.send_pair(part, index, "d")

    def last_step(self, part, step):
        place = self.place

        @pl.when((place.a - step >= 0) & (step >= 0))
        def _():
            for other in (False, True):
                self.last_one(part, place.a - step, other)

        @pl.when((place.a + step < place.chain) & (step > 0))
        def _():
            for other in (False, True):
                self.last_one(part, place.a + step, other)

    def serve(self, group, at):
        chain = self.place.chain

        def one(turn, carry):
            for part in group:
                self.chain_step(part, turn)
            for part in group:
                self.cross_step(part, turn)
            for part in group:
                self.last_step(part, turn - 1)
            return carry

        low, high = at * (chain + 1) // 5, (at + 1) * (chain + 1) // 5
        if high - low == 1:
            one(low, 0)
        else:
            lax.fori_loop(low, high, one, 0)

    def finish(self, part):
        place = self.place

        def one(at, carry):
            self.arrived(part, at * 2 + 1 - place.d)
            return carry

        lax.fori_loop(0, 4 * place.chain, one, 0)
        at, first, width, _ = self.parts[part]
        block = self.full[at].at[pl.ds(0, 7 * place.chain), :, pl.ds(first, width)]
        pltpu.make_async_copy(block, block, self.send_sem.at[part]).wait()

        def sent(step, carry):
            @pl.when((place.a < place.chain - 1) & (place.a - step >= 0))
            def _():
                self.copy(
                    part, place.shard(a=place.a - step), place.device(a=place.a + 1), self.chain_sem.at[part, 0, step]
                ).wait_send()

            @pl.when((place.a > 0) & (place.a + step < place.chain))
            def _():
                self.copy(
                    part, place.shard(a=place.a + step), place.device(a=place.a - 1), self.chain_sem.at[part, 1, step]
                ).wait_send()

            return carry

        lax.fori_loop(0, place.chain - 1, sent, 0)


class Scatter:
    def __init__(self, place, parts, terms, kept, got, sems):
        self.place, self.parts, self.terms = place, parts, terms
        self.kept = kept
        self.got = got
        self.send_sem, self.recv_sem, self.chain_send, self.chain_recv = sems

    def pick(self, ref, lead, part):
        _, first, width, _ = self.parts[part]
        return ref.at[lead + (slice(None), pl.ds(first, width))]

    def exchange(self, part, level, src, dst, to):
        return pltpu.make_async_remote_copy(
            src_ref=src,
            dst_ref=dst,
            send_sem=self.send_sem.at[part, level],
            recv_sem=self.recv_sem.at[part, level],
            device_id=to,
            device_id_type=MESH,
        )

    def core(self, part):
        place = self.place
        at = self.parts[part][0]
        every = slice(None)
        return self.exchange(
            part,
            0,
            self.pick(self.terms[at], (every, every, every, 1 - place.d), part),
            self.pick(self.got[at][0], (every, every, every), part),
            place.device(d=1 - place.d),
        )

    def lead(self, part, level, mine):
        place = self.place
        every = slice(None)
        first = self.parts[part][3]
        b = place.b if mine else 1 - place.b
        c = place.c if mine else 1 - place.c
        if level == 1:
            return (every, b, every) if first == "b" else (every, every, c)
        return (every, c) if first == "b" else (every, b)

    def pair(self, part, level):
        place = self.place
        at, _, _, first = self.parts[part]
        axis = first if level == 1 else ("c" if first == "b" else "b")
        to = place.device(b=1 - place.b) if axis == "b" else place.device(c=1 - place.c)
        every = slice(None)
        dst = (every, every) if level == 1 else (every,)
        return self.exchange(
            part,
            level,
            self.pick(self.got[at][level - 1], self.lead(part, level, False), part),
            self.pick(self.got[at][level], dst, part),
            to,
        )

    def add_core(self, part):
        place = self.place
        at, first, width, _ = self.parts[part]
        self.core(part).wait_recv()
        terms, kept, got = self.terms[at], self.kept[at], self.got[at][0]
        columns = pl.ds(first, width)

        def one(i, carry):
            x = i // 4
            y = i // 2 % 2
            z = i % 2
            term = terms[x, y, z, place.d, :, columns] if kept is None else kept[x, y, z, :, columns]
            got[x, y, z, :, columns] = got[x, y, z, :, columns] + term
            return carry

        lax.fori_loop(0, 4 * place.chain, one, 0)

    def add_pair(self, part, level):
        place = self.place
        at, first, width, axis = self.parts[part]
        self.pair(part, level).wait_recv()
        before, got = self.got[at][level - 1], self.got[at][level]
        columns = pl.ds(first, width)

        def one(i, carry):
            if level == 1:
                x, y = i // 2, i % 2
                if axis == "b":
                    kept = before[x, place.b, y, :, columns]
                else:
                    kept = before[x, y, place.c, :, columns]
                got[x, y, :, columns] = got[x, y, :, columns] + kept
            else:
                kept = before[i, place.c if axis == "b" else place.b, :, columns]
                got[i, :, columns] = got[i, :, columns] + kept
            return carry

        lax.fori_loop(0, (2 if level == 1 else 1) * place.chain, one, 0)

    def hop(self, part, way, row):
        place = self.place
        at = self.parts[part][0]
        to = place.device(a=place.a + 1) if way == 0 else place.device(a=place.a - 1)
        slot = row if way == 0 else jnp.where(row == place.a - 1, place.chain, row)
        return pltpu.make_async_remote_copy(
            src_ref=self.pick(self.got[at][2], (row,), part),
            dst_ref=self.pick(self.got[at][3], (slot,), part),
            send_sem=self.chain_send.at[part, row],
            recv_sem=self.chain_recv.at[part, way, row],
            device_id=to,
            device_id_type=MESH,
        )

    def take(self, part, way, row):
        place = self.place
        at, first, width, _ = self.parts[part]
        columns = pl.ds(first, width)
        self.hop(part, way, row).wait_recv()
        got = self.got[at][2]
        got[row, :, columns] = got[row, :, columns] + self.got[at][3][row, :, columns]

    def chain_step(self, part, step):
        place = self.place
        top = place.chain - 1 - step

        @pl.when(place.a < top)
        def _():
            @pl.when(place.a > 0)
            def _():
                self.take(part, 0, top)

            self.hop(part, 0, top).start()

        @pl.when(place.a > step)
        def _():
            @pl.when(place.a < place.chain - 1)
            def _():
                self.take(part, 1, step)

            self.hop(part, 1, step).start()

    def result(self, part, out):
        place = self.place
        at, first, width, _ = self.parts[part]
        columns = pl.ds(first, width)
        a = place.a
        got = self.got[at]

        def add(way):
            self.hop(part, way, a).wait_recv()
            slot = a if way == 0 else place.chain
            out[at][:, columns] = out[at][:, columns] + got[3][slot, :, columns].astype(jnp.float32)

        out[at][:, columns] = got[2][a, :, columns].astype(jnp.float32)
        pl.when(a > 0)(lambda: add(0))
        pl.when(a < place.chain - 1)(lambda: add(1))

    def finish(self, part):
        place = self.place
        self.core(part).wait_send()
        for level in (1, 2):
            self.pair(part, level).wait_send()

        def one(row, carry):
            @pl.when(row > place.a)
            def _():
                self.hop(part, 0, row).wait_send()

            @pl.when(row < place.a)
            def _():
                self.hop(part, 1, row).wait_send()

            return carry

        lax.fori_loop(0, place.chain, one, 0)

    def chain_all(self, group):
        def step(at, carry):
            for part in group:
                self.chain_step(part, at)
            return carry

        lax.fori_loop(0, self.place.chain - 1, step, 0)

    def up_one(self, group, level):
        for part in group:
            if level == 0:
                self.add_core(part)
            else:
                self.add_pair(part, level)
            if level < 2:
                self.pair(part, level + 1).start()


def normalised(values):
    center = values - jnp.mean(values, axis=-1, keepdims=True)
    spread = jnp.mean(center * center, axis=-1, keepdims=True)
    rate = lax.rsqrt(spread + 1e-05)
    return center * rate, rate


def dot(left, right, left_dim=1, right_dim=0):
    return lax.dot_general(
        left, right, (((left_dim,), (right_dim,)), ((), ())), preferred_element_type=jnp.float32
    )


def pick_matrix(target, slot_rows):
    width = target.shape[-1]
    rows = lax.broadcasted_iota(jnp.int32, (slot_rows, width), 0)
    return jnp.where(rows == target, 1.0, 0.0).astype(jnp.bfloat16)


def column_sum(values):
    return jnp.sum(values, axis=0, keepdims=True)


def unpack(names, refs):
    assert len(names) == len(refs)
    return types.SimpleNamespace(**dict(zip(names, refs)))


QKV, OUT, UP, DOWN, VEC = range(5)
GATHER_IN = ("tokens", "cotangent", "target", "counts", "w0", "w1", "w2", "w3", "w4")
KEPT = ("x", "g", "h1", "qkv", "probs", "context", "middle", "h2", "slope", "gd", "full0", "full1", "full2", "full3")
FORWARD_SCRATCH = KEPT + (
    "full4", "pair", "act", "ub", "chain_sem", "send_sem", "recv_sem", "keep_sem", "save_sem", "load_sem", "back_sem",
)


def forward_kernel(chain, parts, *refs):
    n_in = len(GATHER_IN)
    r = unpack(GATHER_IN, refs[:n_in])
    saved = unpack(KEPT, refs[n_in : n_in + len(KEPT)])
    out_tokens, vec = refs[n_in + len(KEPT) : n_in + len(KEPT) + 2]
    s = unpack(FORWARD_SCRATCH, refs[n_in + len(KEPT) + 2 :])
    model = s.x.shape[1]
    slots, _, both = r.target.shape
    slot_rows = s.x.shape[0] // slots
    total = s.x.shape[0]
    patches = both // 2
    place = Place(chain)
    mine = place.shard()
    own = (r.w0, r.w1, r.w2, r.w3, r.w4)
    full = (s.full0, s.full1, s.full2, s.full3, s.full4)
    saves = []

    def save(name):
        copy = pltpu.make_async_copy(
            getattr(s, name), getattr(saved, name), s.save_sem.at[len(saves)]
        )
        copy.start()
        saves.append(copy)

    def load(source, base):
        copies = [
            pltpu.make_async_copy(
                source.at[pl.ds(half * slots, slots)],
                s.pair.at[:, pl.ds(half * patches, patches)],
                s.load_sem.at[base + half],
            )
            for half in range(2)
        ]
        for copy in copies:
            copy.start()
        return copies

    loads = load(r.tokens, 0)
    place.greet()
    engine = Gather(place, parts, own, full, (s.chain_sem, s.send_sem, s.recv_sem))
    groups = [[at for at, part in enumerate(parts) if part[0] == name] for name in range(5)]
    first = groups[VEC] + groups[QKV] + groups[OUT]
    for part in first:
        engine.begin(part)
    keeps = [pltpu.make_async_copy(own[at], full[at].at[mine], s.keep_sem.at[at]) for at in range(5)]
    for keep in keeps:
        keep.start()

    def rows_of(slot):
        return pl.ds(slot * slot_rows, slot_rows)

    def pack(dst):
        for slot in range(slots):
            dst[rows_of(slot), :] = dot(pick_matrix(r.target[slot], slot_rows), s.pair[slot]).astype(
                jnp.bfloat16
            )

    for copy in loads:
        copy.wait()
    pack(s.x)
    loads = load(r.cotangent, 2)
    save("x")
    engine.serve(first, 0)
    for copy in loads:
        copy.wait()
    pack(s.g)
    save("g")
    engine.serve(first, 1)
    engine.serve(first, 2)
    engine.serve(first, 3)
    for part in groups[UP]:
        engine.begin(part)
    engine.serve(first, 4)
    for part in groups[VEC]:
        engine.finish(part)
    for keep in keeps:
        keep.wait()

    devices = s.full4.shape[0]
    share = model // devices
    up_share = s.full2.shape[2] // devices
    per_row = model // up_share

    def place_vector(at, carry):
        rows, up_rows = carry
        piece = s.full4[at].astype(jnp.float32)
        wide = jnp.concatenate([piece, jnp.zeros((16, model - 128), jnp.float32)], axis=1)
        rows = rows + pltpu.roll(wide[:8], at * share, 1)
        moved = pltpu.roll(wide[8:], (at % per_row) * up_share, 1)
        here = lax.broadcasted_iota(jnp.int32, (8, model), 0) == at // per_row
        up_rows = up_rows + jnp.where(here, jnp.broadcast_to(moved[:1], (8, model)), 0.0)
        return rows, up_rows

    zeros = jnp.zeros((8, model), jnp.float32)
    rows, up_rows = lax.fori_loop(0, devices, place_vector, (zeros, zeros))
    vec[...] = rows
    up_turns = s.full2.shape[2] // model
    for at in range(up_turns):
        s.ub[at] = up_rows[at : at + 1]

    def norm_one(slot, carry):
        at = rows_of(slot)
        n, _ = normalised(s.x[at, :].astype(jnp.float32))
        s.h1[at, :] = (n * vec[0:1] + vec[1:2]).astype(jnp.bfloat16)
        return carry

    lax.fori_loop(0, slots, norm_one, 0)
    save("h1")
    engine.serve(groups[UP], 0)
    for part in groups[QKV]:
        engine.finish(part)
    save("full0")

    def project(section):
        bias = vec[2:3] if section == 0 else vec[3:4]
        columns = pl.ds(section * model, model)
        weight = s.full0[:, :, columns].reshape(model, model)

        def chunk(at, carry):
            here = pl.ds(at * (total // 2), total // 2)
            value = dot(s.h1[here, :], weight)
            if section != 1:
                value = value + bias
            value = value.astype(jnp.bfloat16)
            if section == 0:
                value = value * jnp.bfloat16(HD**-0.5)
            s.qkv[section, here, :] = value
            return carry

        lax.fori_loop(0, 2, chunk, 0)

    project(0)
    engine.serve(groups[UP], 1)
    project(1)
    project(2)
    save("qkv")
    engine.serve(groups[UP], 2)
    for part in groups[OUT]:
        engine.finish(part)
    save("full1")
    low_lane = lax.broadcasted_iota(jnp.int32, (slot_rows, 2 * HD), 1) < HD
    none = jnp.zeros((slot_rows, 2 * HD), jnp.bfloat16)

    def attend(slot):
        one = r.counts[slot]
        two = one + r.counts[slot + slots]
        shape = (slot_rows, slot_rows)
        at_row = lax.broadcasted_iota(jnp.int32, shape, 0)
        at_column = lax.broadcasted_iota(jnp.int32, shape, 1)
        same = ((at_row >= one).astype(jnp.int32) + (at_row >= two).astype(jnp.int32)) == (
            (at_column >= one).astype(jnp.int32) + (at_column >= two).astype(jnp.int32)
        )
        bias = jnp.where(same, 0.0, -1000000000.0)

        def heads(turn, carry):
            for inner in range(2):
                pair = turn * 2 + inner
                columns = pl.ds(pl.multiple_of(pair * 2 * HD, 2 * HD), 2 * HD)
                query = s.qkv[0, rows_of(slot), columns]
                key = s.qkv[1, rows_of(slot), columns]
                value = s.qkv[2, rows_of(slot), columns]
                context = None
                for head in range(2):
                    mask = low_lane if head == 0 else ~low_lane
                    scores = dot(jnp.where(mask, query, none), key, 1, 1) + bias
                    expo = jnp.exp(scores - jnp.max(scores, axis=-1, keepdims=True))
                    probs = (expo / jnp.sum(expo, axis=-1, keepdims=True)).astype(jnp.bfloat16)
                    s.probs[slot * HEADS + pair * 2 + head] = probs
                    term = dot(probs, jnp.where(mask, value, none))
                    context = term if context is None else context + term
                s.context[rows_of(slot), columns] = context.astype(jnp.bfloat16)
            return carry

        lax.fori_loop(0, HEADS // 4, heads, 0)

    attend(0)
    engine.serve(groups[UP], 3)
    attend(1)
    engine.serve(groups[UP], 4)
    for part in groups[DOWN]:
        engine.begin(part)
    attend(2)
    attend(3)
    engine.serve(groups[DOWN], 0)
    save("probs")
    save("context")

    def norm_two(slot, carry):
        at = rows_of(slot)
        weight = s.full1[...].reshape(model, model)
        middle = s.x[at, :].astype(jnp.float32) + dot(s.context[at, :], weight) + vec[4:5]
        s.middle[at, :] = middle
        n, _ = normalised(middle)
        s.h2[at, :] = (n * vec[5:6] + vec[6:7]).astype(jnp.bfloat16)
        return carry

    lax.fori_loop(0, slots, norm_two, 0)
    save("middle")
    save("h2")
    engine.serve(groups[DOWN], 1)
    for part in groups[UP]:
        engine.finish(part)
    save("full2")
    down_rows = s.gd.shape[1]

    def hidden_block(block):
        for half in range(2):
            first_column = block * model + half * (model // 2)
            columns = pl.ds(first_column, model // 2)
            weight = s.full2[:, :, columns].reshape(model, model // 2)
            bias = s.ub[block][:, half * (model // 2) : (half + 1) * (model // 2)]

            def chunk(slot, carry, columns=columns, weight=weight, bias=bias):
                at = rows_of(slot)
                value = dot(s.h2[at, :], weight) + bias
                share_of = 0.5 + 0.5 * lax.erf(value * 0.7071067811865476)
                s.act[at, columns] = (value * share_of).astype(jnp.bfloat16)
                slope = share_of + value * jnp.exp(-0.5 * value * value) * 0.3989422804014327
                s.slope[at, columns] = slope.astype(jnp.bfloat16)
                return carry

            lax.fori_loop(0, slots, chunk, 0)
            grad = dot(s.act[:, columns], s.g[...], 0, 0).astype(jnp.bfloat16)
            for at in range(model // 2 // down_rows):
                s.gd[first_column // down_rows + at] = grad[at * down_rows : (at + 1) * down_rows]

    for block in range(up_turns):
        hidden_block(block)
        if block < 3:
            engine.serve(groups[DOWN], 2 + block)
    save("slope")
    save("gd")
    for part in groups[DOWN]:
        engine.finish(part)
    save("full3")
    hidden_width = s.act.shape[1]

    def last(slot, carry):
        at = rows_of(slot)
        weight = s.full3[...].reshape(hidden_width, model)
        value = s.middle[at, :] + dot(s.act[at, :], weight) + vec[7:8]
        matrix = pick_matrix(r.target[slot], slot_rows)
        s.pair[slot] = dot(matrix, value.astype(jnp.bfloat16), 0, 0).astype(jnp.bfloat16)
        return carry

    lax.fori_loop(0, slots, last, 0)
    backs = [
        pltpu.make_async_copy(
            s.pair.at[:, pl.ds(half * patches, patches)],
            out_tokens.at[pl.ds(half * slots, slots)],
            s.back_sem.at[half],
        )
        for half in range(2)
    ]
    for copy in backs:
        copy.start()
    for copy in saves + backs:
        copy.wait()


def any_spec():
    return pl.BlockSpec(memory_space=pl.ANY)


def vmem_spec():
    return pl.BlockSpec(memory_space=pltpu.VMEM)


def run_forward(chain, tokens, cotangent, target, counts, shards):
    devices = 8 * chain
    samples, patches, model = tokens.shape
    slots = target.shape[0]
    total = samples * patches * 3 // 4
    slot_rows = total // slots
    hidden = shards[UP].shape[1]
    parts = halves([item.shape[1] for item in shards])
    low = jnp.bfloat16
    kept = [
        ((total, model), low),
        ((total, model), low),
        ((total, model), low),
        ((3, total, model), low),
        ((slots * HEADS, slot_rows, slot_rows), low),
        ((total, model), low),
        ((total, model), jnp.float32),
        ((total, model), low),
        ((total, hidden), low),
        ((devices,) + shards[DOWN].shape, low),
    ] + [((devices,) + item.shape, low) for item in shards[:4]]
    outs = kept + [((samples, patches, model), low), ((8, model), jnp.float32)]
    scratch = [pltpu.VMEM(*item) for item in kept] + [
        pltpu.VMEM((devices,) + shards[VEC].shape, low),
        pltpu.VMEM((slots, 2 * patches, model), low),
        pltpu.VMEM((total, hidden), low),
        pltpu.VMEM((hidden // model, 1, model), jnp.float32),
        pltpu.SemaphoreType.DMA((len(parts), 2, chain)),
        pltpu.SemaphoreType.DMA((len(parts),)),
        pltpu.SemaphoreType.DMA((len(parts), devices)),
        pltpu.SemaphoreType.DMA((5,)),
        pltpu.SemaphoreType.DMA((len(KEPT),)),
        pltpu.SemaphoreType.DMA((4,)),
        pltpu.SemaphoreType.DMA((2,)),
    ]
    return pl.pallas_call(
        functools.partial(forward_kernel, chain, parts),
        out_shape=[jax.ShapeDtypeStruct(*item) for item in outs],
        in_specs=[any_spec(), any_spec(), vmem_spec(), pl.BlockSpec(memory_space=pltpu.SMEM)] + [any_spec()] * 5,
        out_specs=[any_spec()] * (len(outs) - 1) + [vmem_spec()],
        scratch_shapes=scratch,
        compiler_params=pltpu.CompilerParams(
            collective_id=0, has_side_effects=True, vmem_limit_bytes=60 * 2**20
        ),
        name="forward",
    )(tokens, cotangent, target, counts, *shards)


BACKWARD_IN = ("g", "slope", "w_down", "h2", "gd", "w_up", "middle", "context", "w_out", "qkv", "probs", "h1", "x", "w_qkv", "target", "vec")
BACKWARD_OUT = ("sum0", "sum1", "sum2", "sum3", "sum4", "grad_tokens")
BACKWARD_SCRATCH = (
    "g", "slope", "w_down", "h2", "gd", "w_up", "middle", "context", "w_out", "probs",
    "vg", "ug", "t0", "t1", "t2", "t4",
)
LOADS = ("g", "w_down", "slope", "h2", "gd", "w_up", "middle", "context", "w_out", "probs", "w_qkv", "qkv0", "qkv1", "qkv2", "x", "h1")


def backward_kernel(chain, parts, *refs):
    n_in, n_out, n_s = len(BACKWARD_IN), len(BACKWARD_OUT), len(BACKWARD_SCRATCH)
    r = unpack(BACKWARD_IN, refs[:n_in])
    o = unpack(BACKWARD_OUT, refs[n_in : n_in + n_out])
    at = n_in + n_out
    s = unpack(BACKWARD_SCRATCH, refs[at : at + n_s])
    buffers = refs[at + n_s : at + n_s + 20]
    load_sem, back_sem, *sems = refs[at + n_s + 20 :]
    got = [buffers[4 * k : 4 * k + 4] for k in range(5)]
    total, model = s.g.shape
    hidden = s.slope.shape[1]
    slots, _, both = r.target.shape
    slot_rows = total // slots
    patches = both // 2
    place = Place(chain)
    loads = {}

    def fetch(name, source, into):
        loads[name] = pltpu.make_async_copy(source, into, load_sem.at[LOADS.index(name)])
        loads[name].start()

    def need(*names):
        for name in names:
            loads[name].wait()

    for name in ("g", "w_down", "slope", "h2"):
        fetch(name, getattr(r, name), getattr(s, name))
    fetch("gd", r.gd.at[:, :, :, place.d], s.gd)
    for name in ("w_up", "middle", "context", "w_out", "probs"):
        fetch(name, getattr(r, name), getattr(s, name))
    place.greet()
    engine = Scatter(
        place, parts, (s.t0, s.t1, s.t2, r.gd, s.t4), (None, None, None, s.gd, None), got, sems
    )
    groups = [[k for k, part in enumerate(parts) if part[0] == name] for name in range(5)]
    outs = (o.sum0, o.sum1, o.sum2, o.sum3, o.sum4)
    for part in groups[DOWN]:
        engine.core(part).start()

    def rows_of(slot):
        return pl.ds(slot * slot_rows, slot_rows)

    def shards_of(value, like):
        return value.reshape(like.shape[:5] + (value.shape[-1],)).astype(jnp.bfloat16)

    need("g", "w_down", "slope", "h2")
    s.vg[...] = jnp.zeros_like(s.vg)
    s.ug[...] = jnp.zeros_like(s.ug)
    s.vg[7:8] = column_sum(s.g[...].astype(jnp.float32))

    def hidden_block(block):
        for half in range(2):
            first_column = block * model + half * (model // 2)
            columns = pl.ds(first_column, model // 2)
            weight = s.w_down[pl.ds(first_column, model // 2), :]

            def chunk(slot, carry, columns=columns, weight=weight):
                here = rows_of(slot)
                value = dot(s.g[here, :], weight, 1, 1) * s.slope[here, columns].astype(jnp.float32)
                value = value.astype(jnp.bfloat16)
                s.slope[here, columns] = value
                return carry + column_sum(value.astype(jnp.float32))

            sums = lax.fori_loop(0, slots, chunk, jnp.zeros((1, model // 2), jnp.float32))
            s.ug[block : block + 1, half * (model // 2) : (half + 1) * (model // 2)] = sums
            s.t2[:, :, :, :, :, columns] = shards_of(dot(s.h2[...], s.slope[:, columns], 0, 0), s.t2)

    up_turns = hidden // model
    up_first, up_second = groups[UP]
    hidden_block(0)
    need("gd")
    engine.up_one(groups[DOWN], 0)
    hidden_block(1)
    engine.core(up_first).start()
    hidden_block(2)
    engine.up_one([up_first], 0)
    hidden_block(3)
    engine.core(up_second).start()
    for section in range(3):
        fetch("qkv%d" % section, r.qkv.at[section], s.w_down.at[pl.ds(section * model, model)])
    fetch("x", r.x, s.w_down.at[pl.ds(3 * model, model)])
    engine.up_one(groups[DOWN], 1)
    need("w_up", "middle")
    half_rows = total // 2

    def middle_part(half):
        grad = dot(s.slope[pl.ds(half * half_rows, half_rows), :], s.w_up[...], 1, 1)
        for inner in range(slots // 2):
            here = rows_of(half * (slots // 2) + inner)
            part = grad[inner * slot_rows : (inner + 1) * slot_rows]
            n, rate = normalised(s.middle[here, :])
            s.vg[5:6] += column_sum(part * n)
            s.vg[6:7] += column_sum(part)
            scaled = part * r.vec[5:6]
            mean_one = jnp.mean(scaled, axis=-1, keepdims=True)
            mean_two = jnp.mean(scaled * n, axis=-1, keepdims=True)
            full_grad = s.g[here, :].astype(jnp.float32) + rate * (scaled - mean_one - n * mean_two)
            s.middle[here, :] = full_grad
            branch = full_grad.astype(jnp.bfloat16)
            s.h2[here, :] = branch
            s.vg[4:5] += column_sum(branch.astype(jnp.float32))

    middle_part(0)
    engine.up_one([up_second], 0)
    middle_part(1)
    joined = pl.ds(0, 3 * model)
    fetch("w_qkv", r.w_qkv, s.w_up.at[:, joined])
    fetch("h1", r.h1, s.slope.at[:, pl.ds(3 * model, model)])
    need("context", "w_out")
    s.t1[...] = shards_of(dot(s.context[...], s.h2[...], 0, 0), s.t1)
    for part in groups[OUT]:
        engine.core(part).start()
    engine.up_one(groups[DOWN], 2)

    def to_context(slot, carry):
        here = rows_of(slot)
        s.context[here, :] = dot(s.h2[here, :], s.w_out[...], 1, 1).astype(jnp.bfloat16)
        return carry

    lax.fori_loop(0, slots, to_context, 0)
    engine.up_one(groups[OUT], 0)
    need("qkv0", "qkv1", "qkv2", "probs")
    low_lane = lax.broadcasted_iota(jnp.int32, (slot_rows, 2 * HD), 1) < HD
    none = jnp.zeros((slot_rows, 2 * HD), jnp.bfloat16)

    def attend(slot):
        def heads(turn, carry):
            for inner in range(2):
                pair = turn * 2 + inner
                first_column = pl.multiple_of(pair * 2 * HD, 2 * HD)
                columns = pl.ds(first_column, 2 * HD)
                query = s.w_down[pl.ds(slot * slot_rows, slot_rows), columns]
                key = s.w_down[pl.ds(model + slot * slot_rows, slot_rows), columns]
                value = s.w_down[pl.ds(2 * model + slot * slot_rows, slot_rows), columns]
                grad = s.context[rows_of(slot), columns]
                totals = [None, None, None]
                for head in range(2):
                    mask = low_lane if head == 0 else ~low_lane
                    grad_here = jnp.where(mask, grad, none)
                    low_probs = s.probs[slot * HEADS + pair * 2 + head]
                    probs = low_probs.astype(jnp.float32)
                    weighted = probs * dot(grad_here, value, 1, 1)
                    share = jnp.sum(weighted, axis=-1, keepdims=True)
                    scores = (weighted - probs * share).astype(jnp.bfloat16)
                    terms = (
                        dot(scores, jnp.where(mask, key, none)),
                        dot(scores, jnp.where(mask, query, none), 0, 0),
                        dot(low_probs, grad_here, 0, 0),
                    )
                    totals = [b if a is None else a + b for a, b in zip(totals, terms)]
                totals[0] = totals[0] * HD**-0.5
                for section in range(3):
                    s.slope[rows_of(slot), pl.ds(section * model + first_column, 2 * HD)] = totals[
                        section
                    ].astype(jnp.bfloat16)
            return carry

        lax.fori_loop(0, HEADS // 4, heads, 0)

    attend(0)
    engine.up_one(groups[UP], 1)
    attend(1)
    engine.chain_all(groups[DOWN])
    engine.up_one(groups[OUT], 1)
    attend(2)
    engine.up_one(groups[UP], 2)
    attend(3)
    engine.up_one(groups[OUT], 2)
    engine.chain_all(groups[UP])
    need("h1", "w_qkv", "x")
    h1 = pl.ds(3 * model, model)
    half_width = 3 * model // 2
    for half in range(2):
        for quarter in range(3):
            columns = pl.ds(half * half_width + quarter * (half_width // 3), half_width // 3)
            s.t0[:, :, :, :, :, columns] = shards_of(dot(s.slope[:, h1], s.slope[:, columns], 0, 0), s.t0)
        engine.core(groups[QKV][half]).start()
    s.vg[2:3] = column_sum(s.slope[:, pl.ds(0, model)].astype(jnp.float32))
    s.vg[3:4] = column_sum(s.slope[:, pl.ds(2 * model, model)].astype(jnp.float32))
    engine.chain_all(groups[OUT])

    def spread_at(slot):
        if slot * both + both <= model:
            return s.w_up, slot * both, 3 * model
        return s.g, 0, 0

    def input_part(half):
        grad = dot(s.slope[pl.ds(half * half_rows, half_rows), joined], s.w_up[:, joined], 1, 1)
        for inner in range(slots // 2):
            slot = half * (slots // 2) + inner
            here = rows_of(slot)
            part = grad[inner * slot_rows : (inner + 1) * slot_rows]
            n, rate = normalised(
                s.w_down[pl.ds(3 * model + slot * slot_rows, slot_rows), :].astype(jnp.float32)
            )
            s.vg[0:1] += column_sum(part * n)
            s.vg[1:2] += column_sum(part)
            scaled = part * r.vec[0:1]
            mean_one = jnp.mean(scaled, axis=-1, keepdims=True)
            mean_two = jnp.mean(scaled * n, axis=-1, keepdims=True)
            full_grad = s.middle[here, :] + rate * (scaled - mean_one - n * mean_two)
            matrix = pick_matrix(r.target[slot], slot_rows)
            spread = dot(matrix, full_grad.astype(jnp.bfloat16), 0, 0).astype(jnp.bfloat16)
            spread_ref, row, column = spread_at(slot)
            spread_ref[pl.ds(row, both), pl.ds(column, model)] = spread

    engine.up_one(groups[QKV], 0)
    input_part(0)
    engine.up_one(groups[QKV], 1)
    input_part(1)
    backs = [
        pltpu.make_async_copy(
            spread_at(slot)[0].at[
                pl.ds(spread_at(slot)[1] + half * patches, patches), pl.ds(spread_at(slot)[2], model)
            ],
            o.grad_tokens.at[half * slots + slot],
            back_sem.at[half * slots + slot],
        )
        for half in range(2)
        for slot in range(slots)
    ]
    for copy in backs:
        copy.start()
    devices = 8 * chain
    share = model // devices
    up_share = hidden // devices
    per_row = model // up_share

    def cut_vector(index, carry):
        rows = pltpu.roll(s.vg[...], model - index * share, 1)[:, :128]
        here = lax.broadcasted_iota(jnp.int32, (8, model), 0) == index // per_row
        row = jnp.broadcast_to(column_sum(jnp.where(here, s.ug[...], 0.0)), (8, model))
        up_rows = pltpu.roll(row, model - (index % per_row) * up_share, 1)[:, :128]
        s.t4[index // 8, index // 4 % 2, index // 2 % 2, index % 2] = jnp.concatenate([rows, up_rows], axis=0)
        return carry

    lax.fori_loop(0, devices, cut_vector, 0)
    for part in groups[VEC]:
        engine.core(part).start()
    engine.up_one(groups[VEC], 0)
    for part in groups[DOWN] + groups[UP]:
        engine.result(part, outs)
    engine.up_one(groups[VEC], 1)
    engine.up_one(groups[VEC], 2)
    engine.up_one(groups[QKV], 2)
    engine.chain_all(groups[VEC] + groups[QKV])
    for part in groups[OUT] + groups[VEC] + groups[QKV]:
        engine.result(part, outs)
    for part in range(len(parts)):
        engine.finish(part)
    for copy in backs:
        copy.wait()


def run_backward(chain, kept, target, vec, shards, samples):
    devices = 8 * chain
    total, model = kept.x.shape
    hidden = shards[UP].shape[1]
    slots, _, both = target.shape
    parts = halves([item.shape[1] for item in shards])
    low, wide = jnp.bfloat16, jnp.float32
    lead = (chain, 2, 2, 2)
    fulls = [
        item.reshape(-1, item.shape[-1]) for item in (kept.full0, kept.full1, kept.full2, kept.full3)
    ]
    given = types.SimpleNamespace(
        g=kept.g, slope=kept.slope, w_down=fulls[DOWN], h2=kept.h2,
        gd=kept.gd.reshape(lead + shards[DOWN].shape), w_up=fulls[UP], middle=kept.middle,
        context=kept.context, w_out=fulls[OUT], qkv=kept.qkv, probs=kept.probs, h1=kept.h1, x=kept.x,
        w_qkv=fulls[QKV], target=target, vec=vec,
    )
    scratch = {name: pltpu.VMEM(getattr(given, name).shape, getattr(given, name).dtype) for name in BACKWARD_IN}
    scratch["gd"] = pltpu.VMEM((chain, 2, 2) + shards[DOWN].shape, low)
    scratch["vg"] = pltpu.VMEM((8, model), wide)
    scratch["ug"] = pltpu.VMEM((8, model), wide)
    for at in (QKV, OUT, UP, VEC):
        scratch["t%d" % at] = pltpu.VMEM(lead + shards[at].shape, wide if at == VEC else low)
    arrivals = []
    for at, item in enumerate(shards):
        for front in ((chain, 2, 2), (chain, 2), (chain,), (chain + 1,)):
            arrivals.append(pltpu.VMEM(front + item.shape, wide if at == VEC else low))
    outs = [(item.shape, wide) for item in shards] + [((samples, both // 2, model), low)]
    return pl.pallas_call(
        functools.partial(backward_kernel, chain, parts),
        out_shape=[jax.ShapeDtypeStruct(*item) for item in outs],
        in_specs=[any_spec()] * (len(BACKWARD_IN) - 2) + [vmem_spec()] * 2,
        out_specs=[vmem_spec()] * 5 + [any_spec()],
        scratch_shapes=[scratch[name] for name in BACKWARD_SCRATCH]
        + arrivals
        + [
            pltpu.SemaphoreType.DMA((len(LOADS),)),
            pltpu.SemaphoreType.DMA((2 * slots,)),
            pltpu.SemaphoreType.DMA((len(parts), 3)),
            pltpu.SemaphoreType.DMA((len(parts), 3)),
            pltpu.SemaphoreType.DMA((len(parts), chain)),
            pltpu.SemaphoreType.DMA((len(parts), 2, chain)),
        ],
        compiler_params=pltpu.CompilerParams(
            collective_id=1, has_side_effects=True, vmem_limit_bytes=63 * 2**20
        ),
        name="backward",
    )(*[getattr(given, name) for name in BACKWARD_IN])


def per_device(
    tokens,
    land_mask,
    counts,
    ln1_gain,
    ln1_shift,
    qkv_weight,
    qv_bias,
    out_weight,
    out_bias,
    ln2_gain,
    ln2_shift,
    up_weight,
    up_bias,
    down_weight,
    down_bias,
    cotangent,
):
    chain = lax.axis_size("gx") // 2
    samples = tokens.shape[0]
    slots = lax.axis_size("gy")
    device = lax.axis_index("gx") * slots + lax.axis_index("gy")
    own_count = lax.dynamic_slice_in_dim(counts, device * samples, samples)
    land_rank = jnp.cumsum(land_mask, axis=1) - 1
    kept = (land_mask == 1) & (land_rank < own_count[:, None])
    offset = jnp.concatenate([jnp.zeros((slots,), jnp.int32), own_count[:slots]])
    target = jnp.where(kept, land_rank + offset[:, None], -1)
    target = jnp.concatenate([target[:slots], target[slots:]], axis=1)[:, None, :]
    small = [ln1_gain, ln1_shift, qv_bias[0], qv_bias[1], out_bias, ln2_gain, ln2_shift, down_bias, up_bias]
    vector_rows = jnp.stack([jnp.pad(item, (0, 128 - item.shape[0])) for item in small])
    vector_rows = jnp.pad(vector_rows, ((0, 16 - len(small)), (0, 0)))
    shards = [qkv_weight, out_weight, up_weight, down_weight, vector_rows]
    *kept_arrays, out_tokens, vec = run_forward(chain, tokens, cotangent, target, own_count, shards)
    *sums, grad_tokens = run_backward(
        chain, unpack(KEPT, kept_arrays), target, vec, shards, samples
    )
    cut = [sums[VEC][at, : item.shape[0]] for at, item in enumerate(small)]
    return (
        out_tokens,
        grad_tokens,
        cut[0],
        cut[1],
        sums[QKV],
        jnp.stack([cut[2], cut[3]]),
        sums[OUT],
        cut[4],
        cut[5],
        cut[6],
        sums[UP],
        cut[8],
        sums[DOWN],
        cut[7],
    )


def solution(mesh):
    placed = (
        P(("gx", "gy"), None, None),
        P(("gx", "gy"), None),
        P(),
        P(("gx", "gy")),
        P(("gx", "gy")),
        P(("gx", "gy"), None),
        P(None, ("gx", "gy")),
        P(("gx", "gy"), None),
        P(("gx", "gy")),
        P(("gx", "gy")),
        P(("gx", "gy")),
        P(("gx", "gy"), None),
        P(("gx", "gy")),
        P(("gx", "gy"), None),
        P(("gx", "gy")),
        P(("gx", "gy"), None, None),
    )
    return jax.shard_map(
        per_device,
        mesh=mesh,
        in_specs=placed,
        out_specs=(
            P(("gx", "gy"), None, None),
            P(("gx", "gy"), None, None),
            P(("gx", "gy")),
            P(("gx", "gy")),
            P(("gx", "gy"), None),
            P(None, ("gx", "gy")),
            P(("gx", "gy"), None),
            P(("gx", "gy")),
            P(("gx", "gy")),
            P(("gx", "gy")),
            P(("gx", "gy"), None),
            P(("gx", "gy")),
            P(("gx", "gy"), None),
            P(("gx", "gy")),
        ),
        check_vma=False,
    )
```

```python
import functools
import types

import jax
import jax.numpy as jnp
from jax import lax
from jax.experimental import pallas as pl
from jax.experimental.pallas import tpu as pltpu
from jax.sharding import PartitionSpec as P

HEADS = 12
HD = 64
MESH = pl.DeviceIdType.MESH


class Place:
    def __init__(self, chain):
        gx = lax.axis_index("gx")
        gy = lax.axis_index("gy")
        self.chain = chain
        self.a = gx // 2
        self.b = gx % 2
        self.c = gy // 2
        self.d = gy % 2

    def shard(self, a=None, b=None, c=None, d=None):
        a = self.a if a is None else a
        b = self.b if b is None else b
        c = self.c if c is None else c
        d = self.d if d is None else d
        return a, b, c, d

    def device(self, a=None, b=None, c=None, d=None):
        a = self.a if a is None else a
        b = self.b if b is None else b
        c = self.c if c is None else c
        d = self.d if d is None else d
        return (a * 2 + b, c * 2 + d)

    def greet(self):
        barrier = pltpu.get_barrier_semaphore()
        has_below = self.a > 0
        has_above = self.a < self.chain - 1
        for to in (
            self.device(d=1 - self.d),
            self.device(c=1 - self.c),
            self.device(b=1 - self.b),
        ):
            pl.semaphore_signal(barrier, inc=1, device_id=to, device_id_type=MESH)

        @pl.when(has_below)
        def _():
            pl.semaphore_signal(
                barrier, inc=1, device_id=self.device(a=self.a - 1), device_id_type=MESH
            )

        @pl.when(has_above)
        def _():
            pl.semaphore_signal(
                barrier, inc=1, device_id=self.device(a=self.a + 1), device_id_type=MESH
            )

        pl.semaphore_wait(
            barrier, 3 + has_below.astype(jnp.int32) + has_above.astype(jnp.int32)
        )


def halves(widths):
    parts = []
    for at, width in enumerate(widths):
        if width % 256:
            parts.append((at, 0, width, "b"))
        else:
            parts.append((at, 0, width // 2, "b"))
            parts.append((at, width // 2, width // 2, "c"))
    return parts


class Gather:
    def __init__(self, place, parts, own, full, sems):
        self.place, self.parts, self.own, self.full = place, parts, own, full
        self.chain_sem, self.send_sem, self.recv_sem, self.share_send, self.share_recv = sems

    def view(self, part, index):
        at, first, width, _ = self.parts[part]
        return self.full[at].at[tuple(index) + (slice(None), pl.ds(first, width))]

    def copy(self, part, index, to, send, own=False):
        at, first, width, _ = self.parts[part]
        a, b, c, d = index
        return pltpu.make_async_remote_copy(
            src_ref=self.own[at].at[:, pl.ds(first, width)] if own else self.view(part, index),
            dst_ref=self.view(part, index),
            send_sem=send,
            recv_sem=self.recv_sem.at[part, ((a * 2 + b) * 2 + c) * 2 + d],
            device_id=to,
            device_id_type=MESH,
        )

    def flip(self, axis):
        return {axis: 1 - (self.place.b if axis == "b" else self.place.c)}

    def links(self, part):
        first = self.parts[part][3]
        return first, ("c" if first == "b" else "b")

    def send_pair(self, part, index, level, own=False):
        to = self.place.device(**self.flip(self.links(part)[level]))
        self.copy(part, index, to, self.send_sem.at[part, level], own).start()

    def arrived(self, part, index):
        self.copy(part, index, self.place.device(d=1 - self.place.d), self.send_sem.at[part, 0]).wait_recv()

    def send_chain(self, part, way, index, step, own=False):
        place = self.place
        to = place.device(a=place.a + 1) if way == 0 else place.device(a=place.a - 1)
        return self.copy(part, index, to, self.chain_sem.at[part, way, step], own)

    def begin(self, part):
        place = self.place
        mine = place.shard()
        pl.when(place.a < place.chain - 1)(lambda: self.send_chain(part, 0, mine, 0, True).start())
        pl.when(place.a > 0)(lambda: self.send_chain(part, 1, mine, 0, True).start())
        for level in range(2):
            self.send_pair(part, mine, level, True)

    def each(self, low, high, one):
        if isinstance(low, int) and high - low == 1:
            one(low, 0)
        else:
            lax.fori_loop(low, high, one, 0)

    def along(self, part, third):
        place = self.place
        steps = place.chain - 1

        def one(step, carry):
            @pl.when(place.a - 1 - step >= 0)
            def _():
                index = place.shard(a=place.a - 1 - step)
                self.arrived(part, index)
                pl.when(place.a < steps)(lambda: self.send_chain(part, 0, index, step + 1).start())
                for level in range(2):
                    self.send_pair(part, index, level)

            @pl.when(place.a + 1 + step <= steps)
            def _():
                index = place.shard(a=place.a + 1 + step)
                self.arrived(part, index)
                pl.when(place.a > 0)(lambda: self.send_chain(part, 1, index, step + 1).start())
                for level in range(2):
                    self.send_pair(part, index, level)

            return carry

        self.each(third * steps // 3, (third + 1) * steps // 3, one)

    def at_distance(self, turn, one):
        place = self.place
        steps = place.chain - 1
        if turn == 0:
            one(place.a)
            return

        def both(step, carry):
            pl.when(place.a - step >= 0)(lambda: one(place.a - step))
            pl.when(place.a + step <= steps)(lambda: one(place.a + step))
            return carry

        self.each(1 + (turn - 1) * steps // 3, 1 + turn * steps // 3, both)

    def across(self, part, turn):
        first, _ = self.links(part)

        def one(row):
            index = self.place.shard(a=row, **self.flip(first))
            self.arrived(part, index)
            self.send_pair(part, index, 1)

        self.at_distance(turn, one)

    def last(self, part, turn):
        first, second = self.links(part)

        def one(row):
            self.arrived(part, self.place.shard(a=row, **self.flip(second)))
            self.arrived(part, self.place.shard(a=row, **self.flip(second), **self.flip(first)))

        self.at_distance(turn, one)

    def sharing(self, part, half):
        place = self.place
        every = slice(None)
        if self.links(part)[1] == "c":
            box = (every, every, 1 - place.c if half else place.c, place.d)
        else:
            box = (every, 1 - place.b if half else place.b, every, place.d)
        return pltpu.make_async_remote_copy(
            src_ref=self.view(part, box),
            dst_ref=self.view(part, box),
            send_sem=self.share_send.at[part, half],
            recv_sem=self.share_recv.at[part, half],
            device_id=place.device(d=1 - place.d),
            device_id_type=MESH,
        )

    def finish(self, part):
        place = self.place
        steps = place.chain - 1
        for half in range(2):
            self.sharing(part, half).wait()
        every = slice(None)
        for level, box in enumerate(((every, 0, 0, 0), (every, every, 0, 0))):
            block = self.view(part, box)
            pltpu.make_async_copy(block, block, self.send_sem.at[part, level]).wait()

        def sent(step, carry):
            @pl.when((place.a < steps) & (place.a - step >= 0))
            def _():
                self.send_chain(part, 0, place.shard(a=place.a - step), step).wait_send()

            @pl.when((place.a > 0) & (place.a + step <= steps))
            def _():
                self.send_chain(part, 1, place.shard(a=place.a + step), step).wait_send()

            return carry

        lax.fori_loop(0, steps, sent, 0)


class Scatter:
    def __init__(self, place, parts, terms, kept, got, sems):
        self.place, self.parts, self.terms = place, parts, terms
        self.kept = kept
        self.got = got
        self.send_sem, self.recv_sem, self.chain_send, self.chain_recv = sems

    def rows(self, part):
        return pl.ds(*self.parts[part][4:])

    def pick(self, ref, lead, part):
        first, width = self.parts[part][1:3]
        return ref.at[lead + (slice(None), pl.ds(first, width))]

    def exchange(self, part, level, src, dst, to):
        return pltpu.make_async_remote_copy(
            src_ref=src,
            dst_ref=dst,
            send_sem=self.send_sem.at[part, level],
            recv_sem=self.recv_sem.at[part, level],
            device_id=to,
            device_id_type=MESH,
        )

    def core(self, part):
        place = self.place
        at = self.parts[part][0]
        every = slice(None)
        return self.exchange(
            part,
            0,
            self.pick(self.terms[at], (self.rows(part), every, every, 1 - place.d), part),
            self.pick(self.got[at][0], (self.rows(part), every, every), part),
            place.device(d=1 - place.d),
        )

    def lead(self, part, level, mine):
        place = self.place
        every = slice(None)
        first = self.parts[part][3]
        b = place.b if mine else 1 - place.b
        c = place.c if mine else 1 - place.c
        rows = self.rows(part)
        if level == 1:
            return (rows, b, every) if first == "b" else (rows, every, c)
        return (rows, c) if first == "b" else (rows, b)

    def pair(self, part, level):
        place = self.place
        at, first = self.parts[part][0], self.parts[part][3]
        axis = first if level == 1 else ("c" if first == "b" else "b")
        to = place.device(b=1 - place.b) if axis == "b" else place.device(c=1 - place.c)
        every = slice(None)
        dst = (self.rows(part), every) if level == 1 else (self.rows(part),)
        return self.exchange(
            part,
            level,
            self.pick(self.got[at][level - 1], self.lead(part, level, False), part),
            self.pick(self.got[at][level], dst, part),
            to,
        )

    def add_core(self, part):
        place = self.place
        at, first, width, _, low, rows = self.parts[part]
        self.core(part).wait_recv()
        terms, kept, got = self.terms[at], self.kept[at], self.got[at][0]
        columns = pl.ds(first, width)

        def one(i, carry):
            x, y, z = low + i // 4, i // 2 % 2, i % 2
            term = terms[x, y, z, place.d, :, columns] if kept is None else kept[x - low, y, z, :, columns]
            got[x, y, z, :, columns] = got[x, y, z, :, columns] + term
            return carry

        lax.fori_loop(0, 4 * rows, one, 0)

    def add_pair(self, part, level):
        place = self.place
        at, first, width, axis, low, rows = self.parts[part]
        self.pair(part, level).wait_recv()
        before, got = self.got[at][level - 1], self.got[at][level]
        columns = pl.ds(first, width)

        def one(i, carry):
            if level == 1:
                x, y = low + i // 2, i % 2
                if axis == "b":
                    kept = before[x, place.b, y, :, columns]
                else:
                    kept = before[x, y, place.c, :, columns]
                got[x, y, :, columns] = got[x, y, :, columns] + kept
            else:
                x = low + i
                kept = before[x, place.c if axis == "b" else place.b, :, columns]
                got[x, :, columns] = got[x, :, columns] + kept
            return carry

        lax.fori_loop(0, (2 if level == 1 else 1) * rows, one, 0)

    def hop(self, part, way, row):
        place = self.place
        at = self.parts[part][0]
        to = place.device(a=place.a + 1) if way == 0 else place.device(a=place.a - 1)
        slot = row if way == 0 else jnp.where(row == place.a - 1, place.chain, row)
        return pltpu.make_async_remote_copy(
            src_ref=self.pick(self.got[at][2], (row,), part),
            dst_ref=self.pick(self.got[at][3], (slot,), part),
            send_sem=self.chain_send.at[part, row],
            recv_sem=self.chain_recv.at[part, way, row],
            device_id=to,
            device_id_type=MESH,
        )

    def take(self, part, way, row):
        place = self.place
        at, first, width = self.parts[part][:3]
        columns = pl.ds(first, width)
        self.hop(part, way, row).wait_recv()
        got = self.got[at][2]
        got[row, :, columns] = got[row, :, columns] + self.got[at][3][row, :, columns]

    def chain_step(self, part, step):
        place = self.place
        top = place.chain - 1 - step

        @pl.when(place.a < top)
        def _():
            @pl.when(place.a > 0)
            def _():
                self.take(part, 0, top)

            self.hop(part, 0, top).start()

        @pl.when(place.a > step)
        def _():
            @pl.when(place.a < place.chain - 1)
            def _():
                self.take(part, 1, step)

            self.hop(part, 1, step).start()

    def result(self, part, out):
        place = self.place
        at, first, width = self.parts[part][:3]
        columns = pl.ds(first, width)
        a = place.a
        got = self.got[at]

        def add(way):
            self.hop(part, way, a).wait_recv()
            slot = a if way == 0 else place.chain
            out[at][:, columns] = out[at][:, columns] + got[3][slot, :, columns].astype(jnp.float32)

        out[at][:, columns] = got[2][a, :, columns].astype(jnp.float32)
        pl.when(a > 0)(lambda: add(0))
        pl.when(a < place.chain - 1)(lambda: add(1))

    def finish_pairs(self, part):
        self.core(part).wait_send()
        for level in (1, 2):
            self.pair(part, level).wait_send()

    def finish(self, part):
        place = self.place
        self.finish_pairs(part)

        def one(row, carry):
            @pl.when(row > place.a)
            def _():
                self.hop(part, 0, row).wait_send()

            @pl.when(row < place.a)
            def _():
                self.hop(part, 1, row).wait_send()

            return carry

        lax.fori_loop(0, place.chain, one, 0)

    def chain_all(self, group):
        def step(at, carry):
            for part in group:
                self.chain_step(part, at)
            return carry

        lax.fori_loop(0, self.place.chain - 1, step, 0)

    def chain_one(self, part, near, row):
        place = self.place
        far = place.chain - 1

        @pl.when(place.a == near)
        def _():
            if near > 0:
                self.take(part, 0, row)
            self.hop(part, 0, row).start()

        @pl.when(place.a == far - near)
        def _():
            if near > 0:
                self.take(part, 1, far - row)
            self.hop(part, 1, far - row).start()

    def up_one(self, part, level):
        if level == 0:
            self.add_core(part)
        else:
            self.add_pair(part, level)
        if level < 2:
            self.pair(part, level + 1).start()


def normalised(values):
    center = values - jnp.mean(values, axis=-1, keepdims=True)
    spread = jnp.mean(center * center, axis=-1, keepdims=True)
    rate = lax.rsqrt(spread + 1e-05)
    return center * rate, rate


def dot(left, right, left_dim=1, right_dim=0):
    return lax.dot_general(
        left, right, (((left_dim,), (right_dim,)), ((), ())), preferred_element_type=jnp.float32
    )


def pick_matrix(target, slot_rows):
    width = target.shape[-1]
    rows = lax.broadcasted_iota(jnp.int32, (slot_rows, width), 0)
    return jnp.where(rows == target, 1.0, 0.0).astype(jnp.bfloat16)


def column_sum(values):
    return jnp.sum(values, axis=0, keepdims=True)


def follow(plan, steps, moves):
    for name, *numbers in plan:
        if numbers:
            moves[name](*numbers)
        else:
            steps[name]()


def unpack(names, refs):
    assert len(names) == len(refs)
    return types.SimpleNamespace(**dict(zip(names, refs)))


QKV, OUT, UP, DOWN, VEC = range(5)
PIECES = 1
FORWARD_PLAN = (
    ("gbegin", 1), ("gbegin", 8), ("gbegin", 0), ("gbegin", 2), ("gbegin", 3), ("gc", 1, 0), ("gx", 1, 0),
    ("gc", 8, 0), ("gx", 8, 0), ("gc", 0, 0), ("gx", 0, 0), ("packx",), ("gc", 2, 0), ("gc", 8, 1), ("gx", 2, 0),
    ("gc", 3, 0), ("gc", 0, 1), ("gx", 8, 1), ("gx", 3, 0), ("gl", 8, 0), ("gc", 1, 1), ("packg",), ("gc", 8, 2),
    ("gx", 8, 2), ("gc", 2, 1), ("gx", 1, 1), ("gc", 3, 1), ("gx", 2, 1), ("gl", 8, 1), ("gl", 2, 0), ("gx", 0, 1),
    ("gx", 3, 1), ("gl", 0, 0), ("gx", 8, 3), ("gc", 0, 2), ("gsh", 8, 0), ("gl", 3, 0), ("gbegin", 5), ("gc", 2, 2),
    ("gl", 1, 0), ("gl", 8, 2), ("gc", 1, 2), ("gc", 3, 2), ("gl", 8, 3), ("gsh", 8, 1), ("gx", 1, 2), ("gl", 1, 1),
    ("gx", 2, 2), ("gx", 3, 2), ("gx", 0, 2), ("gbegin", 4), ("gd", 8), ("vectors",), ("gx", 1, 3), ("gsh", 1, 0),
    ("gl", 0, 1), ("gl", 3, 1), ("gx", 0, 3), ("gsh", 0, 0), ("gl", 1, 2), ("gc", 5, 0), ("ln1",), ("gx", 5, 0),
    ("gl", 2, 1), ("gl", 1, 3), ("gsh", 1, 1), ("gc", 4, 0), ("gl", 0, 2), ("gx", 2, 3), ("gl", 0, 3), ("gsh", 0, 1),
    ("gc", 5, 1), ("gd", 1), ("gx", 3, 3), ("gsh", 3, 0), ("gx", 5, 1), ("gx", 4, 0), ("gsh", 2, 0), ("gc", 4, 1),
    ("gl", 2, 2), ("gl", 3, 2), ("gd", 0), ("p0",), ("gl", 5, 0), ("p1",), ("gc", 5, 2), ("p2",), ("at00",),
    ("gl", 2, 3), ("gx", 4, 1), ("at01",), ("gl", 4, 0), ("gc", 4, 2), ("at02",), ("gbegin", 7), ("at10",),
    ("gx", 5, 2), ("at11",), ("gl", 5, 1), ("gx", 5, 3), ("gl", 3, 3), ("gsh", 3, 1), ("gx", 4, 2), ("at12",),
    ("gsh", 2, 1), ("gl", 4, 1), ("gsh", 5, 0), ("gx", 4, 3), ("gbegin", 6), ("gsh", 4, 0), ("at20",), ("at21",),
    ("at22",), ("gl", 5, 2), ("gd", 3), ("at30",), ("gc", 7, 0), ("gl", 5, 3), ("gl", 4, 2), ("gc", 6, 0),
    ("gsh", 5, 1), ("gl", 4, 3), ("gsh", 4, 1), ("at31",), ("gx", 7, 0), ("gd", 2), ("at32",), ("norm2",), ("gd", 5),
    ("gc", 7, 1), ("gx", 7, 1), ("gx", 6, 0), ("gc", 6, 1), ("gd", 4), ("h0",), ("rc", 1), ("gl", 7, 0),
    ("gx", 6, 1), ("rc", 0), ("gl", 6, 0), ("gc", 7, 2), ("gx", 7, 2), ("gc", 6, 2), ("h1",), ("re", 1, 0),
    ("gl", 7, 1), ("rc", 2), ("re", 0, 0), ("gx", 7, 3), ("gx", 6, 2), ("rc", 3), ("gl", 6, 1), ("gsh", 7, 0),
    ("h2",), ("rc", 4), ("gx", 6, 3), ("re", 0, 1), ("re", 2, 0), ("re", 3, 0), ("gsh", 6, 0), ("gl", 6, 2),
    ("gl", 7, 2), ("rc", 5), ("h3",), ("gl", 7, 3), ("re", 4, 0), ("gsh", 7, 1), ("re", 5, 0), ("re", 0, 2),
    ("re", 3, 1), ("gd", 7), ("re", 1, 1), ("gl", 6, 3), ("re", 2, 1), ("gsh", 6, 1), ("re", 4, 1), ("re", 5, 1),
    ("gd", 6), ("last",), ("re", 1, 2), ("re", 3, 2), ("re", 2, 2), ("re", 4, 2), ("re", 5, 2),
)
BACKWARD_PLAN = (
    ("start",), ("hb0",), ("hb1",), ("core", 7), ("hb2",), ("core", 4), ("e", 7, 0), ("core", 6), ("hb3",), ("mp0",),
    ("core", 5), ("e", 6, 0), ("mp1",), ("og",), ("core", 3), ("e", 7, 1), ("core", 2), ("e", 4, 0), ("e", 5, 0),
    ("tc",), ("at00",), ("at01",), ("at02",), ("at10",), ("e", 3, 0), ("at11",), ("at12",), ("at20",), ("at21",),
    ("at22",), ("at30",), ("e", 2, 0), ("at31",), ("e", 6, 1), ("e", 4, 1), ("e", 5, 1), ("at32",), ("gq0",),
    ("e", 7, 2), ("e", 6, 2), ("core", 0), ("ch", 7, 0, 3), ("gq1",), ("ch", 6, 0, 3), ("core", 1), ("e", 3, 1),
    ("bias",), ("ch", 7, 1, 3), ("e", 0, 0), ("ch", 6, 1, 3), ("ch", 7, 0, 2), ("e", 2, 1), ("ip0",), ("e", 1, 0),
    ("ch", 7, 2, 3), ("e", 4, 2), ("ch", 4, 0, 3), ("ch", 6, 0, 2), ("e", 5, 2), ("ch", 7, 1, 2), ("ch", 7, 0, 1),
    ("ch", 5, 0, 3), ("e", 3, 2), ("ch", 4, 1, 3), ("ch", 3, 0, 3), ("ch", 4, 0, 2), ("ip1",), ("ch", 6, 2, 3),
    ("ch", 6, 1, 2), ("cut",), ("e", 2, 2), ("ch", 5, 1, 3), ("core", 8), ("ch", 2, 0, 3), ("ch", 3, 1, 3),
    ("ch", 2, 1, 3), ("e", 8, 0), ("e", 0, 1), ("ch", 4, 2, 3), ("ch", 3, 0, 2), ("ch", 5, 0, 2), ("ch", 5, 2, 3),
    ("e", 1, 1), ("ch", 5, 1, 2), ("ch", 5, 0, 1), ("ch", 4, 1, 2), ("ch", 4, 0, 1), ("ch", 6, 0, 1), ("e", 8, 1),
    ("ch", 3, 2, 3), ("e", 0, 2), ("ch", 0, 0, 3), ("ch", 2, 0, 2), ("ch", 2, 2, 3), ("ch", 3, 1, 2), ("res", 6, 0),
    ("res", 7, 0), ("ch", 0, 1, 3), ("e", 1, 2), ("ch", 1, 0, 3), ("ch", 1, 1, 3), ("ch", 3, 0, 1), ("e", 8, 2),
    ("ch", 8, 0, 3), ("ch", 8, 1, 3), ("ch", 2, 1, 2), ("res", 3, 0), ("ch", 8, 0, 2), ("ch", 0, 0, 2),
    ("ch", 0, 2, 3), ("ch", 1, 0, 2), ("ch", 0, 1, 2), ("ch", 1, 2, 3), ("ch", 1, 1, 2), ("ch", 1, 0, 1),
    ("res", 5, 0), ("ch", 8, 2, 3), ("ch", 8, 1, 2), ("ch", 8, 0, 1), ("ch", 2, 0, 1), ("res", 2, 0), ("res", 4, 0),
    ("ch", 0, 0, 1), ("res", 1, 0), ("res", 0, 0), ("res", 8, 0),
)
GATHER_IN = ("tokens", "cotangent", "mask", "counts", "w0", "w1", "w2", "w3", "w4")
KEPT = ("x", "g", "h1", "qkv", "probs", "context", "middle", "h2", "slope", "gd", "full0", "full1", "full2", "full3", "early")
FORWARD_SCRATCH = KEPT + (
    "full4", "first_sums", "pair_sums", "sum_send", "sum_recv", "pair", "act", "ub", "chain_sem", "send_sem", "recv_sem", "share_send", "share_recv",
    "keep_sem", "save_sem", "load_sem", "back_sem",
)


def forward_kernel(chain, parts, *refs):
    n_in = len(GATHER_IN)
    r = unpack(GATHER_IN, refs[:n_in])
    saved = unpack(KEPT, refs[n_in : n_in + len(KEPT)])
    packed, vec, target = refs[n_in + len(KEPT) : n_in + len(KEPT) + 3]
    s = unpack(FORWARD_SCRATCH, refs[n_in + len(KEPT) + 3 :])
    model = s.x.shape[1]
    slots, _, both = target.shape
    slot_rows = s.x.shape[0] // slots
    total = s.x.shape[0]
    patches = both // 2
    place = Place(chain)
    mine = place.shard()
    own = (r.w0, r.w1, r.w2, r.w3, r.w4)
    devices = 8 * chain
    share = model // devices
    hidden = s.act.shape[1]
    up_share = hidden // devices
    per_row = model // up_share
    samples = 2 * slots
    first_sample = (lax.axis_index("gx") * slots + lax.axis_index("gy")) * samples
    full = (s.full0, s.full1, s.full2, s.full3, s.full4)
    saves = []

    def save(name, where=Ellipsis):
        copy = pltpu.make_async_copy(
            getattr(s, name).at[where], getattr(saved, name).at[where], s.save_sem.at[len(saves)]
        )
        copy.start()
        saves.append(copy)

    loads = [
        pltpu.make_async_copy(
            r.tokens.at[pl.ds(half * slots, slots)],
            s.pair.at[:, pl.ds(half * patches, patches)],
            s.load_sem.at[half],
        )
        for half in range(2)
    ]
    grad_loads = [
        pltpu.make_async_copy(
            r.cotangent.at[half * slots + slot],
            s.act.at[pl.ds(half * patches, patches), pl.ds(slot * model, model)],
            s.load_sem.at[2 + half * slots + slot],
        )
        for half in range(2)
        for slot in range(slots)
    ]
    for copy in loads + grad_loads:
        copy.start()
    shape = (samples, patches)
    at_sample = lax.broadcasted_iota(jnp.int32, shape, 0)
    limit = jnp.zeros(shape, jnp.int32)
    offset = jnp.zeros(shape, jnp.int32)
    for sample in range(samples):
        limit = jnp.where(at_sample == sample, r.counts[first_sample + sample], limit)
        if sample >= slots:
            offset = jnp.where(at_sample == sample, r.counts[first_sample + sample - slots], offset)
    square = (patches, patches)
    upper = lax.broadcasted_iota(jnp.int32, square, 0) <= lax.broadcasted_iota(jnp.int32, square, 1)
    land = r.mask[...] == 1
    rank = dot(jnp.where(land, 1.0, 0.0).astype(jnp.bfloat16), jnp.where(upper, 1.0, 0.0).astype(jnp.bfloat16))
    rank = rank.astype(jnp.int32) - 1
    places = jnp.where(land & (rank < limit), rank + offset, -1)
    for slot in range(slots):
        target[slot] = jnp.concatenate([places[slot : slot + 1], places[slots + slot : slots + slot + 1]], axis=1)
    engine = Gather(
        place, parts, own, full, (s.chain_sem, s.send_sem, s.recv_sem, s.share_send, s.share_recv)
    )
    keeps = [pltpu.make_async_copy(own[at], full[at].at[mine], s.keep_sem.at[at]) for at in range(5)]
    for keep in keeps:
        keep.start()
    place.greet()

    def rows_of(slot):
        return pl.ds(slot * slot_rows, slot_rows)

    def pack_inputs():
        for copy in loads + keeps:
            copy.wait()
        for slot in range(slots):
            s.x[rows_of(slot), :] = dot(
                pick_matrix(target[slot], slot_rows), s.pair[slot]
            ).astype(jnp.bfloat16)
        save("x")

    def pack_grads():
        for copy in grad_loads:
            copy.wait()
        for slot in range(slots):
            patch_grads = s.act[pl.ds(0, both), pl.ds(slot * model, model)]
            s.g[rows_of(slot), :] = dot(
                pick_matrix(target[slot], slot_rows), patch_grads
            ).astype(jnp.bfloat16)
        save("g")

    def done(part):
        engine.finish(part)
        at, first, width, _ = parts[part]
        if at != VEC:
            save("full%d" % at, (Ellipsis, pl.ds(first, width)))

    def place_vector(at, carry):
        rows, up_rows = carry
        piece = s.full4[at // 8, at // 4 % 2, at // 2 % 2, at % 2].astype(jnp.float32)
        wide = jnp.concatenate([piece, jnp.zeros((16, model - 128), jnp.float32)], axis=1)
        rows = rows + pltpu.roll(wide[:8], at * share, 1)
        moved = pltpu.roll(wide[8:], (at % per_row) * up_share, 1)
        here = lax.broadcasted_iota(jnp.int32, (8, model), 0) == at // per_row
        up_rows = up_rows + jnp.where(here, jnp.broadcast_to(moved[:1], (8, model)), 0.0)
        return rows, up_rows

    up_turns = hidden // model

    def place_vectors():
        zeros = jnp.zeros((8, model), jnp.float32)
        rows, up_rows = lax.fori_loop(0, devices, place_vector, (zeros, zeros))
        vec[...] = rows
        for at in range(up_turns):
            s.ub[at] = up_rows[at : at + 1]

    def norm_one(slot, carry):
        at = rows_of(slot)
        n, _ = normalised(s.x[at, :].astype(jnp.float32))
        s.h1[at, :] = (n * vec[0:1] + vec[1:2]).astype(jnp.bfloat16)
        return carry

    def norm_ones():
        lax.fori_loop(0, slots, norm_one, 0)
        save("h1")

    def project(section):
        bias = vec[2:3] if section == 0 else vec[3:4]
        columns = pl.ds(section * model, model)
        weight = s.full0[:, :, :, :, :, columns].reshape(model, model)

        def chunk(at, carry):
            here = pl.ds(at * (total // 2), total // 2)
            value = dot(s.h1[here, :], weight)
            if section != 1:
                value = value + bias
            value = value.astype(jnp.bfloat16)
            if section == 0:
                value = value * jnp.bfloat16(HD**-0.5)
            s.qkv[section, here, :] = value
            return carry

        lax.fori_loop(0, 2, chunk, 0)
        save("qkv", section)

    low_lane = lax.broadcasted_iota(jnp.int32, (slot_rows, 2 * HD), 1) < HD
    none = jnp.zeros((slot_rows, 2 * HD), jnp.bfloat16)

    def attend(slot, turn):
        one = r.counts[first_sample + slot]
        two = one + r.counts[first_sample + slot + slots]
        shape = (slot_rows, slot_rows)
        at_row = lax.broadcasted_iota(jnp.int32, shape, 0)
        at_column = lax.broadcasted_iota(jnp.int32, shape, 1)
        same = ((at_row >= one).astype(jnp.int32) + (at_row >= two).astype(jnp.int32)) == (
            (at_column >= one).astype(jnp.int32) + (at_column >= two).astype(jnp.int32)
        )
        bias = jnp.where(same, 0.0, -1000000000.0)

        for inner in range(2):
            pair = turn * 2 + inner
            columns = pl.ds(pair * 2 * HD, 2 * HD)
            query = s.qkv[0, rows_of(slot), columns]
            key = s.qkv[1, rows_of(slot), columns]
            value = s.qkv[2, rows_of(slot), columns]
            context = None
            for head in range(2):
                mask = low_lane if head == 0 else ~low_lane
                scores = dot(jnp.where(mask, query, none), key, 1, 1) + bias
                expo = jnp.exp(scores - jnp.max(scores, axis=-1, keepdims=True))
                probs = (expo / jnp.sum(expo, axis=-1, keepdims=True)).astype(jnp.bfloat16)
                s.probs[slot * HEADS + pair * 2 + head] = probs
                term = dot(probs, jnp.where(mask, value, none))
                context = term if context is None else context + term
            s.context[rows_of(slot), columns] = context.astype(jnp.bfloat16)

    def norm_two(slot, carry):
        at = rows_of(slot)
        weight = s.full1[...].reshape(model, model)
        middle = s.x[at, :].astype(jnp.float32) + dot(s.context[at, :], weight) + vec[4:5]
        s.middle[at, :] = middle
        n, _ = normalised(middle)
        s.h2[at, :] = (n * vec[5:6] + vec[6:7]).astype(jnp.bfloat16)
        return carry

    def norm_twos():
        save("probs")
        save("context")
        lax.fori_loop(0, slots, norm_two, 0)
        save("middle")
        save("h2")

    down_rows = s.gd.shape[4]
    block_rows = chain // (hidden // model)
    early_parts = [
        part[:4] + (block * block_rows, block_rows)
        for block in range(hidden // model - 1)
        for part in parts
        if part[0] == DOWN
    ]
    adder = Scatter(
        place,
        early_parts,
        {DOWN: s.gd},
        {DOWN: None},
        {DOWN: (s.first_sums, s.pair_sums, s.early)},
        (s.sum_send, s.sum_recv, None, None),
    )

    def hidden_block(block):
        for half in range(PIECES):
            first_column = block * model + half * (model // PIECES)
            columns = pl.ds(first_column, model // PIECES)
            weight = s.full2[:, :, :, :, :, columns].reshape(model, model // PIECES)
            bias = s.ub[block][:, half * (model // PIECES) : (half + 1) * (model // PIECES)]

            def chunk(slot, carry, columns=columns, weight=weight, bias=bias):
                at = rows_of(slot)
                value = dot(s.h2[at, :], weight) + bias
                share_of = 0.5 + 0.5 * lax.erf(value * 0.7071067811865476)
                s.act[at, columns] = (value * share_of).astype(jnp.bfloat16)
                slope = share_of + value * jnp.exp(-0.5 * value * value) * 0.3989422804014327
                s.slope[at, columns] = slope.astype(jnp.bfloat16)
                return carry

            lax.fori_loop(0, slots, chunk, 0)
            grad = dot(s.act[:, columns], s.g[...], 0, 0).astype(jnp.bfloat16)
            for at in range(model // PIECES // down_rows):
                to = first_column // down_rows + at
                s.gd[to // 8, to // 4 % 2, to // 2 % 2, to % 2] = grad[at * down_rows : (at + 1) * down_rows]
        save("slope", (slice(None), pl.ds(block * model, model)))
        if block == up_turns - 1:
            save("gd", pl.ds(block * block_rows, block_rows))


    def last(slot, carry):
        at = rows_of(slot)
        weight = s.full3[...].reshape(hidden, model)
        value = s.middle[at, :] + dot(s.act[at, :], weight) + vec[7:8]
        s.pair[slot, pl.ds(0, slot_rows), :] = value.astype(jnp.bfloat16)
        return carry

    def lasts():
        lax.fori_loop(0, slots, last, 0)
        copy = pltpu.make_async_copy(s.pair.at[:, pl.ds(0, slot_rows)], packed, s.back_sem)
        copy.start()
        saves.append(copy)

    def early_core(part):
        adder.core(part).start()

    def early_up(part, level):
        adder.up_one(part, level)
        if level == 2:
            _, first, width, _, low, rows = early_parts[part]
            save("early", (pl.ds(low, rows), slice(None), pl.ds(first, width)))

    def share_out(part, half):
        engine.sharing(part, half).start()

    call = functools.partial
    steps = {"packx": pack_inputs, "packg": pack_grads, "vectors": place_vectors, "ln1": norm_ones}
    steps |= {"norm2": norm_twos, "last": lasts}
    for section in range(3):
        steps["p%d" % section] = call(project, section)
    for block in range(up_turns):
        steps["h%d" % block] = call(hidden_block, block)
    for slot in range(slots):
        for turn in range(HEADS // 4):
            steps["at%d%d" % (slot, turn)] = call(attend, slot, turn)
    moves = {"gbegin": engine.begin, "gc": engine.along, "gx": engine.across, "gl": engine.last}
    moves |= {"gsh": share_out, "gd": done, "rc": early_core, "re": early_up}
    follow(FORWARD_PLAN, steps, moves)
    for part in range(len(early_parts)):
        adder.finish_pairs(part)
    for copy in saves:
        copy.wait()


def any_spec():
    return pl.BlockSpec(memory_space=pl.ANY)


def vmem_spec():
    return pl.BlockSpec(memory_space=pltpu.VMEM)


def run_forward(chain, slots, tokens, cotangent, mask, counts, shards):
    devices = 8 * chain
    samples, patches, model = tokens.shape
    total = samples * patches * 3 // 4
    slot_rows = total // slots
    hidden = shards[UP].shape[1]
    parts = halves([item.shape[1] for item in shards])
    down = shards[DOWN].shape
    early_count = 2 * (hidden // model - 1)
    low = jnp.bfloat16
    kept = [
        ((total, model), low),
        ((total, model), low),
        ((total, model), low),
        ((3, total, model), low),
        ((slots * HEADS, slot_rows, slot_rows), low),
        ((total, model), low),
        ((total, model), jnp.float32),
        ((total, model), low),
        ((total, hidden), low),
        ((chain, 2, 2, 2) + down, low),
    ] + [((chain, 2, 2, 2) + item.shape, low) for item in shards[:4]]
    kept.append(((chain,) + down, low))
    outs = kept + [
        ((slots, slot_rows, model), low),
        ((8, model), jnp.float32),
        ((slots, 1, 2 * patches), jnp.int32),
    ]
    scratch = [pltpu.VMEM(*item) for item in kept] + [
        pltpu.VMEM((chain, 2, 2, 2) + shards[VEC].shape, low),
        pltpu.VMEM((chain, 2, 2) + down, low),
        pltpu.VMEM((chain, 2) + down, low),
        pltpu.SemaphoreType.DMA((early_count, 3)),
        pltpu.SemaphoreType.DMA((early_count, 3)),
        pltpu.VMEM((slots, 2 * patches, model), low),
        pltpu.VMEM((total, hidden), low),
        pltpu.VMEM((hidden // model, 1, model), jnp.float32),
        pltpu.SemaphoreType.DMA((len(parts), 2, chain)),
        pltpu.SemaphoreType.DMA((len(parts), 2)),
        pltpu.SemaphoreType.DMA((len(parts), devices)),
        pltpu.SemaphoreType.DMA((len(parts), 2)),
        pltpu.SemaphoreType.DMA((len(parts), 2)),
        pltpu.SemaphoreType.DMA((5,)),
        pltpu.SemaphoreType.DMA((len(KEPT) + 16,)),
        pltpu.SemaphoreType.DMA((2 + 2 * slots,)),
        pltpu.SemaphoreType.DMA,
    ]
    return pl.pallas_call(
        functools.partial(forward_kernel, chain, parts),
        out_shape=[jax.ShapeDtypeStruct(*item) for item in outs],
        in_specs=[any_spec(), any_spec(), vmem_spec(), pl.BlockSpec(memory_space=pltpu.SMEM)]
        + [any_spec()] * 4
        + [vmem_spec()],
        out_specs=[any_spec()] * (len(outs) - 2) + [vmem_spec()] * 2,
        scratch_shapes=scratch,
        compiler_params=pltpu.CompilerParams(
            collective_id=0, has_side_effects=True, vmem_limit_bytes=60 * 2**20
        ),
        name="forward",
    )(tokens, cotangent, mask, counts, *shards)


BACKWARD_IN = ("g", "slope", "w_down", "h2", "gd", "w_up", "middle", "context", "w_out", "qkv", "probs", "h1", "x", "w_qkv", "early", "vec")
BACKWARD_OUT = ("sum0", "sum1", "sum2", "sum3", "sum4", "packed")
BACKWARD_SCRATCH = (
    "g", "slope", "w_down", "h2", "gd", "w_up", "middle", "context", "w_out", "probs",
    "vg", "ug", "t0", "t1", "t2", "t4",
)
LOADS = ("g", "h2", "gd", "d0", "d1", "d2", "d3", "s0", "s1", "s2", "s3", "w_up", "middle", "context", "w_out", "probs", "w_qkv", "qkv0", "qkv1", "qkv2", "x", "h1", "early")


def backward_kernel(chain, parts, *refs):
    n_in, n_out, n_s = len(BACKWARD_IN), len(BACKWARD_OUT), len(BACKWARD_SCRATCH)
    r = unpack(BACKWARD_IN, refs[:n_in])
    o = unpack(BACKWARD_OUT, refs[n_in : n_in + n_out])
    at = n_in + n_out
    s = unpack(BACKWARD_SCRATCH, refs[at : at + n_s])
    buffers = refs[at + n_s : at + n_s + 20]
    load_sem, back_sem, *sems = refs[at + n_s + 20 :]
    got = [buffers[4 * k : 4 * k + 4] for k in range(5)]
    total, model = s.g.shape
    hidden = s.slope.shape[1]
    slots = lax.axis_size("gy")
    slot_rows = total // slots
    place = Place(chain)
    loads = {}

    def fetch(name, source, into):
        loads[name] = pltpu.make_async_copy(source, into, load_sem.at[LOADS.index(name)])
        loads[name].start()

    def need(*names):
        for name in names:
            loads[name].wait()

    done_rows = chain - s.gd.shape[0]
    fetch("g", r.g, s.g)
    for block in range(hidden // model):
        lanes = pl.ds(block * model, model)
        fetch("d%d" % block, r.w_down.at[lanes], s.w_down.at[lanes])
        fetch("s%d" % block, r.slope.at[:, lanes], s.slope.at[:, lanes])
        if block == 0:
            fetch("h2", r.h2, s.h2)
            fetch("gd", r.gd.at[pl.ds(done_rows, chain - done_rows), :, :, place.d], s.gd)
    for name in ("w_up", "middle", "context", "w_out", "probs"):
        fetch(name, getattr(r, name), getattr(s, name))
    fetch("early", r.early.at[pl.ds(0, done_rows)], got[DOWN][2].at[pl.ds(0, done_rows)])
    place.greet()
    engine = Scatter(
        place, parts, (s.t0, s.t1, s.t2, r.gd, s.t4), (None, None, None, s.gd, None), got, sems
    )
    groups = [[k for k, part in enumerate(parts) if part[0] == name] for name in range(5)]
    outs = (o.sum0, o.sum1, o.sum2, o.sum3, o.sum4)

    def rows_of(slot):
        return pl.ds(slot * slot_rows, slot_rows)

    def shards_of(value, like):
        return value.reshape(like.shape[:5] + (value.shape[-1],)).astype(jnp.bfloat16)

    def first_sums():
        need("g", "h2")
        s.vg[...] = jnp.zeros_like(s.vg)
        s.ug[...] = jnp.zeros_like(s.ug)
        s.vg[7:8] = column_sum(s.g[...].astype(jnp.float32))

    def hidden_block(block):
        need("d%d" % block, "s%d" % block)
        for half in range(PIECES):
            first_column = block * model + half * (model // PIECES)
            columns = pl.ds(first_column, model // PIECES)
            weight = s.w_down[pl.ds(first_column, model // PIECES), :]

            def chunk(slot, carry, columns=columns, weight=weight):
                here = rows_of(slot)
                value = dot(s.g[here, :], weight, 1, 1) * s.slope[here, columns].astype(jnp.float32)
                value = value.astype(jnp.bfloat16)
                s.slope[here, columns] = value
                return carry + column_sum(value.astype(jnp.float32))

            sums = lax.fori_loop(0, slots, chunk, jnp.zeros((1, model // PIECES), jnp.float32))
            s.ug[block : block + 1, half * (model // PIECES) : (half + 1) * (model // PIECES)] = sums
            s.t2[:, :, :, :, :, columns] = shards_of(dot(s.h2[...], s.slope[:, columns], 0, 0), s.t2)

    def fetch_more():
        for section in range(3):
            fetch("qkv%d" % section, r.qkv.at[section], s.w_down.at[pl.ds(section * model, model)])
        fetch("x", r.x, s.w_down.at[pl.ds(3 * model, model)])
        need("w_up", "middle")

    half_rows = total // 2

    def middle_part(half):
        if half == 0:
            fetch_more()
        grad = dot(s.slope[pl.ds(half * half_rows, half_rows), :], s.w_up[...], 1, 1)
        for inner in range(slots // 2):
            here = rows_of(half * (slots // 2) + inner)
            part = grad[inner * slot_rows : (inner + 1) * slot_rows]
            n, rate = normalised(s.middle[here, :])
            s.vg[5:6] += column_sum(part * n)
            s.vg[6:7] += column_sum(part)
            scaled = part * r.vec[5:6]
            mean_one = jnp.mean(scaled, axis=-1, keepdims=True)
            mean_two = jnp.mean(scaled * n, axis=-1, keepdims=True)
            full_grad = s.g[here, :].astype(jnp.float32) + rate * (scaled - mean_one - n * mean_two)
            s.middle[here, :] = full_grad
            branch = full_grad.astype(jnp.bfloat16)
            s.h2[here, :] = branch
            s.vg[4:5] += column_sum(branch.astype(jnp.float32))

    joined = pl.ds(0, 3 * model)

    def out_grads():
        fetch("w_qkv", r.w_qkv, s.w_up.at[:, joined])
        fetch("h1", r.h1, s.slope.at[:, pl.ds(3 * model, model)])
        need("context", "w_out")
        s.t1[...] = shards_of(dot(s.context[...], s.h2[...], 0, 0), s.t1)

    def to_context(slot, carry):
        here = rows_of(slot)
        s.context[here, :] = dot(s.h2[here, :], s.w_out[...], 1, 1).astype(jnp.bfloat16)
        return carry

    def to_contexts():
        lax.fori_loop(0, slots, to_context, 0)
        need("qkv0", "qkv1", "qkv2", "probs")

    low_lane = lax.broadcasted_iota(jnp.int32, (slot_rows, 2 * HD), 1) < HD
    none = jnp.zeros((slot_rows, 2 * HD), jnp.bfloat16)

    def attend(slot, turn):
        for inner in range(2):
            pair = turn * 2 + inner
            first_column = pair * 2 * HD
            columns = pl.ds(first_column, 2 * HD)
            query = s.w_down[pl.ds(slot * slot_rows, slot_rows), columns]
            key = s.w_down[pl.ds(model + slot * slot_rows, slot_rows), columns]
            value = s.w_down[pl.ds(2 * model + slot * slot_rows, slot_rows), columns]
            grad = s.context[rows_of(slot), columns]
            totals = [None, None, None]
            for head in range(2):
                mask = low_lane if head == 0 else ~low_lane
                grad_here = jnp.where(mask, grad, none)
                low_probs = s.probs[slot * HEADS + pair * 2 + head]
                probs = low_probs.astype(jnp.float32)
                weighted = probs * dot(grad_here, value, 1, 1)
                share = jnp.sum(weighted, axis=-1, keepdims=True)
                scores = (weighted - probs * share).astype(jnp.bfloat16)
                terms = (
                    dot(scores, jnp.where(mask, key, none)),
                    dot(scores, jnp.where(mask, query, none), 0, 0),
                    dot(low_probs, grad_here, 0, 0),
                )
                totals = [b if a is None else a + b for a, b in zip(totals, terms)]
            totals[0] = totals[0] * HD**-0.5
            for section in range(3):
                s.slope[rows_of(slot), pl.ds(section * model + first_column, 2 * HD)] = totals[
                    section
                ].astype(jnp.bfloat16)

    h1 = pl.ds(3 * model, model)
    half_width = 3 * model // 2

    def qkv_grads(half):
        if half == 0:
            need("h1", "w_qkv", "x")
        for third in range(3):
            columns = pl.ds(half * half_width + third * (half_width // 3), half_width // 3)
            s.t0[:, :, :, :, :, columns] = shards_of(dot(s.slope[:, h1], s.slope[:, columns], 0, 0), s.t0)

    def bias_sums():
        s.vg[2:3] = column_sum(s.slope[:, pl.ds(0, model)].astype(jnp.float32))
        s.vg[3:4] = column_sum(s.slope[:, pl.ds(2 * model, model)].astype(jnp.float32))

    def input_part(half):
        grad = dot(s.slope[pl.ds(half * half_rows, half_rows), joined], s.w_up[:, joined], 1, 1)
        for inner in range(slots // 2):
            slot = half * (slots // 2) + inner
            here = rows_of(slot)
            part = grad[inner * slot_rows : (inner + 1) * slot_rows]
            n, rate = normalised(
                s.w_down[pl.ds(3 * model + slot * slot_rows, slot_rows), :].astype(jnp.float32)
            )
            s.vg[0:1] += column_sum(part * n)
            s.vg[1:2] += column_sum(part)
            scaled = part * r.vec[0:1]
            mean_one = jnp.mean(scaled, axis=-1, keepdims=True)
            mean_two = jnp.mean(scaled * n, axis=-1, keepdims=True)
            full_grad = s.middle[here, :] + rate * (scaled - mean_one - n * mean_two)
            s.g[here, :] = full_grad.astype(jnp.bfloat16)
        here = pl.ds(half * half_rows, half_rows)
        backs.append(pltpu.make_async_copy(s.g.at[here], o.packed.at[here], back_sem.at[half]))
        backs[-1].start()

    backs = []
    devices = 8 * chain
    share = model // devices
    up_share = hidden // devices
    per_row = model // up_share

    def cut_vector(index, carry):
        rows = pltpu.roll(s.vg[...], model - index * share, 1)[:, :128]
        here = lax.broadcasted_iota(jnp.int32, (8, model), 0) == index // per_row
        row = jnp.broadcast_to(column_sum(jnp.where(here, s.ug[...], 0.0)), (8, model))
        up_rows = pltpu.roll(row, model - (index % per_row) * up_share, 1)[:, :128]
        s.t4[index // 8, index // 4 % 2, index // 2 % 2, index % 2] = jnp.concatenate([rows, up_rows], axis=0)
        return carry

    def cut_vectors():
        lax.fori_loop(0, devices, cut_vector, 0)

    def core(part):
        engine.core(part).start()

    unread = (["gd"], ["early"])

    def add_up(part, level):
        if part in groups[DOWN] and unread[0]:
            need(unread[0].pop())
        engine.up_one(part, level)

    def chain_one(part, near, row):
        if part in groups[DOWN] and unread[1]:
            need(unread[1].pop())
        if chain == 4:
            engine.chain_one(part, near, row)
        elif (near, row) == (0, 1):
            engine.chain_all([part])

    def result(part, _):
        engine.result(part, outs)

    call = functools.partial
    steps = {"start": first_sums, "og": out_grads, "tc": to_contexts, "bias": bias_sums, "cut": cut_vectors}
    for half in range(2):
        steps["mp%d" % half] = call(middle_part, half)
        steps["gq%d" % half] = call(qkv_grads, half)
        steps["ip%d" % half] = call(input_part, half)
    for block in range(hidden // model):
        steps["hb%d" % block] = call(hidden_block, block)
    for slot in range(slots):
        for turn in range(HEADS // 4):
            steps["at%d%d" % (slot, turn)] = call(attend, slot, turn)
    moves = {"core": core, "e": add_up, "ch": chain_one, "res": result}
    follow(BACKWARD_PLAN, steps, moves)
    for part in range(len(parts)):
        engine.finish(part)
    for copy in backs:
        copy.wait()


def run_backward(chain, kept, vec, shards):
    total, model = kept.x.shape
    hidden = shards[UP].shape[1]
    last_rows = chain // (hidden // model)
    parts = [
        part + ((chain - last_rows, last_rows) if part[0] == DOWN else (0, chain))
        for part in halves([item.shape[1] for item in shards])
    ]
    low, wide = jnp.bfloat16, jnp.float32
    lead = (chain, 2, 2, 2)
    fulls = [
        item.reshape(-1, item.shape[-1]) for item in (kept.full0, kept.full1, kept.full2, kept.full3)
    ]
    given = types.SimpleNamespace(
        g=kept.g, slope=kept.slope, w_down=fulls[DOWN], h2=kept.h2,
        gd=kept.gd, w_up=fulls[UP], middle=kept.middle,
        context=kept.context, w_out=fulls[OUT], qkv=kept.qkv, probs=kept.probs, h1=kept.h1, x=kept.x,
        w_qkv=fulls[QKV], early=kept.early, vec=vec,
    )
    scratch = {name: pltpu.VMEM(getattr(given, name).shape, getattr(given, name).dtype) for name in BACKWARD_IN}
    scratch["gd"] = pltpu.VMEM((last_rows, 2, 2) + shards[DOWN].shape, low)
    scratch["vg"] = pltpu.VMEM((8, model), wide)
    scratch["ug"] = pltpu.VMEM((8, model), wide)
    for at in (QKV, OUT, UP, VEC):
        scratch["t%d" % at] = pltpu.VMEM(lead + shards[at].shape, wide if at == VEC else low)
    arrivals = []
    for at, item in enumerate(shards):
        for front in ((chain, 2, 2), (chain, 2), (chain,), (chain + 1,)):
            arrivals.append(pltpu.VMEM(front + item.shape, wide if at == VEC else low))
    outs = [(item.shape, wide) for item in shards] + [((total, model), low)]
    return pl.pallas_call(
        functools.partial(backward_kernel, chain, parts),
        out_shape=[jax.ShapeDtypeStruct(*item) for item in outs],
        in_specs=[any_spec()] * (len(BACKWARD_IN) - 1) + [vmem_spec()],
        out_specs=[vmem_spec()] * 5 + [any_spec()],
        scratch_shapes=[scratch[name] for name in BACKWARD_SCRATCH]
        + arrivals
        + [
            pltpu.SemaphoreType.DMA((len(LOADS),)),
            pltpu.SemaphoreType.DMA((2,)),
            pltpu.SemaphoreType.DMA((len(parts), 3)),
            pltpu.SemaphoreType.DMA((len(parts), 3)),
            pltpu.SemaphoreType.DMA((len(parts), chain)),
            pltpu.SemaphoreType.DMA((len(parts), 2, chain)),
        ],
        compiler_params=pltpu.CompilerParams(
            collective_id=1, has_side_effects=True, vmem_limit_bytes=63 * 2**20
        ),
        name="backward",
    )(*[getattr(given, name) for name in BACKWARD_IN])


def spread_kernel(target, rows, grads, *refs):
    sums, out_tokens, grad_tokens, outs = refs[:5], refs[5], refs[6], refs[7:]
    slot_rows = rows.shape[1]
    patches = out_tokens.shape[2]
    matrix = pick_matrix(target[0], slot_rows)
    for source, to in ((rows, out_tokens), (grads, grad_tokens)):
        spread = dot(matrix, source[0], 0, 0).astype(jnp.bfloat16)
        for half in range(2):
            to[half, 0] = spread[half * patches : (half + 1) * patches]

    @pl.when(pl.program_id(0) == 0)
    def _():
        for at in range(4):
            outs[at][...] = sums[at][...]
        table = sums[VEC]
        share = outs[4].shape[1]
        outs[6][...] = table[2:4, :share]
        for ref, row in zip((outs[4], outs[5]) + outs[7:], (0, 1, 4, 5, 6, 7, 8)):
            ref[...] = table[row : row + 1, : ref.shape[1]]


def run_spread(target, rows, grads, sums, share, up_share):
    slots, slot_rows, model = rows.shape
    patches = target.shape[2] // 2
    wide = jnp.float32

    def whole(shape):
        return pl.BlockSpec(shape, lambda i: (0,) * len(shape))

    tokens_spec = pl.BlockSpec((2, 1, patches, model), lambda i: (0, i, 0, 0))
    slot_spec = pl.BlockSpec((1, slot_rows, model), lambda i: (i, 0, 0))
    shapes = [item.shape for item in sums[:4]]
    shapes += [(1, share), (1, share), (2, share)] + [(1, share)] * 4 + [(1, up_share)]
    tokens_shape = jax.ShapeDtypeStruct((2, slots, patches, model), jnp.bfloat16)
    return pl.pallas_call(
        spread_kernel,
        grid=(slots,),
        out_shape=[tokens_shape] * 2 + [jax.ShapeDtypeStruct(shape, wide) for shape in shapes],
        in_specs=[pl.BlockSpec((1, 1, 2 * patches), lambda i: (i, 0, 0)), slot_spec, slot_spec]
        + [whole(item.shape) for item in sums],
        out_specs=[tokens_spec] * 2 + [whole(shape) for shape in shapes],
        compiler_params=pltpu.CompilerParams(vmem_limit_bytes=60 * 2**20),
        name="spread",
    )(target, rows, grads, *sums)


def per_device(
    tokens,
    land_mask,
    counts,
    ln1_gain,
    ln1_shift,
    qkv_weight,
    qv_bias,
    out_weight,
    out_bias,
    ln2_gain,
    ln2_shift,
    up_weight,
    up_bias,
    down_weight,
    down_bias,
    cotangent,
):
    chain = lax.axis_size("gx") // 2
    slots = lax.axis_size("gy")
    share, up_share = ln1_gain.shape[0], up_bias.shape[0]
    small = [ln1_gain, ln1_shift, qv_bias[0], qv_bias[1], out_bias, ln2_gain, ln2_shift, down_bias, up_bias]
    table = sum(
        jnp.pad(item[None], ((at, 15 - at), (0, 128 - item.shape[0]))) for at, item in enumerate(small)
    )
    shards = [qkv_weight, out_weight, up_weight, down_weight, table]
    *kept, packed, vec, target = run_forward(
        chain, slots, tokens, cotangent, land_mask, counts, shards
    )
    *sums, packed_grads = run_backward(chain, unpack(KEPT, kept), vec, shards)
    out_tokens, grad_tokens, *finals = run_spread(
        target, packed, packed_grads.reshape(packed.shape), sums, share, up_share
    )
    sum_qkv, sum_out, sum_up, sum_down, gain_one, shift_one, pair_bias = finals[:7]
    bias_out, gain_two, shift_two, bias_down, bias_up = finals[7:]
    return (
        out_tokens.reshape(tokens.shape),
        grad_tokens.reshape(tokens.shape),
        gain_one[0],
        shift_one[0],
        sum_qkv,
        pair_bias,
        sum_out,
        bias_out[0],
        gain_two[0],
        shift_two[0],
        sum_up,
        bias_up[0],
        sum_down,
        bias_down[0],
    )


def solution(mesh):
    placed = (
        P(("gx", "gy"), None, None),
        P(("gx", "gy"), None),
        P(),
        P(("gx", "gy")),
        P(("gx", "gy")),
        P(("gx", "gy"), None),
        P(None, ("gx", "gy")),
        P(("gx", "gy"), None),
        P(("gx", "gy")),
        P(("gx", "gy")),
        P(("gx", "gy")),
        P(("gx", "gy"), None),
        P(("gx", "gy")),
        P(("gx", "gy"), None),
        P(("gx", "gy")),
        P(("gx", "gy"), None, None),
    )
    return jax.shard_map(
        per_device,
        mesh=mesh,
        in_specs=placed,
        out_specs=(
            P(("gx", "gy"), None, None),
            P(("gx", "gy"), None, None),
            P(("gx", "gy")),
            P(("gx", "gy")),
            P(("gx", "gy"), None),
            P(None, ("gx", "gy")),
            P(("gx", "gy"), None),
            P(("gx", "gy")),
            P(("gx", "gy")),
            P(("gx", "gy")),
            P(("gx", "gy"), None),
            P(("gx", "gy")),
            P(("gx", "gy"), None),
            P(("gx", "gy")),
        ),
        check_vma=False,
    )
```

```python
import functools
import types

import jax
import jax.numpy as jnp
from jax import lax
from jax.experimental import pallas as pl
from jax.experimental.pallas import tpu as pltpu
from jax.sharding import PartitionSpec as P

HEADS = 12
HD = 64
MESH = pl.DeviceIdType.MESH


class Place:
    def __init__(self, chain):
        gx = lax.axis_index("gx")
        gy = lax.axis_index("gy")
        self.chain = chain
        self.a = gx // 2
        self.b = gx % 2
        self.c = gy // 2
        self.d = gy % 2

    def shard(self, a=None, b=None, c=None, d=None):
        a = self.a if a is None else a
        b = self.b if b is None else b
        c = self.c if c is None else c
        d = self.d if d is None else d
        return a, b, c, d

    def device(self, a=None, b=None, c=None, d=None):
        a = self.a if a is None else a
        b = self.b if b is None else b
        c = self.c if c is None else c
        d = self.d if d is None else d
        return (a * 2 + b, c * 2 + d)

    def greet(self, far=False):
        barrier = pltpu.get_barrier_semaphore()
        for to in (
            self.device(d=1 - self.d),
            self.device(c=1 - self.c),
            self.device(b=1 - self.b),
        ):
            pl.semaphore_signal(barrier, inc=1, device_id=to, device_id_type=MESH)

        def greet_row(row, carry):
            near = (row == self.a - 1) | (row == self.a + 1)

            @pl.when((row != self.a) if far else near)
            def _():
                pl.semaphore_signal(barrier, inc=1, device_id=self.device(a=row), device_id_type=MESH)

            return carry

        lax.fori_loop(0, self.chain, greet_row, 0)
        ends = (self.a > 0).astype(jnp.int32) + (self.a < self.chain - 1).astype(jnp.int32)
        pl.semaphore_wait(barrier, 3 + (self.chain - 1 if far else ends))


def halves(widths):
    parts = []
    for at, width in enumerate(widths):
        if width % 256:
            parts.append((at, 0, width, "b"))
        else:
            parts.append((at, 0, width // 2, "b"))
            parts.append((at, width // 2, width // 2, "c"))
    return parts


def gather_parts(widths):
    parts = []
    for at, width in enumerate(widths):
        third = width // 4 if at == UP else width // 3
        pair = (width - third) // 2
        if at in (UP, DOWN) and third % 128 == 0 and pair % 128 == 0:
            parts += [(at, 0, pair, "b"), (at, pair, pair, "c"), (at, 2 * pair, third, "z")]
        else:
            parts += [(at,) + part[1:] for part in halves([width])]
    return parts


class Gather:
    def __init__(self, place, parts, own, full, sems):
        self.place, self.parts, self.own, self.full = place, parts, own, full
        self.chain_sem, self.send_sem, self.recv_sem, self.share_send, self.share_recv = sems

    def view(self, part, index):
        at, first, width, _ = self.parts[part]
        return self.full[at].at[tuple(index) + (slice(None), pl.ds(first, width))]

    def copy(self, part, index, to, send, own=False):
        at, first, width, _ = self.parts[part]
        a, b, c, d = index
        return pltpu.make_async_remote_copy(
            src_ref=self.own[at].at[:, pl.ds(first, width)] if own else self.view(part, index),
            dst_ref=self.view(part, index),
            send_sem=send,
            recv_sem=self.recv_sem.at[part, ((a * 2 + b) * 2 + c) * 2 + d],
            device_id=to,
            device_id_type=MESH,
        )

    def flip(self, axis):
        return {axis: 1 - (self.place.b if axis == "b" else self.place.c)}

    def links(self, part):
        first = self.parts[part][3]
        return ("c", "b") if first == "c" else ("b", "c")

    def send_pair(self, part, index, level, own=False):
        to = self.place.device(**self.flip(self.links(part)[level]))
        self.copy(part, index, to, self.send_sem.at[part, level], own).start()

    def arrived(self, part, index):
        self.copy(part, index, self.place.device(d=1 - self.place.d), self.send_sem.at[part, 0]).wait_recv()

    def send_chain(self, part, way, index, step, own=False):
        place = self.place
        to = place.device(a=place.a + 1) if way == 0 else place.device(a=place.a - 1)
        column = index[1] * 2 + index[2]
        return self.copy(part, index, to, self.chain_sem.at[part, way, step, column], own)

    def send_ends(self, part, index, step, own=False):
        place = self.place
        pl.when(place.a < place.chain - 1)(lambda: self.send_chain(part, 0, index, step, own).start())
        pl.when(place.a > 0)(lambda: self.send_chain(part, 1, index, step, own).start())

    def cross_first(self, part):
        index = self.place.shard(b=1 - self.place.b)
        self.arrived(part, index)
        self.send_pair(part, index, 1)
        self.send_ends(part, index, 0)

    def cross_second(self, part):
        place = self.place
        for b in (place.b, 1 - place.b):
            index = place.shard(b=b, c=1 - place.c)
            self.arrived(part, index)
            self.send_ends(part, index, 0)

    def along_last(self, part, third):
        place = self.place
        steps = place.chain - 1

        def one(step, carry):
            for b in (place.b, 1 - place.b):
                for c in (place.c, 1 - place.c):

                    @pl.when(place.a - 1 - step >= 0)
                    def _(b=b, c=c):
                        index = place.shard(a=place.a - 1 - step, b=b, c=c)
                        self.arrived(part, index)
                        pl.when(place.a < steps)(lambda: self.send_chain(part, 0, index, step + 1).start())

                    @pl.when(place.a + 1 + step <= steps)
                    def _(b=b, c=c):
                        index = place.shard(a=place.a + 1 + step, b=b, c=c)
                        self.arrived(part, index)
                        pl.when(place.a > 0)(lambda: self.send_chain(part, 1, index, step + 1).start())

            return carry

        self.each(third * steps // 3, (third + 1) * steps // 3, one)

    def begin(self, part):
        place = self.place
        mine = place.shard()
        self.send_ends(part, mine, 0, True)
        for level in range(2):
            self.send_pair(part, mine, level, True)

    def each(self, low, high, one):
        if isinstance(low, int) and high - low == 1:
            one(low, 0)
        else:
            lax.fori_loop(low, high, one, 0)

    def along(self, part, third):
        place = self.place
        steps = place.chain - 1

        def one(step, carry):
            @pl.when(place.a - 1 - step >= 0)
            def _():
                index = place.shard(a=place.a - 1 - step)
                self.arrived(part, index)
                pl.when(place.a < steps)(lambda: self.send_chain(part, 0, index, step + 1).start())
                for level in range(2):
                    self.send_pair(part, index, level)

            @pl.when(place.a + 1 + step <= steps)
            def _():
                index = place.shard(a=place.a + 1 + step)
                self.arrived(part, index)
                pl.when(place.a > 0)(lambda: self.send_chain(part, 1, index, step + 1).start())
                for level in range(2):
                    self.send_pair(part, index, level)

            return carry

        self.each(third * steps // 3, (third + 1) * steps // 3, one)

    def at_distance(self, turn, one):
        place = self.place
        steps = place.chain - 1
        if turn == 0:
            one(place.a)
            return

        def both(step, carry):
            pl.when(place.a - step >= 0)(lambda: one(place.a - step))
            pl.when(place.a + step <= steps)(lambda: one(place.a + step))
            return carry

        self.each(1 + (turn - 1) * steps // 3, 1 + turn * steps // 3, both)

    def across(self, part, turn):
        first, _ = self.links(part)

        def one(row):
            index = self.place.shard(a=row, **self.flip(first))
            self.arrived(part, index)
            self.send_pair(part, index, 1)

        self.at_distance(turn, one)

    def last(self, part, turn):
        first, second = self.links(part)

        def one(row):
            self.arrived(part, self.place.shard(a=row, **self.flip(second)))
            self.arrived(part, self.place.shard(a=row, **self.flip(second), **self.flip(first)))

        self.at_distance(turn, one)

    def sharing(self, part, half):
        place = self.place
        every = slice(None)
        if self.links(part)[1] == "c":
            box = (every, every, 1 - place.c if half else place.c, place.d)
        else:
            box = (every, 1 - place.b if half else place.b, every, place.d)
        return pltpu.make_async_remote_copy(
            src_ref=self.view(part, box),
            dst_ref=self.view(part, box),
            send_sem=self.share_send.at[part, half],
            recv_sem=self.share_recv.at[part, half],
            device_id=place.device(d=1 - place.d),
            device_id_type=MESH,
        )

    def finish(self, part):
        place = self.place
        steps = place.chain - 1
        for half in range(2):
            self.sharing(part, half).wait()
        every = slice(None)
        chain_last = self.parts[part][3] == "z"
        boxes = ((pl.ds(0, 1), 0, 0, 0), (0, every, 0, 0)) if chain_last else ((every, 0, 0, 0), (every, every, 0, 0))
        for level, box in enumerate(boxes):
            block = self.view(part, box)
            pltpu.make_async_copy(block, block, self.send_sem.at[part, level]).wait()
        columns = [(place.b, place.c)]
        if chain_last:
            columns = [(b, c) for b in range(2) for c in range(2)]

        def sent(step, carry):
            for b, c in columns:

                @pl.when((place.a < steps) & (place.a - step >= 0))
                def _(b=b, c=c):
                    self.send_chain(part, 0, place.shard(a=place.a - step, b=b, c=c), step).wait_send()

                @pl.when((place.a > 0) & (place.a + step <= steps))
                def _(b=b, c=c):
                    self.send_chain(part, 1, place.shard(a=place.a + step, b=b, c=c), step).wait_send()

            return carry

        lax.fori_loop(0, steps, sent, 0)


def scatter_parts(widths):
    parts = []
    for at, width in enumerate(widths):
        if at == QKV:
            half, more = width // 2, -(-width // 512) * 128
            parts += [(at, 0, more, "b"), (at, half, more, "c")]
            parts += [(at, more, half - more, "b"), (at, half + more, half - more, "c")]
        else:
            parts += [(at,) + part[1:] for part in halves([width])]
    return parts


class Scatter:
    def __init__(self, place, parts, terms, kept, got, sems):
        self.place, self.parts, self.terms = place, parts, terms
        self.kept = kept
        self.got = got
        self.send_sem, self.recv_sem, self.chain_send, self.chain_recv = sems

    def rows(self, part):
        return pl.ds(*self.parts[part][4:])

    def pick(self, ref, lead, part):
        first, width = self.parts[part][1:3]
        return ref.at[lead + (slice(None), pl.ds(first, width))]

    def exchange(self, part, level, src, dst, to):
        return pltpu.make_async_remote_copy(
            src_ref=src,
            dst_ref=dst,
            send_sem=self.send_sem.at[part, level],
            recv_sem=self.recv_sem.at[part, level],
            device_id=to,
            device_id_type=MESH,
        )

    def core(self, part):
        place = self.place
        at = self.parts[part][0]
        every = slice(None)
        return self.exchange(
            part,
            0,
            self.pick(self.terms[at], (self.rows(part), every, every, 1 - place.d), part),
            self.pick(self.got[at][0], (self.rows(part), every, every), part),
            place.device(d=1 - place.d),
        )

    def lead(self, part, level, mine):
        place = self.place
        every = slice(None)
        first = self.parts[part][3]
        b = place.b if mine else 1 - place.b
        c = place.c if mine else 1 - place.c
        rows = self.rows(part)
        if level == 1:
            return (rows, b, every) if first == "b" else (rows, every, c)
        return (rows, c) if first == "b" else (rows, b)

    def pair(self, part, level):
        place = self.place
        at, first = self.parts[part][0], self.parts[part][3]
        axis = first if level == 1 else ("c" if first == "b" else "b")
        to = place.device(b=1 - place.b) if axis == "b" else place.device(c=1 - place.c)
        every = slice(None)
        dst = (self.rows(part), every) if level == 1 else (self.rows(part),)
        return self.exchange(
            part,
            level,
            self.pick(self.got[at][level - 1], self.lead(part, level, False), part),
            self.pick(self.got[at][level], dst, part),
            to,
        )

    def add_core(self, part):
        place = self.place
        at, first, width, _, low, rows = self.parts[part]
        self.core(part).wait_recv()
        terms, kept, got = self.terms[at], self.kept[at], self.got[at][0]
        columns = pl.ds(first, width)

        def one(i, carry):
            x, y, z = low + i // 4, i // 2 % 2, i % 2
            term = terms[x, y, z, place.d, :, columns] if kept is None else kept[x - low, y, z, :, columns]
            got[x, y, z, :, columns] = got[x, y, z, :, columns] + term
            return carry

        lax.fori_loop(0, 4 * rows, one, 0)

    def add_pair(self, part, level):
        place = self.place
        at, first, width, axis, low, rows = self.parts[part]
        self.pair(part, level).wait_recv()
        before, got = self.got[at][level - 1], self.got[at][level]
        columns = pl.ds(first, width)

        def one(i, carry):
            if level == 1:
                x, y = low + i // 2, i % 2
                if axis == "b":
                    kept = before[x, place.b, y, :, columns]
                else:
                    kept = before[x, y, place.c, :, columns]
                got[x, y, :, columns] = got[x, y, :, columns] + kept
            else:
                x = low + i
                kept = before[x, place.c if axis == "b" else place.b, :, columns]
                got[x, :, columns] = got[x, :, columns] + kept
            return carry

        lax.fori_loop(0, (2 if level == 1 else 1) * rows, one, 0)

    def toward(self, part, row):
        place = self.place
        at = self.parts[part][0]
        return pltpu.make_async_remote_copy(
            src_ref=self.pick(self.got[at][2], (row,), part),
            dst_ref=self.pick(self.got[at][3], (place.a,), part),
            send_sem=self.chain_send.at[part, row],
            recv_sem=self.chain_recv.at[part, place.a],
            device_id=place.device(a=row),
            device_id_type=MESH,
        )

    def along(self, part):
        place = self.place

        def one(back, carry):
            far = place.chain - 1 - back
            pl.when(place.a + far < place.chain)(lambda: self.toward(part, place.a + far).start())
            pl.when(place.a - far >= 0)(lambda: self.toward(part, place.a - far).start())
            return carry

        lax.fori_loop(0, place.chain - 1, one, 0)

    def result(self, part, out):
        place = self.place
        at, first, width = self.parts[part][:3]
        columns = pl.ds(first, width)
        got = self.got[at]
        out[at][:, columns] = got[2][place.a, :, columns].astype(jnp.float32)

        def one(row, carry):
            @pl.when(row != place.a)
            def _():
                pltpu.make_async_remote_copy(
                    src_ref=self.pick(got[3], (row,), part),
                    dst_ref=self.pick(got[3], (row,), part),
                    send_sem=self.chain_send.at[part, row],
                    recv_sem=self.chain_recv.at[part, row],
                    device_id=place.device(a=row),
                    device_id_type=MESH,
                ).wait_recv()
                out[at][:, columns] = out[at][:, columns] + got[3][row, :, columns].astype(jnp.float32)

            return carry

        lax.fori_loop(0, place.chain, one, 0)

    def finish_pairs(self, part):
        self.core(part).wait_send()
        for level in (1, 2):
            self.pair(part, level).wait_send()

    def finish(self, part):
        place = self.place
        self.finish_pairs(part)

        def one(row, carry):
            pl.when(row != place.a)(lambda: self.toward(part, row).wait_send())
            return carry

        lax.fori_loop(0, place.chain, one, 0)

    def up_one(self, part, level):
        if level == 0:
            self.add_core(part)
        else:
            self.add_pair(part, level)
        if level < 2:
            self.pair(part, level + 1).start()


def normalised(values):
    center = values - jnp.mean(values, axis=-1, keepdims=True)
    spread = jnp.mean(center * center, axis=-1, keepdims=True)
    rate = lax.rsqrt(spread + 1e-05)
    return center * rate, rate


def dot(left, right, left_dim=1, right_dim=0):
    return lax.dot_general(
        left, right, (((left_dim,), (right_dim,)), ((), ())), preferred_element_type=jnp.float32
    )


def pick_matrix(target, slot_rows):
    width = target.shape[-1]
    rows = lax.broadcasted_iota(jnp.int32, (slot_rows, width), 0)
    return jnp.where(rows == target, 1.0, 0.0).astype(jnp.bfloat16)


def column_sum(values):
    return jnp.sum(values, axis=0, keepdims=True)


def follow(plan, steps, moves):
    for name, *numbers in plan:
        if numbers:
            moves[name](*numbers)
        else:
            steps[name]()


def unpack(names, refs):
    assert len(names) == len(refs)
    return types.SimpleNamespace(**dict(zip(names, refs)))


QKV, OUT, UP, DOWN, VEC = range(5)
PIECES = 1
EARLY_BLOCKS = 2
FORWARD_PLAN = (
    ("gbegin", 1), ("gbegin", 3), ("gbegin", 10), ("gbegin", 2), ("gbegin", 0), ("gc", 1, 0), ("gc", 10, 0),
    ("gx", 1, 0), ("gx", 10, 0), ("gc", 0, 0), ("gc", 2, 0), ("packx",), ("gc", 10, 1), ("gx", 10, 1), ("gx", 2, 0),
    ("gc", 3, 0), ("gx", 3, 0), ("gx", 0, 0), ("gc", 0, 1), ("gc", 1, 1), ("gl", 10, 0), ("packg",), ("gc", 10, 2),
    ("gx", 10, 2), ("gc", 3, 1), ("gx", 0, 1), ("gx", 3, 1), ("gc", 2, 1), ("gl", 10, 1), ("gl", 3, 0),
    ("gx", 10, 3), ("gx", 2, 1), ("gx", 1, 1), ("gl", 0, 0), ("gl", 2, 0), ("gsh", 10, 0), ("gc", 0, 2),
    ("gbegin", 6), ("gl", 1, 0), ("gx", 0, 2), ("gbegin", 5), ("gl", 10, 2), ("gc", 3, 2), ("gc", 1, 2),
    ("gl", 10, 3), ("gc", 2, 2), ("gsh", 10, 1), ("gx", 1, 2), ("gbegin", 4), ("gx", 3, 2), ("gx", 2, 2), ("gd", 10),
    ("vectors",), ("gl", 0, 1), ("gl", 1, 1), ("gx", 0, 3), ("gx", 1, 3), ("zx", 6), ("gsh", 0, 0), ("gl", 2, 1),
    ("gsh", 1, 0), ("gc", 5, 0), ("ln1",), ("gl", 3, 1), ("gx", 2, 3), ("gl", 0, 2), ("gl", 0, 3), ("gsh", 0, 1),
    ("gc", 4, 0), ("gx", 3, 3), ("gl", 1, 2), ("gx", 5, 0), ("gl", 1, 3), ("gsh", 1, 1), ("gsh", 2, 0), ("gc", 5, 1),
    ("gl", 2, 2), ("gx", 4, 0), ("gbegin", 8), ("gbegin", 9), ("gl", 2, 3), ("zy", 6), ("gx", 5, 1), ("gsh", 3, 0),
    ("gc", 4, 1), ("gd", 1), ("gd", 0), ("p0",), ("p1",), ("gl", 5, 0), ("p2",), ("gx", 4, 1), ("gc", 8, 0),
    ("gl", 3, 2), ("at00",), ("gl", 3, 3), ("zc", 6, 0), ("at01",), ("gc", 5, 2), ("gl", 4, 0), ("at02",),
    ("gc", 4, 2), ("gx", 8, 0), ("gsh", 3, 1), ("at10",), ("gsh", 2, 1), ("at11",), ("gx", 4, 2), ("gbegin", 7),
    ("at12",), ("zc", 6, 1), ("gl", 4, 1), ("gx", 5, 2), ("at20",), ("gl", 5, 1), ("gx", 4, 3), ("gx", 5, 3),
    ("gsh", 5, 0), ("gc", 8, 1), ("at21",), ("gx", 8, 1), ("zx", 9), ("gsh", 4, 0), ("at22",), ("at30",),
    ("gl", 4, 2), ("zc", 6, 2), ("gsh", 6, 0), ("gc", 7, 0), ("gx", 7, 0), ("gd", 3), ("gd", 2), ("gl", 4, 3),
    ("gl", 8, 0), ("gsh", 4, 1), ("at31",), ("gl", 5, 2), ("gl", 5, 3), ("gsh", 5, 1), ("gsh", 6, 1), ("gc", 8, 2),
    ("at32",), ("zy", 9), ("norm2",), ("gc", 7, 1), ("gx", 7, 1), ("gx", 8, 2), ("gd", 5), ("gl", 7, 0), ("gd", 4),
    ("gd", 6), ("h0",), ("rc", 0), ("gc", 7, 2), ("zc", 9, 0), ("gl", 8, 1), ("gx", 7, 2), ("rc", 1), ("gl", 7, 1),
    ("h1",), ("rc", 3), ("re", 0, 0), ("gx", 7, 3), ("rc", 2), ("gsh", 7, 0), ("re", 1, 0), ("gx", 8, 3),
    ("zc", 9, 1), ("h2",), ("re", 3, 0), ("re", 2, 0), ("gsh", 8, 0), ("h3",), ("zc", 9, 2), ("gl", 8, 2),
    ("gl", 7, 2), ("gl", 8, 3), ("gl", 7, 3), ("re", 1, 1), ("gsh", 7, 1), ("gsh", 9, 0), ("gsh", 8, 1),
    ("re", 3, 1), ("re", 2, 1), ("gsh", 9, 1), ("re", 0, 1), ("re", 3, 2), ("re", 1, 2), ("gd", 9), ("gd", 7),
    ("gd", 8), ("last",), ("re", 0, 2), ("re", 2, 2),
)
BACKWARD_PLAN = (
    ("start",), ("core", 9), ("core", 8), ("hb0",), ("hb1",), ("e", 9, 0), ("e", 8, 0), ("core", 6), ("hb2",),
    ("hb3",), ("core", 7), ("e", 6, 0), ("mp0",), ("e", 8, 1), ("e", 7, 0), ("mp1",), ("og",), ("tc",), ("at00",),
    ("core", 5), ("at01",), ("at02",), ("e", 8, 2), ("e", 9, 1), ("at10",), ("at11",), ("e", 6, 1), ("zs", 8),
    ("at12",), ("at20",), ("e", 9, 2), ("at21",), ("e", 7, 1), ("core", 4), ("e", 5, 0), ("zs", 9), ("at22",),
    ("at30",), ("e", 4, 0), ("at31",), ("at32",), ("gq0",), ("core", 0), ("gq1",), ("core", 1), ("gq2",),
    ("e", 7, 2), ("zs", 7), ("e", 5, 1), ("e", 0, 0), ("gq3",), ("e", 1, 0), ("core", 2), ("e", 6, 2), ("bias",),
    ("core", 3), ("ip0",), ("e", 4, 1), ("zs", 6), ("e", 2, 0), ("e", 5, 2), ("ip1",), ("zs", 5), ("e", 3, 0),
    ("e", 0, 1), ("e", 1, 1), ("cut",), ("core", 10), ("res", 7, 0), ("e", 4, 2), ("zs", 4), ("e", 10, 0),
    ("res", 6, 0), ("e", 2, 1), ("res", 9, 0), ("e", 1, 2), ("zs", 1), ("e", 3, 1), ("e", 10, 1), ("e", 0, 2),
    ("zs", 0), ("res", 8, 0), ("e", 3, 2), ("e", 2, 2), ("zs", 3), ("res", 4, 0), ("e", 10, 2), ("zs", 10),
    ("res", 1, 0), ("zs", 2), ("res", 10, 0), ("res", 0, 0), ("res", 5, 0), ("res", 3, 0), ("res", 2, 0),
)
GATHER_IN = ("tokens", "cotangent", "mask", "counts", "w0", "w1", "w2", "w3", "w4")
KEPT = ("x", "g", "h1", "qkv", "probs", "context", "middle", "h2", "slope", "gd", "full0", "full1", "full2", "full3", "early")
FORWARD_SCRATCH = KEPT + (
    "full4", "first_sums", "pair_sums", "sum_send", "sum_recv", "pair", "act", "ub", "chain_sem", "send_sem", "recv_sem", "share_send", "share_recv",
    "keep_sem", "save_sem", "load_sem", "back_sem",
)


def forward_kernel(chain, parts, *refs):
    n_in = len(GATHER_IN)
    r = unpack(GATHER_IN, refs[:n_in])
    saved = unpack(KEPT, refs[n_in : n_in + len(KEPT)])
    packed, vec, target = refs[n_in + len(KEPT) : n_in + len(KEPT) + 3]
    s = unpack(FORWARD_SCRATCH, refs[n_in + len(KEPT) + 3 :])
    model = s.x.shape[1]
    slots, _, both = target.shape
    slot_rows = s.x.shape[0] // slots
    total = s.x.shape[0]
    patches = both // 2
    place = Place(chain)
    mine = place.shard()
    own = (r.w0, r.w1, r.w2, r.w3, r.w4)
    devices = 8 * chain
    share = model // devices
    hidden = s.act.shape[1]
    up_share = hidden // devices
    per_row = model // up_share
    samples = 2 * slots
    first_sample = (lax.axis_index("gx") * slots + lax.axis_index("gy")) * samples
    full = (s.full0, s.full1, s.full2, s.full3, s.full4)
    saves = []

    def save(name, where=Ellipsis):
        copy = pltpu.make_async_copy(
            getattr(s, name).at[where], getattr(saved, name).at[where], s.save_sem.at[len(saves)]
        )
        copy.start()
        saves.append(copy)

    loads = [
        pltpu.make_async_copy(
            r.tokens.at[pl.ds(half * slots, slots)],
            s.pair.at[:, pl.ds(half * patches, patches)],
            s.load_sem.at[half],
        )
        for half in range(2)
    ]
    grad_loads = [
        pltpu.make_async_copy(
            r.cotangent.at[half * slots + slot],
            s.act.at[pl.ds(half * patches, patches), pl.ds(slot * model, model)],
            s.load_sem.at[2 + half * slots + slot],
        )
        for half in range(2)
        for slot in range(slots)
    ]
    for copy in loads + grad_loads:
        copy.start()
    shape = (samples, patches)
    at_sample = lax.broadcasted_iota(jnp.int32, shape, 0)
    limit = jnp.zeros(shape, jnp.int32)
    offset = jnp.zeros(shape, jnp.int32)
    for sample in range(samples):
        limit = jnp.where(at_sample == sample, r.counts[first_sample + sample], limit)
        if sample >= slots:
            offset = jnp.where(at_sample == sample, r.counts[first_sample + sample - slots], offset)
    square = (patches, patches)
    upper = lax.broadcasted_iota(jnp.int32, square, 0) <= lax.broadcasted_iota(jnp.int32, square, 1)
    land = r.mask[...] == 1
    rank = dot(jnp.where(land, 1.0, 0.0).astype(jnp.bfloat16), jnp.where(upper, 1.0, 0.0).astype(jnp.bfloat16))
    rank = rank.astype(jnp.int32) - 1
    places = jnp.where(land & (rank < limit), rank + offset, -1)
    for slot in range(slots):
        target[slot] = jnp.concatenate([places[slot : slot + 1], places[slots + slot : slots + slot + 1]], axis=1)
    engine = Gather(
        place, parts, own, full, (s.chain_sem, s.send_sem, s.recv_sem, s.share_send, s.share_recv)
    )
    keeps = [pltpu.make_async_copy(own[at], full[at].at[mine], s.keep_sem.at[at]) for at in range(5)]
    for keep in keeps:
        keep.start()
    place.greet()

    def rows_of(slot):
        return pl.ds(slot * slot_rows, slot_rows)

    def pack_inputs():
        for copy in loads + keeps:
            copy.wait()
        for slot in range(slots):
            s.x[rows_of(slot), :] = dot(
                pick_matrix(target[slot], slot_rows), s.pair[slot]
            ).astype(jnp.bfloat16)
        save("x")

    def pack_grads():
        for copy in grad_loads:
            copy.wait()
        for slot in range(slots):
            patch_grads = s.act[pl.ds(0, both), pl.ds(slot * model, model)]
            s.g[rows_of(slot), :] = dot(
                pick_matrix(target[slot], slot_rows), patch_grads
            ).astype(jnp.bfloat16)
        save("g")

    def done(part):
        engine.finish(part)
        at, first, width, _ = parts[part]
        if at != VEC:
            save("full%d" % at, (Ellipsis, pl.ds(first, width)))

    def place_vector(at, carry):
        rows, up_rows = carry
        piece = s.full4[at // 8, at // 4 % 2, at // 2 % 2, at % 2].astype(jnp.float32)
        wide = jnp.concatenate([piece, jnp.zeros((16, model - 128), jnp.float32)], axis=1)
        rows = rows + pltpu.roll(wide[:8], at * share, 1)
        moved = pltpu.roll(wide[8:], (at % per_row) * up_share, 1)
        here = lax.broadcasted_iota(jnp.int32, (8, model), 0) == at // per_row
        up_rows = up_rows + jnp.where(here, jnp.broadcast_to(moved[:1], (8, model)), 0.0)
        return rows, up_rows

    up_turns = hidden // model

    def place_vectors():
        zeros = jnp.zeros((8, model), jnp.float32)
        rows, up_rows = lax.fori_loop(0, devices, place_vector, (zeros, zeros))
        vec[...] = rows
        for at in range(up_turns):
            s.ub[at] = up_rows[at : at + 1]

    def norm_one(slot, carry):
        at = rows_of(slot)
        n, _ = normalised(s.x[at, :].astype(jnp.float32))
        s.h1[at, :] = (n * vec[0:1] + vec[1:2]).astype(jnp.bfloat16)
        return carry

    def norm_ones():
        lax.fori_loop(0, slots, norm_one, 0)
        save("h1")

    def project(section):
        bias = vec[2:3] if section == 0 else vec[3:4]
        columns = pl.ds(section * model, model)
        weight = s.full0[:, :, :, :, :, columns].reshape(model, model)

        def chunk(at, carry):
            here = pl.ds(at * (total // 2), total // 2)
            value = dot(s.h1[here, :], weight)
            if section != 1:
                value = value + bias
            value = value.astype(jnp.bfloat16)
            if section == 0:
                value = value * jnp.bfloat16(HD**-0.5)
            s.qkv[section, here, :] = value
            return carry

        lax.fori_loop(0, 2, chunk, 0)
        save("qkv", section)

    low_lane = lax.broadcasted_iota(jnp.int32, (slot_rows, 2 * HD), 1) < HD
    none = jnp.zeros((slot_rows, 2 * HD), jnp.bfloat16)

    def attend(slot, turn):
        one = r.counts[first_sample + slot]
        two = one + r.counts[first_sample + slot + slots]
        shape = (slot_rows, slot_rows)
        at_row = lax.broadcasted_iota(jnp.int32, shape, 0)
        at_column = lax.broadcasted_iota(jnp.int32, shape, 1)
        same = ((at_row >= one).astype(jnp.int32) + (at_row >= two).astype(jnp.int32)) == (
            (at_column >= one).astype(jnp.int32) + (at_column >= two).astype(jnp.int32)
        )
        bias = jnp.where(same, 0.0, -1000000000.0)

        for inner in range(2):
            pair = turn * 2 + inner
            columns = pl.ds(pair * 2 * HD, 2 * HD)
            query = s.qkv[0, rows_of(slot), columns]
            key = s.qkv[1, rows_of(slot), columns]
            value = s.qkv[2, rows_of(slot), columns]
            context = None
            for head in range(2):
                mask = low_lane if head == 0 else ~low_lane
                scores = dot(jnp.where(mask, query, none), key, 1, 1) + bias
                expo = jnp.exp(scores - jnp.max(scores, axis=-1, keepdims=True))
                probs = (expo / jnp.sum(expo, axis=-1, keepdims=True)).astype(jnp.bfloat16)
                s.probs[slot * HEADS + pair * 2 + head] = probs
                term = dot(probs, jnp.where(mask, value, none))
                context = term if context is None else context + term
            s.context[rows_of(slot), columns] = context.astype(jnp.bfloat16)

    def norm_two(slot, carry):
        at = rows_of(slot)
        weight = s.full1[...].reshape(model, model)
        middle = s.x[at, :].astype(jnp.float32) + dot(s.context[at, :], weight) + vec[4:5]
        s.middle[at, :] = middle
        n, _ = normalised(middle)
        s.h2[at, :] = (n * vec[5:6] + vec[6:7]).astype(jnp.bfloat16)
        return carry

    def norm_twos():
        save("probs")
        save("context")
        lax.fori_loop(0, slots, norm_two, 0)
        save("middle")
        save("h2")

    down_rows = s.gd.shape[4]
    block_rows = chain // (hidden // model)
    early_parts = [
        part[:4] + (block * block_rows, block_rows)
        for block in range(hidden // model - 1)
        for part in halves([item.shape[-1] for item in full])
        if part[0] == DOWN
    ][: 2 * EARLY_BLOCKS]
    adder = Scatter(
        place,
        early_parts,
        {DOWN: s.gd},
        {DOWN: None},
        {DOWN: (s.first_sums, s.pair_sums, s.early)},
        (s.sum_send, s.sum_recv, None, None),
    )

    def hidden_block(block):
        for half in range(PIECES):
            first_column = block * model + half * (model // PIECES)
            columns = pl.ds(first_column, model // PIECES)
            weight = s.full2[:, :, :, :, :, columns].reshape(model, model // PIECES)
            bias = s.ub[block][:, half * (model // PIECES) : (half + 1) * (model // PIECES)]

            def chunk(slot, carry, columns=columns, weight=weight, bias=bias):
                at = rows_of(slot)
                value = dot(s.h2[at, :], weight) + bias
                share_of = 0.5 + 0.5 * lax.erf(value * 0.7071067811865476)
                s.act[at, columns] = (value * share_of).astype(jnp.bfloat16)
                slope = share_of + value * jnp.exp(-0.5 * value * value) * 0.3989422804014327
                s.slope[at, columns] = slope.astype(jnp.bfloat16)
                return carry

            lax.fori_loop(0, slots, chunk, 0)
            grad = dot(s.act[:, columns], s.g[...], 0, 0).astype(jnp.bfloat16)
            for at in range(model // PIECES // down_rows):
                to = first_column // down_rows + at
                s.gd[to // 8, to // 4 % 2, to // 2 % 2, to % 2] = grad[at * down_rows : (at + 1) * down_rows]
        save("slope", (slice(None), pl.ds(block * model, model)))
        if block >= EARLY_BLOCKS:
            save("gd", pl.ds(block * block_rows, block_rows))


    def last(slot, carry):
        at = rows_of(slot)
        weight = s.full3[...].reshape(hidden, model)
        value = s.middle[at, :] + dot(s.act[at, :], weight) + vec[7:8]
        s.pair[slot, pl.ds(0, slot_rows), :] = value.astype(jnp.bfloat16)
        return carry

    def lasts():
        lax.fori_loop(0, slots, last, 0)
        copy = pltpu.make_async_copy(s.pair.at[:, pl.ds(0, slot_rows)], packed, s.back_sem)
        copy.start()
        saves.append(copy)

    def early_core(part):
        adder.core(part).start()

    def early_up(part, level):
        adder.up_one(part, level)
        if level == 2:
            _, first, width, _, low, rows = early_parts[part]
            save("early", (pl.ds(low, rows), slice(None), pl.ds(first, width)))

    def share_out(part, half):
        engine.sharing(part, half).start()

    call = functools.partial
    steps = {"packx": pack_inputs, "packg": pack_grads, "vectors": place_vectors, "ln1": norm_ones}
    steps |= {"norm2": norm_twos, "last": lasts}
    for section in range(3):
        steps["p%d" % section] = call(project, section)
    for block in range(up_turns):
        steps["h%d" % block] = call(hidden_block, block)
    for slot in range(slots):
        for turn in range(HEADS // 4):
            steps["at%d%d" % (slot, turn)] = call(attend, slot, turn)
    moves = {"gbegin": engine.begin, "gc": engine.along, "gx": engine.across, "gl": engine.last}
    moves |= {"gsh": share_out, "gd": done, "rc": early_core, "re": early_up}
    moves |= {"zx": engine.cross_first, "zy": engine.cross_second, "zc": engine.along_last}
    follow(FORWARD_PLAN, steps, moves)
    for part in range(len(early_parts)):
        adder.finish_pairs(part)
    for copy in saves:
        copy.wait()


def any_spec():
    return pl.BlockSpec(memory_space=pl.ANY)


def vmem_spec():
    return pl.BlockSpec(memory_space=pltpu.VMEM)


def run_forward(chain, slots, tokens, cotangent, mask, counts, shards):
    devices = 8 * chain
    samples, patches, model = tokens.shape
    total = samples * patches * 3 // 4
    slot_rows = total // slots
    hidden = shards[UP].shape[1]
    parts = gather_parts([item.shape[1] for item in shards])
    down = shards[DOWN].shape
    early_count = 2 * EARLY_BLOCKS
    low = jnp.bfloat16
    kept = [
        ((total, model), low),
        ((total, model), low),
        ((total, model), low),
        ((3, total, model), low),
        ((slots * HEADS, slot_rows, slot_rows), low),
        ((total, model), low),
        ((total, model), jnp.float32),
        ((total, model), low),
        ((total, hidden), low),
        ((chain, 2, 2, 2) + down, low),
    ] + [((chain, 2, 2, 2) + item.shape, low) for item in shards[:4]]
    kept.append(((chain,) + down, low))
    outs = kept + [
        ((slots, slot_rows, model), low),
        ((8, model), jnp.float32),
        ((slots, 1, 2 * patches), jnp.int32),
    ]
    scratch = [pltpu.VMEM(*item) for item in kept] + [
        pltpu.VMEM((chain, 2, 2, 2) + shards[VEC].shape, low),
        pltpu.VMEM((chain, 2, 2) + down, low),
        pltpu.VMEM((chain, 2) + down, low),
        pltpu.SemaphoreType.DMA((early_count, 3)),
        pltpu.SemaphoreType.DMA((early_count, 3)),
        pltpu.VMEM((slots, 2 * patches, model), low),
        pltpu.VMEM((total, hidden), low),
        pltpu.VMEM((hidden // model, 1, model), jnp.float32),
        pltpu.SemaphoreType.DMA((len(parts), 2, chain, 4)),
        pltpu.SemaphoreType.DMA((len(parts), 2)),
        pltpu.SemaphoreType.DMA((len(parts), devices)),
        pltpu.SemaphoreType.DMA((len(parts), 2)),
        pltpu.SemaphoreType.DMA((len(parts), 2)),
        pltpu.SemaphoreType.DMA((5,)),
        pltpu.SemaphoreType.DMA((len(KEPT) + 16,)),
        pltpu.SemaphoreType.DMA((2 + 2 * slots,)),
        pltpu.SemaphoreType.DMA,
    ]
    return pl.pallas_call(
        functools.partial(forward_kernel, chain, parts),
        out_shape=[jax.ShapeDtypeStruct(*item) for item in outs],
        in_specs=[any_spec(), any_spec(), vmem_spec(), pl.BlockSpec(memory_space=pltpu.SMEM)]
        + [any_spec()] * 4
        + [vmem_spec()],
        out_specs=[any_spec()] * (len(outs) - 2) + [vmem_spec()] * 2,
        scratch_shapes=scratch,
        compiler_params=pltpu.CompilerParams(
            collective_id=0, has_side_effects=True, vmem_limit_bytes=60 * 2**20
        ),
        name="forward",
    )(tokens, cotangent, mask, counts, *shards)


BACKWARD_IN = ("g", "slope", "w_down", "h2", "gd", "w_up", "middle", "context", "w_out", "qkv", "probs", "h1", "x", "w_qkv", "early", "vec")
BACKWARD_OUT = ("sum0", "sum1", "sum2", "sum3", "sum4", "packed")
BACKWARD_SCRATCH = (
    "g", "slope", "w_down", "h2", "gd", "w_up", "middle", "context", "w_out", "probs",
    "vg", "ug", "t0", "t1", "t2", "t4",
)
LOADS = ("g", "h2", "gd", "d0", "d1", "d2", "d3", "s0", "s1", "s2", "s3", "w_up", "middle", "context", "w_out", "probs", "w_qkv", "qkv0", "qkv1", "qkv2", "x", "h1", "early")


def backward_kernel(chain, parts, *refs):
    n_in, n_out, n_s = len(BACKWARD_IN), len(BACKWARD_OUT), len(BACKWARD_SCRATCH)
    r = unpack(BACKWARD_IN, refs[:n_in])
    o = unpack(BACKWARD_OUT, refs[n_in : n_in + n_out])
    at = n_in + n_out
    s = unpack(BACKWARD_SCRATCH, refs[at : at + n_s])
    buffers = refs[at + n_s : at + n_s + 20]
    load_sem, back_sem, *sems = refs[at + n_s + 20 :]
    got = [buffers[4 * k : 4 * k + 4] for k in range(5)]
    total, model = s.g.shape
    hidden = s.slope.shape[1]
    slots = lax.axis_size("gy")
    slot_rows = total // slots
    place = Place(chain)
    loads = {}

    def fetch(name, source, into):
        loads[name] = pltpu.make_async_copy(source, into, load_sem.at[LOADS.index(name)])
        loads[name].start()

    def need(*names):
        for name in names:
            loads[name].wait()

    done_rows = chain - s.gd.shape[0]
    fetch("g", r.g, s.g)
    for block in range(hidden // model):
        lanes = pl.ds(block * model, model)
        fetch("d%d" % block, r.w_down.at[lanes], s.w_down.at[lanes])
        fetch("s%d" % block, r.slope.at[:, lanes], s.slope.at[:, lanes])
        if block == 0:
            fetch("h2", r.h2, s.h2)
            fetch("gd", r.gd.at[pl.ds(done_rows, chain - done_rows), :, :, place.d], s.gd)
    for name in ("w_up", "middle", "context", "w_out", "probs"):
        fetch(name, getattr(r, name), getattr(s, name))
    fetch("early", r.early.at[pl.ds(0, done_rows)], got[DOWN][2].at[pl.ds(0, done_rows)])
    place.greet(far=True)
    engine = Scatter(
        place, parts, (s.t0, s.t1, s.t2, r.gd, s.t4), (None, None, None, s.gd, None), got, sems
    )
    groups = [[k for k, part in enumerate(parts) if part[0] == name] for name in range(5)]
    outs = (o.sum0, o.sum1, o.sum2, o.sum3, o.sum4)

    def rows_of(slot):
        return pl.ds(slot * slot_rows, slot_rows)

    def shards_of(value, like):
        return value.reshape(like.shape[:5] + (value.shape[-1],)).astype(jnp.bfloat16)

    def first_sums():
        need("g", "h2")
        s.vg[...] = jnp.zeros_like(s.vg)
        s.ug[...] = jnp.zeros_like(s.ug)
        s.vg[7:8] = column_sum(s.g[...].astype(jnp.float32))

    def hidden_block(block):
        need("d%d" % block, "s%d" % block)
        for half in range(PIECES):
            first_column = block * model + half * (model // PIECES)
            columns = pl.ds(first_column, model // PIECES)
            weight = s.w_down[pl.ds(first_column, model // PIECES), :]

            def chunk(slot, carry, columns=columns, weight=weight):
                here = rows_of(slot)
                value = dot(s.g[here, :], weight, 1, 1) * s.slope[here, columns].astype(jnp.float32)
                value = value.astype(jnp.bfloat16)
                s.slope[here, columns] = value
                return carry + column_sum(value.astype(jnp.float32))

            sums = lax.fori_loop(0, slots, chunk, jnp.zeros((1, model // PIECES), jnp.float32))
            s.ug[block : block + 1, half * (model // PIECES) : (half + 1) * (model // PIECES)] = sums
            s.t2[:, :, :, :, :, columns] = shards_of(dot(s.h2[...], s.slope[:, columns], 0, 0), s.t2)

    def fetch_more():
        for section in range(3):
            fetch("qkv%d" % section, r.qkv.at[section], s.w_down.at[pl.ds(section * model, model)])
        fetch("x", r.x, s.w_down.at[pl.ds(3 * model, model)])
        need("w_up", "middle")

    half_rows = total // 2

    def middle_part(half):
        if half == 0:
            fetch_more()
        grad = dot(s.slope[pl.ds(half * half_rows, half_rows), :], s.w_up[...], 1, 1)
        for inner in range(slots // 2):
            here = rows_of(half * (slots // 2) + inner)
            part = grad[inner * slot_rows : (inner + 1) * slot_rows]
            n, rate = normalised(s.middle[here, :])
            s.vg[5:6] += column_sum(part * n)
            s.vg[6:7] += column_sum(part)
            scaled = part * r.vec[5:6]
            mean_one = jnp.mean(scaled, axis=-1, keepdims=True)
            mean_two = jnp.mean(scaled * n, axis=-1, keepdims=True)
            full_grad = s.g[here, :].astype(jnp.float32) + rate * (scaled - mean_one - n * mean_two)
            s.middle[here, :] = full_grad
            branch = full_grad.astype(jnp.bfloat16)
            s.h2[here, :] = branch
            s.vg[4:5] += column_sum(branch.astype(jnp.float32))

    joined = pl.ds(0, 3 * model)

    def out_grads():
        fetch("w_qkv", r.w_qkv, s.w_up.at[:, joined])
        fetch("h1", r.h1, s.slope.at[:, pl.ds(3 * model, model)])
        need("context", "w_out")
        s.t1[...] = shards_of(dot(s.context[...], s.h2[...], 0, 0), s.t1)

    def to_context(slot, carry):
        here = rows_of(slot)
        s.context[here, :] = dot(s.h2[here, :], s.w_out[...], 1, 1).astype(jnp.bfloat16)
        return carry

    def to_contexts():
        lax.fori_loop(0, slots, to_context, 0)
        need("qkv0", "qkv1", "qkv2", "probs")

    low_lane = lax.broadcasted_iota(jnp.int32, (slot_rows, 2 * HD), 1) < HD
    none = jnp.zeros((slot_rows, 2 * HD), jnp.bfloat16)

    def attend(slot, turn):
        for inner in range(2):
            pair = turn * 2 + inner
            first_column = pair * 2 * HD
            columns = pl.ds(first_column, 2 * HD)
            query = s.w_down[pl.ds(slot * slot_rows, slot_rows), columns]
            key = s.w_down[pl.ds(model + slot * slot_rows, slot_rows), columns]
            value = s.w_down[pl.ds(2 * model + slot * slot_rows, slot_rows), columns]
            grad = s.context[rows_of(slot), columns]
            totals = [None, None, None]
            for head in range(2):
                mask = low_lane if head == 0 else ~low_lane
                grad_here = jnp.where(mask, grad, none)
                low_probs = s.probs[slot * HEADS + pair * 2 + head]
                probs = low_probs.astype(jnp.float32)
                weighted = probs * dot(grad_here, value, 1, 1)
                share = jnp.sum(weighted, axis=-1, keepdims=True)
                scores = (weighted - probs * share).astype(jnp.bfloat16)
                terms = (
                    dot(scores, jnp.where(mask, key, none)),
                    dot(scores, jnp.where(mask, query, none), 0, 0),
                    dot(low_probs, grad_here, 0, 0),
                )
                totals = [b if a is None else a + b for a, b in zip(totals, terms)]
            totals[0] = totals[0] * HD**-0.5
            for section in range(3):
                s.slope[rows_of(slot), pl.ds(section * model + first_column, 2 * HD)] = totals[
                    section
                ].astype(jnp.bfloat16)

    h1 = pl.ds(3 * model, model)

    def qkv_grads(turn):
        if turn == 0:
            need("h1", "w_qkv", "x")
        _, first, width, *_ = parts[groups[QKV][turn]]
        columns = pl.ds(first, width)
        s.t0[:, :, :, :, :, columns] = shards_of(dot(s.slope[:, h1], s.slope[:, columns], 0, 0), s.t0)

    def bias_sums():
        s.vg[2:3] = column_sum(s.slope[:, pl.ds(0, model)].astype(jnp.float32))
        s.vg[3:4] = column_sum(s.slope[:, pl.ds(2 * model, model)].astype(jnp.float32))

    def input_part(half):
        grad = dot(s.slope[pl.ds(half * half_rows, half_rows), joined], s.w_up[:, joined], 1, 1)
        for inner in range(slots // 2):
            slot = half * (slots // 2) + inner
            here = rows_of(slot)
            part = grad[inner * slot_rows : (inner + 1) * slot_rows]
            n, rate = normalised(
                s.w_down[pl.ds(3 * model + slot * slot_rows, slot_rows), :].astype(jnp.float32)
            )
            s.vg[0:1] += column_sum(part * n)
            s.vg[1:2] += column_sum(part)
            scaled = part * r.vec[0:1]
            mean_one = jnp.mean(scaled, axis=-1, keepdims=True)
            mean_two = jnp.mean(scaled * n, axis=-1, keepdims=True)
            full_grad = s.middle[here, :] + rate * (scaled - mean_one - n * mean_two)
            s.g[here, :] = full_grad.astype(jnp.bfloat16)
        here = pl.ds(half * half_rows, half_rows)
        backs.append(pltpu.make_async_copy(s.g.at[here], o.packed.at[here], back_sem.at[half]))
        backs[-1].start()

    backs = []
    devices = 8 * chain
    share = model // devices
    up_share = hidden // devices
    per_row = model // up_share

    def cut_vector(index, carry):
        rows = pltpu.roll(s.vg[...], model - index * share, 1)[:, :128]
        here = lax.broadcasted_iota(jnp.int32, (8, model), 0) == index // per_row
        row = jnp.broadcast_to(column_sum(jnp.where(here, s.ug[...], 0.0)), (8, model))
        up_rows = pltpu.roll(row, model - (index % per_row) * up_share, 1)[:, :128]
        s.t4[index // 8, index // 4 % 2, index // 2 % 2, index % 2] = jnp.concatenate([rows, up_rows], axis=0)
        return carry

    def cut_vectors():
        lax.fori_loop(0, devices, cut_vector, 0)

    def core(part):
        engine.core(part).start()

    unread = (["gd"], ["early"])

    def add_up(part, level):
        if part in groups[DOWN] and unread[0]:
            need(unread[0].pop())
        engine.up_one(part, level)

    def along(part):
        if part in groups[DOWN] and unread[1]:
            need(unread[1].pop())
        engine.along(part)

    def result(part, _):
        engine.result(part, outs)

    call = functools.partial
    steps = {"start": first_sums, "og": out_grads, "tc": to_contexts, "bias": bias_sums, "cut": cut_vectors}
    for half in range(2):
        steps["mp%d" % half] = call(middle_part, half)
        steps["ip%d" % half] = call(input_part, half)
    for turn in range(4):
        steps["gq%d" % turn] = call(qkv_grads, turn)
    for block in range(hidden // model):
        steps["hb%d" % block] = call(hidden_block, block)
    for slot in range(slots):
        for turn in range(HEADS // 4):
            steps["at%d%d" % (slot, turn)] = call(attend, slot, turn)
    moves = {"core": core, "e": add_up, "zs": along, "res": result}
    follow(BACKWARD_PLAN, steps, moves)
    for part in range(len(parts)):
        engine.finish(part)
    for copy in backs:
        copy.wait()


def run_backward(chain, kept, vec, shards):
    total, model = kept.x.shape
    hidden = shards[UP].shape[1]
    last_rows = chain - chain // (hidden // model) * EARLY_BLOCKS
    parts = [
        part + ((chain - last_rows, last_rows) if part[0] == DOWN else (0, chain))
        for part in scatter_parts([item.shape[1] for item in shards])
    ]
    low, wide = jnp.bfloat16, jnp.float32
    lead = (chain, 2, 2, 2)
    fulls = [
        item.reshape(-1, item.shape[-1]) for item in (kept.full0, kept.full1, kept.full2, kept.full3)
    ]
    given = types.SimpleNamespace(
        g=kept.g, slope=kept.slope, w_down=fulls[DOWN], h2=kept.h2,
        gd=kept.gd, w_up=fulls[UP], middle=kept.middle,
        context=kept.context, w_out=fulls[OUT], qkv=kept.qkv, probs=kept.probs, h1=kept.h1, x=kept.x,
        w_qkv=fulls[QKV], early=kept.early, vec=vec,
    )
    scratch = {name: pltpu.VMEM(getattr(given, name).shape, getattr(given, name).dtype) for name in BACKWARD_IN}
    scratch["gd"] = pltpu.VMEM((last_rows, 2, 2) + shards[DOWN].shape, low)
    scratch["vg"] = pltpu.VMEM((8, model), wide)
    scratch["ug"] = pltpu.VMEM((8, model), wide)
    for at in (QKV, OUT, UP, VEC):
        scratch["t%d" % at] = pltpu.VMEM(lead + shards[at].shape, wide if at == VEC else low)
    arrivals = []
    for at, item in enumerate(shards):
        for front in ((chain, 2, 2), (chain, 2), (chain,), (chain,)):
            arrivals.append(pltpu.VMEM(front + item.shape, wide if at == VEC else low))
    outs = [(item.shape, wide) for item in shards] + [((total, model), low)]
    return pl.pallas_call(
        functools.partial(backward_kernel, chain, parts),
        out_shape=[jax.ShapeDtypeStruct(*item) for item in outs],
        in_specs=[any_spec()] * (len(BACKWARD_IN) - 1) + [vmem_spec()],
        out_specs=[vmem_spec()] * 5 + [any_spec()],
        scratch_shapes=[scratch[name] for name in BACKWARD_SCRATCH]
        + arrivals
        + [
            pltpu.SemaphoreType.DMA((len(LOADS),)),
            pltpu.SemaphoreType.DMA((2,)),
            pltpu.SemaphoreType.DMA((len(parts), 3)),
            pltpu.SemaphoreType.DMA((len(parts), 3)),
            pltpu.SemaphoreType.DMA((len(parts), chain)),
            pltpu.SemaphoreType.DMA((len(parts), chain)),
        ],
        compiler_params=pltpu.CompilerParams(
            collective_id=1, has_side_effects=True, vmem_limit_bytes=63 * 2**20
        ),
        name="backward",
    )(*[getattr(given, name) for name in BACKWARD_IN])


def spread_kernel(target, rows, grads, *refs):
    sums, out_tokens, grad_tokens, outs = refs[:5], refs[5], refs[6], refs[7:]
    slot_rows = rows.shape[1]
    patches = out_tokens.shape[2]
    matrix = pick_matrix(target[0], slot_rows)
    for source, to in ((rows, out_tokens), (grads, grad_tokens)):
        spread = dot(matrix, source[0], 0, 0).astype(jnp.bfloat16)
        for half in range(2):
            to[half, 0] = spread[half * patches : (half + 1) * patches]

    @pl.when(pl.program_id(0) == 0)
    def _():
        for at in range(4):
            outs[at][...] = sums[at][...]
        table = sums[VEC]
        share = outs[4].shape[1]
        outs[6][...] = table[2:4, :share]
        for ref, row in zip((outs[4], outs[5]) + outs[7:], (0, 1, 4, 5, 6, 7, 8)):
            ref[...] = table[row : row + 1, : ref.shape[1]]


def run_spread(target, rows, grads, sums, share, up_share):
    slots, slot_rows, model = rows.shape
    patches = target.shape[2] // 2
    wide = jnp.float32

    def whole(shape):
        return pl.BlockSpec(shape, lambda i: (0,) * len(shape))

    tokens_spec = pl.BlockSpec((2, 1, patches, model), lambda i: (0, i, 0, 0))
    slot_spec = pl.BlockSpec((1, slot_rows, model), lambda i: (i, 0, 0))
    shapes = [item.shape for item in sums[:4]]
    shapes += [(1, share), (1, share), (2, share)] + [(1, share)] * 4 + [(1, up_share)]
    tokens_shape = jax.ShapeDtypeStruct((2, slots, patches, model), jnp.bfloat16)
    return pl.pallas_call(
        spread_kernel,
        grid=(slots,),
        out_shape=[tokens_shape] * 2 + [jax.ShapeDtypeStruct(shape, wide) for shape in shapes],
        in_specs=[pl.BlockSpec((1, 1, 2 * patches), lambda i: (i, 0, 0)), slot_spec, slot_spec]
        + [whole(item.shape) for item in sums],
        out_specs=[tokens_spec] * 2 + [whole(shape) for shape in shapes],
        compiler_params=pltpu.CompilerParams(vmem_limit_bytes=60 * 2**20),
        name="spread",
    )(target, rows, grads, *sums)


def per_device(
    tokens,
    land_mask,
    counts,
    ln1_gain,
    ln1_shift,
    qkv_weight,
    qv_bias,
    out_weight,
    out_bias,
    ln2_gain,
    ln2_shift,
    up_weight,
    up_bias,
    down_weight,
    down_bias,
    cotangent,
):
    chain = lax.axis_size("gx") // 2
    slots = lax.axis_size("gy")
    share, up_share = ln1_gain.shape[0], up_bias.shape[0]
    small = [ln1_gain, ln1_shift, qv_bias[0], qv_bias[1], out_bias, ln2_gain, ln2_shift, down_bias, up_bias]
    table = sum(
        jnp.pad(item[None], ((at, 15 - at), (0, 128 - item.shape[0]))) for at, item in enumerate(small)
    )
    shards = [qkv_weight, out_weight, up_weight, down_weight, table]
    *kept, packed, vec, target = run_forward(
        chain, slots, tokens, cotangent, land_mask, counts, shards
    )
    *sums, packed_grads = run_backward(chain, unpack(KEPT, kept), vec, shards)
    out_tokens, grad_tokens, *finals = run_spread(
        target, packed, packed_grads.reshape(packed.shape), sums, share, up_share
    )
    sum_qkv, sum_out, sum_up, sum_down, gain_one, shift_one, pair_bias = finals[:7]
    bias_out, gain_two, shift_two, bias_down, bias_up = finals[7:]
    return (
        out_tokens.reshape(tokens.shape),
        grad_tokens.reshape(tokens.shape),
        gain_one[0],
        shift_one[0],
        sum_qkv,
        pair_bias,
        sum_out,
        bias_out[0],
        gain_two[0],
        shift_two[0],
        sum_up,
        bias_up[0],
        sum_down,
        bias_down[0],
    )


def solution(mesh):
    placed = (
        P(("gx", "gy"), None, None),
        P(("gx", "gy"), None),
        P(),
        P(("gx", "gy")),
        P(("gx", "gy")),
        P(("gx", "gy"), None),
        P(None, ("gx", "gy")),
        P(("gx", "gy"), None),
        P(("gx", "gy")),
        P(("gx", "gy")),
        P(("gx", "gy")),
        P(("gx", "gy"), None),
        P(("gx", "gy")),
        P(("gx", "gy"), None),
        P(("gx", "gy")),
        P(("gx", "gy"), None, None),
    )
    return jax.shard_map(
        per_device,
        mesh=mesh,
        in_specs=placed,
        out_specs=(
            P(("gx", "gy"), None, None),
            P(("gx", "gy"), None, None),
            P(("gx", "gy")),
            P(("gx", "gy")),
            P(("gx", "gy"), None),
            P(None, ("gx", "gy")),
            P(("gx", "gy"), None),
            P(("gx", "gy")),
            P(("gx", "gy")),
            P(("gx", "gy")),
            P(("gx", "gy"), None),
            P(("gx", "gy")),
            P(("gx", "gy"), None),
            P(("gx", "gy")),
        ),
        check_vma=False,
    )
```

```python
import functools
import types

import jax
import jax.numpy as jnp
from jax import lax
from jax.experimental import pallas as pl
from jax.experimental.pallas import tpu as pltpu
from jax.sharding import PartitionSpec as P

HEADS = 12
HD = 64
MESH = pl.DeviceIdType.MESH


class Place:
    def __init__(self, chain):
        gx = lax.axis_index("gx")
        gy = lax.axis_index("gy")
        self.chain = chain
        self.a = gx // 2
        self.b = gx % 2
        self.c = gy // 2
        self.d = gy % 2

    def shard(self, a=None, b=None, c=None, d=None):
        a = self.a if a is None else a
        b = self.b if b is None else b
        c = self.c if c is None else c
        d = self.d if d is None else d
        return a, b, c, d

    def device(self, a=None, b=None, c=None, d=None):
        a = self.a if a is None else a
        b = self.b if b is None else b
        c = self.c if c is None else c
        d = self.d if d is None else d
        return (a * 2 + b, c * 2 + d)

    def greet(self, far=False):
        barrier = pltpu.get_barrier_semaphore()
        for to in (
            self.device(d=1 - self.d),
            self.device(c=1 - self.c),
            self.device(b=1 - self.b),
        ):
            pl.semaphore_signal(barrier, inc=1, device_id=to, device_id_type=MESH)

        def greet_row(row, carry):
            near = (row == self.a - 1) | (row == self.a + 1)

            @pl.when((row != self.a) if far else near)
            def _():
                pl.semaphore_signal(barrier, inc=1, device_id=self.device(a=row), device_id_type=MESH)

            return carry

        lax.fori_loop(0, self.chain, greet_row, 0)
        ends = (self.a > 0).astype(jnp.int32) + (self.a < self.chain - 1).astype(jnp.int32)
        pl.semaphore_wait(barrier, 3 + (self.chain - 1 if far else ends))


def halves(widths):
    parts = []
    for at, width in enumerate(widths):
        if width % 256:
            parts.append((at, 0, width, "b"))
        else:
            parts.append((at, 0, width // 2, "b"))
            parts.append((at, width // 2, width // 2, "c"))
    return parts


def gather_parts(widths):
    parts = []
    for at, width in enumerate(widths):
        third = width // 4 if at == UP else width // 3
        pair = (width - third) // 2
        if at in (UP, DOWN) and third % 128 == 0 and pair % 128 == 0:
            parts += [(at, 0, pair, "b"), (at, pair, pair, "c"), (at, 2 * pair, third, "z")]
        else:
            parts += [(at,) + part[1:] for part in halves([width])]
    return parts


class Gather:
    def __init__(self, place, parts, own, full, sems):
        self.place, self.parts, self.own, self.full = place, parts, own, full
        self.chain_sem, self.send_sem, self.recv_sem, self.share_send, self.share_recv = sems

    def view(self, part, index):
        at, first, width, _ = self.parts[part]
        return self.full[at].at[tuple(index) + (slice(None), pl.ds(first, width))]

    def copy(self, part, index, to, send, own=False):
        at, first, width, _ = self.parts[part]
        a, b, c, d = index
        return pltpu.make_async_remote_copy(
            src_ref=self.own[at].at[:, pl.ds(first, width)] if own else self.view(part, index),
            dst_ref=self.view(part, index),
            send_sem=send,
            recv_sem=self.recv_sem.at[part, ((a * 2 + b) * 2 + c) * 2 + d],
            device_id=to,
            device_id_type=MESH,
        )

    def flip(self, axis):
        return {axis: 1 - (self.place.b if axis == "b" else self.place.c)}

    def links(self, part):
        first = self.parts[part][3]
        return ("c", "b") if first == "c" else ("b", "c")

    def send_pair(self, part, index, level, own=False):
        to = self.place.device(**self.flip(self.links(part)[level]))
        self.copy(part, index, to, self.send_sem.at[part, level], own).start()

    def arrived(self, part, index):
        self.copy(part, index, self.place.device(d=1 - self.place.d), self.send_sem.at[part, 0]).wait_recv()

    def send_chain(self, part, way, index, step, own=False):
        place = self.place
        to = place.device(a=place.a + 1) if way == 0 else place.device(a=place.a - 1)
        column = index[1] * 2 + index[2]
        return self.copy(part, index, to, self.chain_sem.at[part, way, step, column], own)

    def send_ends(self, part, index, step, own=False):
        place = self.place
        pl.when(place.a < place.chain - 1)(lambda: self.send_chain(part, 0, index, step, own).start())
        pl.when(place.a > 0)(lambda: self.send_chain(part, 1, index, step, own).start())

    def cross_first(self, part):
        index = self.place.shard(b=1 - self.place.b)
        self.arrived(part, index)
        self.send_pair(part, index, 1)
        self.send_ends(part, index, 0)

    def cross_second(self, part):
        place = self.place
        for b in (place.b, 1 - place.b):
            index = place.shard(b=b, c=1 - place.c)
            self.arrived(part, index)
            self.send_ends(part, index, 0)

    def along_last(self, part, third):
        place = self.place
        steps = place.chain - 1

        def one(step, carry):
            for b in (place.b, 1 - place.b):
                for c in (place.c, 1 - place.c):

                    @pl.when(place.a - 1 - step >= 0)
                    def _(b=b, c=c):
                        index = place.shard(a=place.a - 1 - step, b=b, c=c)
                        self.arrived(part, index)
                        pl.when(place.a < steps)(lambda: self.send_chain(part, 0, index, step + 1).start())

                    @pl.when(place.a + 1 + step <= steps)
                    def _(b=b, c=c):
                        index = place.shard(a=place.a + 1 + step, b=b, c=c)
                        self.arrived(part, index)
                        pl.when(place.a > 0)(lambda: self.send_chain(part, 1, index, step + 1).start())

            return carry

        self.each(third * steps // 3, (third + 1) * steps // 3, one)

    def begin(self, part):
        place = self.place
        mine = place.shard()
        self.send_ends(part, mine, 0, True)
        for level in range(2):
            self.send_pair(part, mine, level, True)

    def each(self, low, high, one):
        if isinstance(low, int) and high - low == 1:
            one(low, 0)
        else:
            lax.fori_loop(low, high, one, 0)

    def along(self, part, third):
        place = self.place
        steps = place.chain - 1

        def one(step, carry):
            @pl.when(place.a - 1 - step >= 0)
            def _():
                index = place.shard(a=place.a - 1 - step)
                self.arrived(part, index)
                pl.when(place.a < steps)(lambda: self.send_chain(part, 0, index, step + 1).start())
                for level in range(2):
                    self.send_pair(part, index, level)

            @pl.when(place.a + 1 + step <= steps)
            def _():
                index = place.shard(a=place.a + 1 + step)
                self.arrived(part, index)
                pl.when(place.a > 0)(lambda: self.send_chain(part, 1, index, step + 1).start())
                for level in range(2):
                    self.send_pair(part, index, level)

            return carry

        self.each(third * steps // 3, (third + 1) * steps // 3, one)

    def at_distance(self, turn, one):
        place = self.place
        steps = place.chain - 1
        if turn == 0:
            one(place.a)
            return

        def both(step, carry):
            pl.when(place.a - step >= 0)(lambda: one(place.a - step))
            pl.when(place.a + step <= steps)(lambda: one(place.a + step))
            return carry

        self.each(1 + (turn - 1) * steps // 3, 1 + turn * steps // 3, both)

    def across(self, part, turn):
        first, _ = self.links(part)

        def one(row):
            index = self.place.shard(a=row, **self.flip(first))
            self.arrived(part, index)
            self.send_pair(part, index, 1)

        self.at_distance(turn, one)

    def last(self, part, turn):
        first, second = self.links(part)

        def one(row):
            self.arrived(part, self.place.shard(a=row, **self.flip(second)))
            self.arrived(part, self.place.shard(a=row, **self.flip(second), **self.flip(first)))

        self.at_distance(turn, one)

    def sharing(self, part, half):
        place = self.place
        every = slice(None)
        if self.links(part)[1] == "c":
            box = (every, every, 1 - place.c if half else place.c, place.d)
        else:
            box = (every, 1 - place.b if half else place.b, every, place.d)
        return pltpu.make_async_remote_copy(
            src_ref=self.view(part, box),
            dst_ref=self.view(part, box),
            send_sem=self.share_send.at[part, half],
            recv_sem=self.share_recv.at[part, half],
            device_id=place.device(d=1 - place.d),
            device_id_type=MESH,
        )

    def finish(self, part):
        place = self.place
        steps = place.chain - 1
        for half in range(2):
            self.sharing(part, half).wait()
        every = slice(None)
        chain_last = self.parts[part][3] == "z"
        boxes = ((pl.ds(0, 1), 0, 0, 0), (0, every, 0, 0)) if chain_last else ((every, 0, 0, 0), (every, every, 0, 0))
        for level, box in enumerate(boxes):
            block = self.view(part, box)
            pltpu.make_async_copy(block, block, self.send_sem.at[part, level]).wait()
        columns = [(place.b, place.c)]
        if chain_last:
            columns = [(b, c) for b in range(2) for c in range(2)]

        def sent(step, carry):
            for b, c in columns:

                @pl.when((place.a < steps) & (place.a - step >= 0))
                def _(b=b, c=c):
                    self.send_chain(part, 0, place.shard(a=place.a - step, b=b, c=c), step).wait_send()

                @pl.when((place.a > 0) & (place.a + step <= steps))
                def _(b=b, c=c):
                    self.send_chain(part, 1, place.shard(a=place.a + step, b=b, c=c), step).wait_send()

            return carry

        lax.fori_loop(0, steps, sent, 0)


def scatter_parts(widths):
    parts = []
    for at, width in enumerate(widths):
        if at == QKV:
            half, more = width // 2, -(-width // 512) * 128
            parts += [(at, 0, more, "b"), (at, half, more, "c")]
            parts += [(at, more, half - more, "b"), (at, half + more, half - more, "c")]
        else:
            parts += [(at,) + part[1:] for part in halves([width])]
    return parts


class Scatter:
    def __init__(self, place, parts, terms, kept, got, sems):
        self.place, self.parts, self.terms = place, parts, terms
        self.kept = kept
        self.got = got
        self.send_sem, self.recv_sem, self.chain_send, self.chain_recv = sems

    def rows(self, part):
        return pl.ds(*self.parts[part][4:])

    def pick(self, ref, lead, part):
        first, width = self.parts[part][1:3]
        return ref.at[lead + (slice(None), pl.ds(first, width))]

    def exchange(self, part, level, src, dst, to):
        return pltpu.make_async_remote_copy(
            src_ref=src,
            dst_ref=dst,
            send_sem=self.send_sem.at[part, level],
            recv_sem=self.recv_sem.at[part, level],
            device_id=to,
            device_id_type=MESH,
        )

    def core(self, part):
        place = self.place
        at = self.parts[part][0]
        every = slice(None)
        return self.exchange(
            part,
            0,
            self.pick(self.terms[at], (self.rows(part), every, every, 1 - place.d), part),
            self.pick(self.got[at][0], (self.rows(part), every, every), part),
            place.device(d=1 - place.d),
        )

    def lead(self, part, level, mine):
        place = self.place
        every = slice(None)
        first = self.parts[part][3]
        b = place.b if mine else 1 - place.b
        c = place.c if mine else 1 - place.c
        rows = self.rows(part)
        if level == 1:
            return (rows, b, every) if first == "b" else (rows, every, c)
        return (rows, c) if first == "b" else (rows, b)

    def pair(self, part, level):
        place = self.place
        at, first = self.parts[part][0], self.parts[part][3]
        axis = first if level == 1 else ("c" if first == "b" else "b")
        to = place.device(b=1 - place.b) if axis == "b" else place.device(c=1 - place.c)
        every = slice(None)
        dst = (self.rows(part), every) if level == 1 else (self.rows(part),)
        return self.exchange(
            part,
            level,
            self.pick(self.got[at][level - 1], self.lead(part, level, False), part),
            self.pick(self.got[at][level], dst, part),
            to,
        )

    def add_core(self, part):
        place = self.place
        at, first, width, _, low, rows = self.parts[part]
        self.core(part).wait_recv()
        terms, kept, got = self.terms[at], self.kept[at], self.got[at][0]
        columns = pl.ds(first, width)

        def one(i, carry):
            x, y, z = low + i // 4, i // 2 % 2, i % 2
            term = terms[x, y, z, place.d, :, columns] if kept is None else kept[x - low, y, z, :, columns]
            got[x, y, z, :, columns] = got[x, y, z, :, columns] + term
            return carry

        lax.fori_loop(0, 4 * rows, one, 0)

    def add_pair(self, part, level):
        place = self.place
        at, first, width, axis, low, rows = self.parts[part]
        self.pair(part, level).wait_recv()
        before, got = self.got[at][level - 1], self.got[at][level]
        columns = pl.ds(first, width)

        def one(i, carry):
            if level == 1:
                x, y = low + i // 2, i % 2
                if axis == "b":
                    kept = before[x, place.b, y, :, columns]
                else:
                    kept = before[x, y, place.c, :, columns]
                got[x, y, :, columns] = got[x, y, :, columns] + kept
            else:
                x = low + i
                kept = before[x, place.c if axis == "b" else place.b, :, columns]
                got[x, :, columns] = got[x, :, columns] + kept
            return carry

        lax.fori_loop(0, (2 if level == 1 else 1) * rows, one, 0)

    def toward(self, part, row):
        place = self.place
        at = self.parts[part][0]
        return pltpu.make_async_remote_copy(
            src_ref=self.pick(self.got[at][2], (row,), part),
            dst_ref=self.pick(self.got[at][3], (place.a,), part),
            send_sem=self.chain_send.at[part, row],
            recv_sem=self.chain_recv.at[part, place.a],
            device_id=place.device(a=row),
            device_id_type=MESH,
        )

    def along(self, part):
        place = self.place

        def one(back, carry):
            far = place.chain - 1 - back
            pl.when(place.a + far < place.chain)(lambda: self.toward(part, place.a + far).start())
            pl.when(place.a - far >= 0)(lambda: self.toward(part, place.a - far).start())
            return carry

        lax.fori_loop(0, place.chain - 1, one, 0)

    def result(self, part, out):
        place = self.place
        at, first, width = self.parts[part][:3]
        columns = pl.ds(first, width)
        got = self.got[at]
        out[at][:, columns] = got[2][place.a, :, columns].astype(jnp.float32)

        def one(row, carry):
            @pl.when(row != place.a)
            def _():
                pltpu.make_async_remote_copy(
                    src_ref=self.pick(got[3], (row,), part),
                    dst_ref=self.pick(got[3], (row,), part),
                    send_sem=self.chain_send.at[part, row],
                    recv_sem=self.chain_recv.at[part, row],
                    device_id=place.device(a=row),
                    device_id_type=MESH,
                ).wait_recv()
                out[at][:, columns] = out[at][:, columns] + got[3][row, :, columns].astype(jnp.float32)

            return carry

        lax.fori_loop(0, place.chain, one, 0)

    def finish_pairs(self, part):
        self.core(part).wait_send()
        for level in (1, 2):
            self.pair(part, level).wait_send()

    def finish(self, part):
        place = self.place
        self.finish_pairs(part)

        def one(row, carry):
            pl.when(row != place.a)(lambda: self.toward(part, row).wait_send())
            return carry

        lax.fori_loop(0, place.chain, one, 0)

    def up_one(self, part, level):
        if level == 0:
            self.add_core(part)
        else:
            self.add_pair(part, level)
        if level < 2:
            self.pair(part, level + 1).start()


def normalised(values):
    center = values - jnp.mean(values, axis=-1, keepdims=True)
    spread = jnp.mean(center * center, axis=-1, keepdims=True)
    rate = lax.rsqrt(spread + 1e-05)
    return center * rate, rate


def dot(left, right, left_dim=1, right_dim=0):
    return lax.dot_general(
        left, right, (((left_dim,), (right_dim,)), ((), ())), preferred_element_type=jnp.float32
    )


def pick_matrix(target, slot_rows):
    width = target.shape[-1]
    rows = lax.broadcasted_iota(jnp.int32, (slot_rows, width), 0)
    return jnp.where(rows == target, 1.0, 0.0).astype(jnp.bfloat16)


def column_sum(values):
    return jnp.sum(values, axis=0, keepdims=True)


def follow(plan, steps, moves):
    for name, *numbers in plan:
        if numbers:
            moves[name](*numbers)
        else:
            steps[name]()


def unpack(names, refs):
    assert len(names) == len(refs)
    return types.SimpleNamespace(**dict(zip(names, refs)))


QKV, OUT, UP, DOWN, VEC = range(5)
PIECES = 1
EARLY_BLOCKS = 2
FORWARD_PLAN = (
    ("gbegin", 1), ("gbegin", 2), ("gbegin", 10), ("gbegin", 0), ("gbegin", 3), ("gc", 1, 0), ("gc", 10, 0),
    ("gc", 2, 0), ("gx", 1, 0), ("gx", 10, 0), ("gx", 2, 0), ("gc", 0, 0), ("packx",), ("gx", 0, 0), ("gc", 10, 1),
    ("gc", 3, 0), ("gx", 3, 0), ("gc", 1, 1), ("gx", 10, 1), ("packg",), ("gc", 0, 1), ("gl", 10, 0), ("gc", 10, 2),
    ("gx", 10, 2), ("gc", 2, 1), ("gc", 3, 1), ("gx", 0, 1), ("gx", 1, 1), ("gl", 1, 0), ("gbegin", 6), ("gl", 0, 0),
    ("gl", 10, 1), ("gx", 10, 3), ("gx", 2, 1), ("gsh", 10, 0), ("gc", 1, 2), ("gl", 2, 0), ("gx", 3, 1),
    ("gc", 0, 2), ("gl", 3, 0), ("gx", 0, 2), ("gx", 1, 2), ("gc", 3, 2), ("gl", 10, 2), ("gl", 10, 3),
    ("gsh", 10, 1), ("gbegin", 5), ("gc", 2, 2), ("gx", 3, 2), ("gbegin", 4), ("gx", 2, 2), ("gd", 10), ("vectors",),
    ("gl", 1, 1), ("gl", 0, 1), ("gx", 0, 3), ("gx", 1, 3), ("zx", 6), ("gsh", 1, 0), ("gsh", 0, 0), ("gc", 5, 0),
    ("gl", 2, 1), ("ln1",), ("gl", 0, 2), ("gl", 1, 2), ("gl", 0, 3), ("gsh", 0, 1), ("gl", 3, 1), ("gl", 1, 3),
    ("gc", 4, 0), ("gsh", 1, 1), ("gbegin", 9), ("gbegin", 8), ("gx", 2, 3), ("gx", 5, 0), ("gx", 3, 3),
    ("gsh", 2, 0), ("gsh", 3, 0), ("gx", 4, 0), ("zy", 6), ("gd", 0), ("gbegin", 7), ("gc", 5, 1), ("gd", 1),
    ("p0",), ("gl", 2, 2), ("gx", 5, 1), ("p1",), ("gc", 4, 1), ("gl", 3, 2), ("gx", 4, 1), ("p2",), ("zc", 6, 0),
    ("at00",), ("gl", 5, 0), ("at01",), ("gl", 4, 0), ("gc", 4, 2), ("at02",), ("gc", 8, 0), ("gc", 5, 2), ("at10",),
    ("at11",), ("gx", 8, 0), ("zc", 6, 1), ("at12",), ("zx", 9), ("gl", 2, 3), ("gx", 5, 2), ("at20",), ("gl", 3, 3),
    ("gsh", 2, 1), ("gsh", 3, 1), ("gx", 4, 2), ("at21",), ("gl", 4, 1), ("gl", 5, 1), ("gx", 5, 3), ("gc", 8, 1),
    ("gsh", 5, 0), ("at22",), ("zc", 6, 2), ("gx", 4, 3), ("gd", 2), ("gsh", 4, 0), ("gc", 7, 0), ("gsh", 6, 0),
    ("at30",), ("gsh", 6, 1), ("zy", 9), ("gx", 7, 0), ("gl", 5, 2), ("gx", 8, 1), ("gl", 8, 0), ("at31",),
    ("gl", 5, 3), ("gsh", 5, 1), ("gd", 3), ("at32",), ("gl", 4, 2), ("gc", 8, 2), ("gl", 4, 3), ("gsh", 4, 1),
    ("gc", 7, 1), ("gx", 8, 2), ("gd", 6), ("norm2",), ("gl", 8, 1), ("gx", 7, 1), ("gd", 4), ("zc", 9, 0),
    ("gl", 7, 0), ("gd", 5), ("h0",), ("rc", 0), ("gc", 7, 2), ("gx", 7, 2), ("rc", 1), ("h1",), ("rc", 3),
    ("re", 1, 0), ("gl", 7, 1), ("gx", 8, 3), ("rc", 2), ("gsh", 8, 0), ("zc", 9, 1), ("re", 0, 0), ("gx", 7, 3),
    ("gl", 8, 2), ("gsh", 7, 0), ("h2",), ("re", 2, 0), ("re", 3, 0), ("gl", 8, 3), ("gsh", 8, 1), ("h3",),
    ("zc", 9, 2), ("gl", 7, 2), ("gsh", 9, 0), ("re", 0, 1), ("gl", 7, 3), ("re", 1, 1), ("gsh", 7, 1),
    ("gsh", 9, 1), ("re", 2, 1), ("re", 3, 1), ("gd", 9), ("gd", 8), ("gd", 7), ("last",), ("re", 1, 2),
    ("re", 2, 2), ("re", 0, 2), ("re", 3, 2),
)
BACKWARD_PLAN = (
    ("start",), ("core", 8), ("core", 9), ("hb0",), ("hb1",), ("e", 8, 0), ("core", 6), ("e", 9, 0), ("hb2",),
    ("hb3",), ("core", 7), ("e", 6, 0), ("mp0",), ("e", 8, 1), ("e", 7, 0), ("mp1",), ("og",), ("e", 9, 1), ("tc",),
    ("at00",), ("e", 8, 2), ("at01",), ("at02",), ("core", 5), ("core", 4), ("zs", 8), ("at10",), ("at11",),
    ("at12",), ("e", 9, 2), ("at20",), ("e", 5, 0), ("zs", 9), ("at21",), ("e", 7, 1), ("e", 4, 0), ("at22",),
    ("e", 6, 1), ("at30",), ("at31",), ("at32",), ("gq0",), ("core", 0), ("gq1",), ("core", 1), ("e", 5, 1),
    ("e", 7, 2), ("zs", 7), ("gq2",), ("e", 0, 0), ("core", 2), ("e", 1, 0), ("gq3",), ("bias",), ("e", 6, 2),
    ("core", 3), ("zs", 6), ("e", 2, 0), ("e", 4, 1), ("ip0",), ("ip1",), ("e", 3, 0), ("e", 5, 2), ("e", 1, 1),
    ("cut",), ("core", 10), ("zs", 5), ("e", 4, 2), ("res", 7, 0), ("e", 0, 1), ("e", 2, 1), ("zs", 4), ("e", 10, 0),
    ("e", 1, 2), ("zs", 1), ("e", 3, 1), ("e", 10, 1), ("e", 0, 2), ("zs", 0), ("e", 3, 2), ("e", 2, 2), ("zs", 3),
    ("e", 10, 2), ("res", 6, 0), ("zs", 10), ("res", 8, 0), ("zs", 2), ("res", 3, 0), ("res", 10, 0), ("res", 1, 0),
    ("res", 5, 0), ("res", 9, 0), ("res", 4, 0), ("res", 0, 0), ("res", 2, 0),
)
GATHER_IN = ("tokens", "cotangent", "mask", "counts", "w0", "w1", "w2", "w3", "w4")
KEPT = ("x", "g", "h1", "qkv", "probs", "context", "middle", "h2", "slope", "gd", "full0", "full1", "full2", "full3", "early")
FORWARD_SCRATCH = KEPT + (
    "full4", "first_sums", "pair_sums", "sum_send", "sum_recv", "pair", "act", "ub", "chain_sem", "send_sem", "recv_sem", "share_send", "share_recv",
    "keep_sem", "save_sem", "load_sem", "back_sem",
)


def forward_kernel(chain, parts, *refs):
    n_in = len(GATHER_IN)
    r = unpack(GATHER_IN, refs[:n_in])
    saved = unpack(KEPT, refs[n_in : n_in + len(KEPT)])
    packed, vec, target = refs[n_in + len(KEPT) : n_in + len(KEPT) + 3]
    s = unpack(FORWARD_SCRATCH, refs[n_in + len(KEPT) + 3 :])
    model = s.x.shape[1]
    slots, _, both = target.shape
    slot_rows = s.x.shape[0] // slots
    total = s.x.shape[0]
    patches = both // 2
    place = Place(chain)
    mine = place.shard()
    own = (r.w0, r.w1, r.w2, r.w3, r.w4)
    devices = 8 * chain
    share = model // devices
    hidden = s.act.shape[1]
    up_share = hidden // devices
    per_row = model // up_share
    samples = 2 * slots
    first_sample = (lax.axis_index("gx") * slots + lax.axis_index("gy")) * samples
    full = (s.full0, s.full1, s.full2, s.full3, s.full4)
    saves = []

    def save(name, where=Ellipsis):
        copy = pltpu.make_async_copy(
            getattr(s, name).at[where], getattr(saved, name).at[where], s.save_sem.at[len(saves)]
        )
        copy.start()
        saves.append(copy)

    loads = [
        pltpu.make_async_copy(
            r.tokens.at[pl.ds(half * slots, slots)],
            s.pair.at[:, pl.ds(half * patches, patches)],
            s.load_sem.at[half],
        )
        for half in range(2)
    ]
    grad_loads = [
        pltpu.make_async_copy(
            r.cotangent.at[half * slots + slot],
            s.act.at[pl.ds(half * patches, patches), pl.ds(slot * model, model)],
            s.load_sem.at[2 + half * slots + slot],
        )
        for half in range(2)
        for slot in range(slots)
    ]
    for copy in loads + grad_loads:
        copy.start()
    shape = (samples, patches)
    at_sample = lax.broadcasted_iota(jnp.int32, shape, 0)
    limit = jnp.zeros(shape, jnp.int32)
    offset = jnp.zeros(shape, jnp.int32)
    for sample in range(samples):
        limit = jnp.where(at_sample == sample, r.counts[first_sample + sample], limit)
        if sample >= slots:
            offset = jnp.where(at_sample == sample, r.counts[first_sample + sample - slots], offset)
    square = (patches, patches)
    upper = lax.broadcasted_iota(jnp.int32, square, 0) <= lax.broadcasted_iota(jnp.int32, square, 1)
    land = r.mask[...] == 1
    rank = dot(jnp.where(land, 1.0, 0.0).astype(jnp.bfloat16), jnp.where(upper, 1.0, 0.0).astype(jnp.bfloat16))
    rank = rank.astype(jnp.int32) - 1
    places = jnp.where(land & (rank < limit), rank + offset, -1)
    for slot in range(slots):
        target[slot] = jnp.concatenate([places[slot : slot + 1], places[slots + slot : slots + slot + 1]], axis=1)
    engine = Gather(
        place, parts, own, full, (s.chain_sem, s.send_sem, s.recv_sem, s.share_send, s.share_recv)
    )
    keeps = [pltpu.make_async_copy(own[at], full[at].at[mine], s.keep_sem.at[at]) for at in range(5)]
    for keep in keeps:
        keep.start()
    place.greet()

    def rows_of(slot):
        return pl.ds(slot * slot_rows, slot_rows)

    def pack_inputs():
        for copy in loads + keeps:
            copy.wait()
        for slot in range(slots):
            s.x[rows_of(slot), :] = dot(
                pick_matrix(target[slot], slot_rows), s.pair[slot]
            ).astype(jnp.bfloat16)
        save("x")

    def pack_grads():
        for copy in grad_loads:
            copy.wait()
        for slot in range(slots):
            patch_grads = s.act[pl.ds(0, both), pl.ds(slot * model, model)]
            s.g[rows_of(slot), :] = dot(
                pick_matrix(target[slot], slot_rows), patch_grads
            ).astype(jnp.bfloat16)
        save("g")

    def done(part):
        engine.finish(part)
        at, first, width, _ = parts[part]
        if at != VEC:
            save("full%d" % at, (Ellipsis, pl.ds(first, width)))

    def place_vector(at, carry):
        rows, up_rows = carry
        piece = s.full4[at // 8, at // 4 % 2, at // 2 % 2, at % 2].astype(jnp.float32)
        wide = jnp.concatenate([piece, jnp.zeros((16, model - 128), jnp.float32)], axis=1)
        rows = rows + pltpu.roll(wide[:8], at * share, 1)
        moved = pltpu.roll(wide[8:], (at % per_row) * up_share, 1)
        here = lax.broadcasted_iota(jnp.int32, (8, model), 0) == at // per_row
        up_rows = up_rows + jnp.where(here, jnp.broadcast_to(moved[:1], (8, model)), 0.0)
        return rows, up_rows

    up_turns = hidden // model

    def place_vectors():
        zeros = jnp.zeros((8, model), jnp.float32)
        rows, up_rows = lax.fori_loop(0, devices, place_vector, (zeros, zeros))
        vec[...] = rows
        for at in range(up_turns):
            s.ub[at] = up_rows[at : at + 1]

    def norm_one(slot, carry):
        at = rows_of(slot)
        n, _ = normalised(s.x[at, :].astype(jnp.float32))
        s.h1[at, :] = (n * vec[0:1] + vec[1:2]).astype(jnp.bfloat16)
        return carry

    def norm_ones():
        lax.fori_loop(0, slots, norm_one, 0)
        save("h1")

    def project(section):
        bias = vec[2:3] if section == 0 else vec[3:4]
        columns = pl.ds(section * model, model)
        weight = s.full0[:, :, :, :, :, columns].reshape(model, model)

        def chunk(at, carry):
            here = pl.ds(at * (total // 2), total // 2)
            value = dot(s.h1[here, :], weight)
            if section != 1:
                value = value + bias
            value = value.astype(jnp.bfloat16)
            if section == 0:
                value = value * jnp.bfloat16(HD**-0.5)
            s.qkv[section, here, :] = value
            return carry

        lax.fori_loop(0, 2, chunk, 0)
        save("qkv", section)

    low_lane = lax.broadcasted_iota(jnp.int32, (slot_rows, 2 * HD), 1) < HD
    none = jnp.zeros((slot_rows, 2 * HD), jnp.bfloat16)

    def attend(slot, turn):
        one = r.counts[first_sample + slot]
        two = one + r.counts[first_sample + slot + slots]
        shape = (slot_rows, slot_rows)
        at_row = lax.broadcasted_iota(jnp.int32, shape, 0)
        at_column = lax.broadcasted_iota(jnp.int32, shape, 1)
        same = ((at_row >= one).astype(jnp.int32) + (at_row >= two).astype(jnp.int32)) == (
            (at_column >= one).astype(jnp.int32) + (at_column >= two).astype(jnp.int32)
        )
        bias = jnp.where(same, 0.0, -1000000000.0)

        for inner in range(2):
            pair = turn * 2 + inner
            columns = pl.ds(pair * 2 * HD, 2 * HD)
            query = s.qkv[0, rows_of(slot), columns]
            key = s.qkv[1, rows_of(slot), columns]
            value = s.qkv[2, rows_of(slot), columns]
            context = None
            for head in range(2):
                mask = low_lane if head == 0 else ~low_lane
                scores = dot(jnp.where(mask, query, none), key, 1, 1) + bias
                expo = jnp.exp(scores - jnp.max(scores, axis=-1, keepdims=True))
                probs = (expo / jnp.sum(expo, axis=-1, keepdims=True)).astype(jnp.bfloat16)
                s.probs[slot * HEADS + pair * 2 + head] = probs
                term = dot(probs, jnp.where(mask, value, none))
                context = term if context is None else context + term
            s.context[rows_of(slot), columns] = context.astype(jnp.bfloat16)

    def norm_two(slot, carry):
        at = rows_of(slot)
        weight = s.full1[...].reshape(model, model)
        middle = s.x[at, :].astype(jnp.float32) + dot(s.context[at, :], weight) + vec[4:5]
        s.middle[at, :] = middle
        n, _ = normalised(middle)
        s.h2[at, :] = (n * vec[5:6] + vec[6:7]).astype(jnp.bfloat16)
        return carry

    def norm_twos():
        save("probs")
        save("context")
        lax.fori_loop(0, slots, norm_two, 0)
        save("middle")
        save("h2")

    down_rows = s.gd.shape[4]
    block_rows = chain // (hidden // model)
    early_parts = [
        part[:4] + (block * block_rows, block_rows)
        for block in range(hidden // model - 1)
        for part in halves([item.shape[-1] for item in full])
        if part[0] == DOWN
    ][: 2 * EARLY_BLOCKS]
    adder = Scatter(
        place,
        early_parts,
        {DOWN: s.gd},
        {DOWN: None},
        {DOWN: (s.first_sums, s.pair_sums, s.early)},
        (s.sum_send, s.sum_recv, None, None),
    )

    def hidden_block(block):
        for half in range(PIECES):
            first_column = block * model + half * (model // PIECES)
            columns = pl.ds(first_column, model // PIECES)
            weight = s.full2[:, :, :, :, :, columns].reshape(model, model // PIECES)
            bias = s.ub[block][:, half * (model // PIECES) : (half + 1) * (model // PIECES)]

            def chunk(slot, carry, columns=columns, weight=weight, bias=bias):
                at = rows_of(slot)
                value = dot(s.h2[at, :], weight) + bias
                share_of = 0.5 + 0.5 * lax.erf(value * 0.7071067811865476)
                s.act[at, columns] = (value * share_of).astype(jnp.bfloat16)
                slope = share_of + value * jnp.exp(-0.5 * value * value) * 0.3989422804014327
                s.slope[at, columns] = slope.astype(jnp.bfloat16)
                return carry

            lax.fori_loop(0, slots, chunk, 0)
            grad = dot(s.act[:, columns], s.g[...], 0, 0).astype(jnp.bfloat16)
            for at in range(model // PIECES // down_rows):
                to = first_column // down_rows + at
                s.gd[to // 8, to // 4 % 2, to // 2 % 2, to % 2] = grad[at * down_rows : (at + 1) * down_rows]
        save("slope", (slice(None), pl.ds(block * model, model)))
        if block >= EARLY_BLOCKS:
            save("gd", pl.ds(block * block_rows, block_rows))


    def last(slot):
        at = rows_of(slot)
        weight = s.full3[...].reshape(hidden, model)
        value = s.middle[at, :] + dot(s.act[at, :], weight) + vec[7:8]
        s.pair[slot, pl.ds(0, slot_rows), :] = value.astype(jnp.bfloat16)

    def lasts():
        for slot in range(slots):
            last(slot)
            copy = pltpu.make_async_copy(s.pair.at[slot, pl.ds(0, slot_rows)], packed.at[slot], s.back_sem.at[slot])
            copy.start()
            saves.append(copy)

    def early_core(part):
        adder.core(part).start()

    def early_up(part, level):
        adder.up_one(part, level)
        if level == 2:
            _, first, width, _, low, rows = early_parts[part]
            save("early", (pl.ds(low, rows), slice(None), pl.ds(first, width)))

    def share_out(part, half):
        engine.sharing(part, half).start()

    call = functools.partial
    steps = {"packx": pack_inputs, "packg": pack_grads, "vectors": place_vectors, "ln1": norm_ones}
    steps |= {"norm2": norm_twos, "last": lasts}
    for section in range(3):
        steps["p%d" % section] = call(project, section)
    for block in range(up_turns):
        steps["h%d" % block] = call(hidden_block, block)
    for slot in range(slots):
        for turn in range(HEADS // 4):
            steps["at%d%d" % (slot, turn)] = call(attend, slot, turn)
    moves = {"gbegin": engine.begin, "gc": engine.along, "gx": engine.across, "gl": engine.last}
    moves |= {"gsh": share_out, "gd": done, "rc": early_core, "re": early_up}
    moves |= {"zx": engine.cross_first, "zy": engine.cross_second, "zc": engine.along_last}
    follow(FORWARD_PLAN, steps, moves)
    for part in range(len(early_parts)):
        adder.finish_pairs(part)
    for copy in saves:
        copy.wait()


def any_spec():
    return pl.BlockSpec(memory_space=pl.ANY)


def vmem_spec():
    return pl.BlockSpec(memory_space=pltpu.VMEM)


def run_forward(chain, slots, tokens, cotangent, mask, counts, shards):
    devices = 8 * chain
    samples, patches, model = tokens.shape
    total = samples * patches * 3 // 4
    slot_rows = total // slots
    hidden = shards[UP].shape[1]
    parts = gather_parts([item.shape[1] for item in shards])
    down = shards[DOWN].shape
    early_count = 2 * EARLY_BLOCKS
    low = jnp.bfloat16
    kept = [
        ((total, model), low),
        ((total, model), low),
        ((total, model), low),
        ((3, total, model), low),
        ((slots * HEADS, slot_rows, slot_rows), low),
        ((total, model), low),
        ((total, model), jnp.float32),
        ((total, model), low),
        ((total, hidden), low),
        ((chain, 2, 2, 2) + down, low),
    ] + [((chain, 2, 2, 2) + item.shape, low) for item in shards[:4]]
    kept.append(((chain,) + down, low))
    outs = kept + [
        ((slots, slot_rows, model), low),
        ((8, model), jnp.float32),
        ((slots, 1, 2 * patches), jnp.int32),
    ]
    scratch = [pltpu.VMEM(*item) for item in kept] + [
        pltpu.VMEM((chain, 2, 2, 2) + shards[VEC].shape, low),
        pltpu.VMEM((chain, 2, 2) + down, low),
        pltpu.VMEM((chain, 2) + down, low),
        pltpu.SemaphoreType.DMA((early_count, 3)),
        pltpu.SemaphoreType.DMA((early_count, 3)),
        pltpu.VMEM((slots, 2 * patches, model), low),
        pltpu.VMEM((total, hidden), low),
        pltpu.VMEM((hidden // model, 1, model), jnp.float32),
        pltpu.SemaphoreType.DMA((len(parts), 2, chain, 4)),
        pltpu.SemaphoreType.DMA((len(parts), 2)),
        pltpu.SemaphoreType.DMA((len(parts), devices)),
        pltpu.SemaphoreType.DMA((len(parts), 2)),
        pltpu.SemaphoreType.DMA((len(parts), 2)),
        pltpu.SemaphoreType.DMA((5,)),
        pltpu.SemaphoreType.DMA((len(KEPT) + 32,)),
        pltpu.SemaphoreType.DMA((2 + 2 * slots,)),
        pltpu.SemaphoreType.DMA((slots,)),
    ]
    return pl.pallas_call(
        functools.partial(forward_kernel, chain, parts),
        out_shape=[jax.ShapeDtypeStruct(*item) for item in outs],
        in_specs=[any_spec(), any_spec(), vmem_spec(), pl.BlockSpec(memory_space=pltpu.SMEM)]
        + [any_spec()] * 4
        + [vmem_spec()],
        out_specs=[any_spec()] * (len(outs) - 2) + [vmem_spec()] * 2,
        scratch_shapes=scratch,
        compiler_params=pltpu.CompilerParams(
            collective_id=0, has_side_effects=True, vmem_limit_bytes=60 * 2**20
        ),
        name="forward",
    )(tokens, cotangent, mask, counts, *shards)


BACKWARD_IN = ("g", "slope", "w_down", "h2", "gd", "w_up", "middle", "context", "w_out", "qkv", "probs", "h1", "x", "w_qkv", "early", "vec")
BACKWARD_OUT = ("sum0", "sum1", "sum2", "sum3", "sum4", "packed")
BACKWARD_SCRATCH = (
    "g", "slope", "w_down", "h2", "gd", "w_up", "middle", "context", "w_out", "probs",
    "vg", "ug", "t0", "t1", "t2", "t4",
)
LOADS = ("g", "h2", "gd", "d0", "d1", "d2", "d3", "s0", "s1", "s2", "s3", "w_up", "middle", "context", "w_out", "probs", "w_qkv", "qkv0", "qkv1", "qkv2", "x", "h1", "early")


def backward_kernel(chain, parts, *refs):
    n_in, n_out, n_s = len(BACKWARD_IN), len(BACKWARD_OUT), len(BACKWARD_SCRATCH)
    r = unpack(BACKWARD_IN, refs[:n_in])
    o = unpack(BACKWARD_OUT, refs[n_in : n_in + n_out])
    at = n_in + n_out
    s = unpack(BACKWARD_SCRATCH, refs[at : at + n_s])
    buffers = refs[at + n_s : at + n_s + 20]
    load_sem, back_sem, *sems = refs[at + n_s + 20 :]
    got = [buffers[4 * k : 4 * k + 4] for k in range(5)]
    total, model = s.g.shape
    hidden = s.slope.shape[1]
    slots = lax.axis_size("gy")
    slot_rows = total // slots
    place = Place(chain)
    loads = {}

    def fetch(name, source, into):
        loads[name] = pltpu.make_async_copy(source, into, load_sem.at[LOADS.index(name)])
        loads[name].start()

    def need(*names):
        for name in names:
            loads[name].wait()

    done_rows = chain - s.gd.shape[0]
    fetch("g", r.g, s.g)
    for block in range(hidden // model):
        lanes = pl.ds(block * model, model)
        fetch("d%d" % block, r.w_down.at[lanes], s.w_down.at[lanes])
        fetch("s%d" % block, r.slope.at[:, lanes], s.slope.at[:, lanes])
        if block == 0:
            fetch("h2", r.h2, s.h2)
            fetch("gd", r.gd.at[pl.ds(done_rows, chain - done_rows), :, :, place.d], s.gd)
    for name in ("w_up", "middle", "context", "w_out", "probs"):
        fetch(name, getattr(r, name), getattr(s, name))
    fetch("early", r.early.at[pl.ds(0, done_rows)], got[DOWN][2].at[pl.ds(0, done_rows)])
    place.greet(far=True)
    engine = Scatter(
        place, parts, (s.t0, s.t1, s.t2, r.gd, s.t4), (None, None, None, s.gd, None), got, sems
    )
    groups = [[k for k, part in enumerate(parts) if part[0] == name] for name in range(5)]
    outs = (o.sum0, o.sum1, o.sum2, o.sum3, o.sum4)

    def rows_of(slot):
        return pl.ds(slot * slot_rows, slot_rows)

    def shards_of(value, like):
        return value.reshape(like.shape[:5] + (value.shape[-1],)).astype(jnp.bfloat16)

    def first_sums():
        need("g", "h2")
        s.vg[...] = jnp.zeros_like(s.vg)
        s.ug[...] = jnp.zeros_like(s.ug)
        s.vg[7:8] = column_sum(s.g[...].astype(jnp.float32))

    def hidden_block(block):
        need("d%d" % block, "s%d" % block)
        for half in range(PIECES):
            first_column = block * model + half * (model // PIECES)
            columns = pl.ds(first_column, model // PIECES)
            weight = s.w_down[pl.ds(first_column, model // PIECES), :]

            def chunk(slot, carry, columns=columns, weight=weight):
                here = rows_of(slot)
                value = dot(s.g[here, :], weight, 1, 1) * s.slope[here, columns].astype(jnp.float32)
                value = value.astype(jnp.bfloat16)
                s.slope[here, columns] = value
                return carry + column_sum(value.astype(jnp.float32))

            sums = lax.fori_loop(0, slots, chunk, jnp.zeros((1, model // PIECES), jnp.float32))
            s.ug[block : block + 1, half * (model // PIECES) : (half + 1) * (model // PIECES)] = sums
            s.t2[:, :, :, :, :, columns] = shards_of(dot(s.h2[...], s.slope[:, columns], 0, 0), s.t2)

    def fetch_more():
        for section in range(3):
            fetch("qkv%d" % section, r.qkv.at[section], s.w_down.at[pl.ds(section * model, model)])
        fetch("x", r.x, s.w_down.at[pl.ds(3 * model, model)])
        need("w_up", "middle")

    half_rows = total // 2

    def middle_part(half):
        if half == 0:
            fetch_more()
        grad = dot(s.slope[pl.ds(half * half_rows, half_rows), :], s.w_up[...], 1, 1)
        for inner in range(slots // 2):
            here = rows_of(half * (slots // 2) + inner)
            part = grad[inner * slot_rows : (inner + 1) * slot_rows]
            n, rate = normalised(s.middle[here, :])
            s.vg[5:6] += column_sum(part * n)
            s.vg[6:7] += column_sum(part)
            scaled = part * r.vec[5:6]
            mean_one = jnp.mean(scaled, axis=-1, keepdims=True)
            mean_two = jnp.mean(scaled * n, axis=-1, keepdims=True)
            full_grad = s.g[here, :].astype(jnp.float32) + rate * (scaled - mean_one - n * mean_two)
            s.middle[here, :] = full_grad
            branch = full_grad.astype(jnp.bfloat16)
            s.h2[here, :] = branch
            s.vg[4:5] += column_sum(branch.astype(jnp.float32))

    joined = pl.ds(0, 3 * model)

    def out_grads():
        fetch("w_qkv", r.w_qkv, s.w_up.at[:, joined])
        fetch("h1", r.h1, s.slope.at[:, pl.ds(3 * model, model)])
        need("context", "w_out")
        s.t1[...] = shards_of(dot(s.context[...], s.h2[...], 0, 0), s.t1)

    def to_context(slot, carry):
        here = rows_of(slot)
        s.context[here, :] = dot(s.h2[here, :], s.w_out[...], 1, 1).astype(jnp.bfloat16)
        return carry

    def to_contexts():
        lax.fori_loop(0, slots, to_context, 0)
        need("qkv0", "qkv1", "qkv2", "probs")

    low_lane = lax.broadcasted_iota(jnp.int32, (slot_rows, 2 * HD), 1) < HD
    none = jnp.zeros((slot_rows, 2 * HD), jnp.bfloat16)

    def attend(slot, turn):
        for inner in range(2):
            pair = turn * 2 + inner
            first_column = pair * 2 * HD
            columns = pl.ds(first_column, 2 * HD)
            query = s.w_down[pl.ds(slot * slot_rows, slot_rows), columns]
            key = s.w_down[pl.ds(model + slot * slot_rows, slot_rows), columns]
            value = s.w_down[pl.ds(2 * model + slot * slot_rows, slot_rows), columns]
            grad = s.context[rows_of(slot), columns]
            totals = [None, None, None]
            for head in range(2):
                mask = low_lane if head == 0 else ~low_lane
                grad_here = jnp.where(mask, grad, none)
                low_probs = s.probs[slot * HEADS + pair * 2 + head]
                probs = low_probs.astype(jnp.float32)
                weighted = probs * dot(grad_here, value, 1, 1)
                share = jnp.sum(weighted, axis=-1, keepdims=True)
                scores = (weighted - probs * share).astype(jnp.bfloat16)
                terms = (
                    dot(scores, jnp.where(mask, key, none)),
                    dot(scores, jnp.where(mask, query, none), 0, 0),
                    dot(low_probs, grad_here, 0, 0),
                )
                totals = [b if a is None else a + b for a, b in zip(totals, terms)]
            totals[0] = totals[0] * HD**-0.5
            for section in range(3):
                s.slope[rows_of(slot), pl.ds(section * model + first_column, 2 * HD)] = totals[
                    section
                ].astype(jnp.bfloat16)

    h1 = pl.ds(3 * model, model)

    def qkv_grads(turn):
        if turn == 0:
            need("h1", "w_qkv", "x")
        _, first, width, *_ = parts[groups[QKV][turn]]
        columns = pl.ds(first, width)
        s.t0[:, :, :, :, :, columns] = shards_of(dot(s.slope[:, h1], s.slope[:, columns], 0, 0), s.t0)

    def bias_sums():
        s.vg[2:3] = column_sum(s.slope[:, pl.ds(0, model)].astype(jnp.float32))
        s.vg[3:4] = column_sum(s.slope[:, pl.ds(2 * model, model)].astype(jnp.float32))

    def input_part(half):
        grad = dot(s.slope[pl.ds(half * half_rows, half_rows), joined], s.w_up[:, joined], 1, 1)
        for inner in range(slots // 2):
            slot = half * (slots // 2) + inner
            here = rows_of(slot)
            part = grad[inner * slot_rows : (inner + 1) * slot_rows]
            n, rate = normalised(
                s.w_down[pl.ds(3 * model + slot * slot_rows, slot_rows), :].astype(jnp.float32)
            )
            s.vg[0:1] += column_sum(part * n)
            s.vg[1:2] += column_sum(part)
            scaled = part * r.vec[0:1]
            mean_one = jnp.mean(scaled, axis=-1, keepdims=True)
            mean_two = jnp.mean(scaled * n, axis=-1, keepdims=True)
            full_grad = s.middle[here, :] + rate * (scaled - mean_one - n * mean_two)
            s.g[here, :] = full_grad.astype(jnp.bfloat16)
        here = pl.ds(half * half_rows, half_rows)
        backs.append(pltpu.make_async_copy(s.g.at[here], o.packed.at[here], back_sem.at[half]))
        backs[-1].start()

    backs = []
    devices = 8 * chain
    share = model // devices
    up_share = hidden // devices
    per_row = model // up_share

    def cut_vector(index, carry):
        rows = pltpu.roll(s.vg[...], model - index * share, 1)[:, :128]
        here = lax.broadcasted_iota(jnp.int32, (8, model), 0) == index // per_row
        row = jnp.broadcast_to(column_sum(jnp.where(here, s.ug[...], 0.0)), (8, model))
        up_rows = pltpu.roll(row, model - (index % per_row) * up_share, 1)[:, :128]
        s.t4[index // 8, index // 4 % 2, index // 2 % 2, index % 2] = jnp.concatenate([rows, up_rows], axis=0)
        return carry

    def cut_vectors():
        lax.fori_loop(0, devices, cut_vector, 0)

    def core(part):
        engine.core(part).start()

    unread = (["gd"], ["early"])

    def add_up(part, level):
        if part in groups[DOWN] and unread[0]:
            need(unread[0].pop())
        engine.up_one(part, level)

    def along(part):
        if part in groups[DOWN] and unread[1]:
            need(unread[1].pop())
        engine.along(part)

    def result(part, _):
        engine.result(part, outs)

    call = functools.partial
    steps = {"start": first_sums, "og": out_grads, "tc": to_contexts, "bias": bias_sums, "cut": cut_vectors}
    for half in range(2):
        steps["mp%d" % half] = call(middle_part, half)
        steps["ip%d" % half] = call(input_part, half)
    for turn in range(4):
        steps["gq%d" % turn] = call(qkv_grads, turn)
    for block in range(hidden // model):
        steps["hb%d" % block] = call(hidden_block, block)
    for slot in range(slots):
        for turn in range(HEADS // 4):
            steps["at%d%d" % (slot, turn)] = call(attend, slot, turn)
    moves = {"core": core, "e": add_up, "zs": along, "res": result}
    follow(BACKWARD_PLAN, steps, moves)
    for part in range(len(parts)):
        engine.finish(part)
    for copy in backs:
        copy.wait()


def run_backward(chain, kept, vec, shards):
    total, model = kept.x.shape
    hidden = shards[UP].shape[1]
    last_rows = chain - chain // (hidden // model) * EARLY_BLOCKS
    parts = [
        part + ((chain - last_rows, last_rows) if part[0] == DOWN else (0, chain))
        for part in scatter_parts([item.shape[1] for item in shards])
    ]
    low, wide = jnp.bfloat16, jnp.float32
    lead = (chain, 2, 2, 2)
    fulls = [
        item.reshape(-1, item.shape[-1]) for item in (kept.full0, kept.full1, kept.full2, kept.full3)
    ]
    given = types.SimpleNamespace(
        g=kept.g, slope=kept.slope, w_down=fulls[DOWN], h2=kept.h2,
        gd=kept.gd, w_up=fulls[UP], middle=kept.middle,
        context=kept.context, w_out=fulls[OUT], qkv=kept.qkv, probs=kept.probs, h1=kept.h1, x=kept.x,
        w_qkv=fulls[QKV], early=kept.early, vec=vec,
    )
    scratch = {name: pltpu.VMEM(getattr(given, name).shape, getattr(given, name).dtype) for name in BACKWARD_IN}
    scratch["gd"] = pltpu.VMEM((last_rows, 2, 2) + shards[DOWN].shape, low)
    scratch["vg"] = pltpu.VMEM((8, model), wide)
    scratch["ug"] = pltpu.VMEM((8, model), wide)
    for at in (QKV, OUT, UP, VEC):
        scratch["t%d" % at] = pltpu.VMEM(lead + shards[at].shape, wide if at == VEC else low)
    arrivals = []
    for at, item in enumerate(shards):
        for front in ((chain, 2, 2), (chain, 2), (chain,), (chain,)):
            arrivals.append(pltpu.VMEM(front + item.shape, wide if at == VEC else low))
    outs = [(item.shape, wide) for item in shards] + [((total, model), low)]
    return pl.pallas_call(
        functools.partial(backward_kernel, chain, parts),
        out_shape=[jax.ShapeDtypeStruct(*item) for item in outs],
        in_specs=[any_spec()] * (len(BACKWARD_IN) - 1) + [vmem_spec()],
        out_specs=[vmem_spec()] * 5 + [any_spec()],
        scratch_shapes=[scratch[name] for name in BACKWARD_SCRATCH]
        + arrivals
        + [
            pltpu.SemaphoreType.DMA((len(LOADS),)),
            pltpu.SemaphoreType.DMA((2,)),
            pltpu.SemaphoreType.DMA((len(parts), 3)),
            pltpu.SemaphoreType.DMA((len(parts), 3)),
            pltpu.SemaphoreType.DMA((len(parts), chain)),
            pltpu.SemaphoreType.DMA((len(parts), chain)),
        ],
        compiler_params=pltpu.CompilerParams(
            collective_id=1, has_side_effects=True, vmem_limit_bytes=63 * 2**20
        ),
        name="backward",
    )(*[getattr(given, name) for name in BACKWARD_IN])


def spread_kernel(target, rows, grads, *refs):
    sums, out_tokens, grad_tokens, outs = refs[:5], refs[5], refs[6], refs[7:]
    slot_rows = rows.shape[1]
    patches = out_tokens.shape[2]
    matrix = pick_matrix(target[0], slot_rows)
    for source, to in ((rows, out_tokens), (grads, grad_tokens)):
        spread = dot(matrix, source[0], 0, 0).astype(jnp.bfloat16)
        for half in range(2):
            to[half, 0] = spread[half * patches : (half + 1) * patches]

    @pl.when(pl.program_id(0) == 0)
    def _():
        for at in range(4):
            outs[at][...] = sums[at][...]
        table = sums[VEC]
        share = outs[4].shape[1]
        outs[6][...] = table[2:4, :share]
        for ref, row in zip((outs[4], outs[5]) + outs[7:], (0, 1, 4, 5, 6, 7, 8)):
            ref[...] = table[row : row + 1, : ref.shape[1]]


def run_spread(target, rows, grads, sums, share, up_share):
    slots, slot_rows, model = rows.shape
    patches = target.shape[2] // 2
    wide = jnp.float32

    def whole(shape):
        return pl.BlockSpec(shape, lambda i: (0,) * len(shape))

    tokens_spec = pl.BlockSpec((2, 1, patches, model), lambda i: (0, i, 0, 0))
    slot_spec = pl.BlockSpec((1, slot_rows, model), lambda i: (i, 0, 0))
    shapes = [item.shape for item in sums[:4]]
    shapes += [(1, share), (1, share), (2, share)] + [(1, share)] * 4 + [(1, up_share)]
    tokens_shape = jax.ShapeDtypeStruct((2, slots, patches, model), jnp.bfloat16)
    return pl.pallas_call(
        spread_kernel,
        grid=(slots,),
        out_shape=[tokens_shape] * 2 + [jax.ShapeDtypeStruct(shape, wide) for shape in shapes],
        in_specs=[pl.BlockSpec((1, 1, 2 * patches), lambda i: (i, 0, 0)), slot_spec, slot_spec]
        + [whole(item.shape) for item in sums],
        out_specs=[tokens_spec] * 2 + [whole(shape) for shape in shapes],
        compiler_params=pltpu.CompilerParams(vmem_limit_bytes=60 * 2**20),
        name="spread",
    )(target, rows, grads, *sums)


def per_device(
    tokens,
    land_mask,
    counts,
    ln1_gain,
    ln1_shift,
    qkv_weight,
    qv_bias,
    out_weight,
    out_bias,
    ln2_gain,
    ln2_shift,
    up_weight,
    up_bias,
    down_weight,
    down_bias,
    cotangent,
):
    chain = lax.axis_size("gx") // 2
    slots = lax.axis_size("gy")
    share, up_share = ln1_gain.shape[0], up_bias.shape[0]
    small = [ln1_gain, ln1_shift, qv_bias[0], qv_bias[1], out_bias, ln2_gain, ln2_shift, down_bias, up_bias]
    table = sum(
        jnp.pad(item[None], ((at, 15 - at), (0, 128 - item.shape[0]))) for at, item in enumerate(small)
    )
    shards = [qkv_weight, out_weight, up_weight, down_weight, table]
    *kept, packed, vec, target = run_forward(
        chain, slots, tokens, cotangent, land_mask, counts, shards
    )
    *sums, packed_grads = run_backward(chain, unpack(KEPT, kept), vec, shards)
    out_tokens, grad_tokens, *finals = run_spread(
        target, packed, packed_grads.reshape(packed.shape), sums, share, up_share
    )
    sum_qkv, sum_out, sum_up, sum_down, gain_one, shift_one, pair_bias = finals[:7]
    bias_out, gain_two, shift_two, bias_down, bias_up = finals[7:]
    return (
        out_tokens.reshape(tokens.shape),
        grad_tokens.reshape(tokens.shape),
        gain_one[0],
        shift_one[0],
        sum_qkv,
        pair_bias,
        sum_out,
        bias_out[0],
        gain_two[0],
        shift_two[0],
        sum_up,
        bias_up[0],
        sum_down,
        bias_down[0],
    )


def solution(mesh):
    placed = (
        P(("gx", "gy"), None, None),
        P(("gx", "gy"), None),
        P(),
        P(("gx", "gy")),
        P(("gx", "gy")),
        P(("gx", "gy"), None),
        P(None, ("gx", "gy")),
        P(("gx", "gy"), None),
        P(("gx", "gy")),
        P(("gx", "gy")),
        P(("gx", "gy")),
        P(("gx", "gy"), None),
        P(("gx", "gy")),
        P(("gx", "gy"), None),
        P(("gx", "gy")),
        P(("gx", "gy"), None, None),
    )
    return jax.shard_map(
        per_device,
        mesh=mesh,
        in_specs=placed,
        out_specs=(
            P(("gx", "gy"), None, None),
            P(("gx", "gy"), None, None),
            P(("gx", "gy")),
            P(("gx", "gy")),
            P(("gx", "gy"), None),
            P(None, ("gx", "gy")),
            P(("gx", "gy"), None),
            P(("gx", "gy")),
            P(("gx", "gy")),
            P(("gx", "gy")),
            P(("gx", "gy"), None),
            P(("gx", "gy")),
            P(("gx", "gy"), None),
            P(("gx", "gy")),
        ),
        check_vma=False,
    )
```
